128 devices in a mesh: section: 2 (over z_hi), dp: 8 (over z_lo, y), tensor: 8 (over x, core).
Axes of the slice: x: 4, y: 4, z: 4 (z_hi: 2, z_lo: 2; z = z_hi * 2 + z_lo), core: 2. Of those that a mesh axis runs over, the one named last changes fastest.
Arguments:
- inputs: bfloat16 [2, 1024, 8, 1024], P(None, 'tensor', 'dp'), may hold values from -6 to 6
- memory_states: bfloat16 [2, 256, 8, 1024], P(None, 'tensor', 'dp'), may hold values from -6 to 6
- source_lengths: int32 [2, 8], P(None, 'dp'), may hold values from 64 to 256, as said below
- cotangent: bfloat16 [2, 1024, 8, 1024], P(None, 'tensor', 'dp'), may hold values from -6 to 6
- norm_gain: float32 [2, 3, 1024], P('section'), may hold values from 0.5 to 1.5
- norm_bias: float32 [2, 3, 1024], P('section'), may hold values from -2 to 2
- w_self: bfloat16 [2, 1024, 3, 1024], P('section', None, None, 'tensor'), may hold values from -0.1875 to 0.1875
- w_self_out: bfloat16 [2, 1024, 1024], P('section', 'tensor'), may hold values from -2 to 2
- w_cross_q: bfloat16 [2, 1024, 1024], P('section', None, 'tensor'), may hold values from -0.1875 to 0.1875
- w_cross_kv: bfloat16 [2, 1024, 2, 1024], P('section', None, None, 'tensor'), may hold values from -0.1875 to 0.1875
- w_cross_out: bfloat16 [2, 1024, 1024], P('section', 'tensor'), may hold values from -2 to 2
- up_weight: bfloat16 [2, 1024, 4096], P('section', None, 'tensor'), may hold values from -0.1875 to 0.1875
- down_weight: bfloat16 [2, 4096, 1024], P('section', 'tensor'), may hold values from -0.09375 to 0.09375
Outputs:
- states: bfloat16 [2, 2, 1024, 8, 1024], P('section', None, 'tensor', 'dp')
- input_grads: bfloat16 [2, 2, 1024, 8, 1024], P('section', None, 'tensor', 'dp')
- grad_norm_gain: float32 [2, 2, 1024], P('section')
- grad_norm_bias: float32 [2, 2, 1024], P('section')
- grad_ffn_norm: float32 [2, 2, 1024], P('section')
- grad_w_self: float32 [2, 1024, 3, 1024], P('section', None, None, 'tensor')
- grad_w_self_out: float32 [2, 1024, 1024], P('section', 'tensor')
- grad_w_cross_q: float32 [2, 1024, 1024], P('section', None, 'tensor')
- grad_w_cross_kv: float32 [2, 1024, 2, 1024], P('section', None, None, 'tensor')
- grad_w_cross_out: float32 [2, 1024, 1024], P('section', 'tensor')
- grad_w_up: float32 [2, 1024, 4096], P('section', None, 'tensor')
- grad_w_down: float32 [2, 4096, 1024], P('section', 'tensor')
The draws below stay inside these ranges and needn't reach their ends.
Inputs may be any that keep to these rules, and one draw needn't show every extreme that they name: `source_lengths`: in each micro-batch one sequence, drawn from the seed, has 256 valid encoder states, and another has 64.
All inputs are finite; a program needn't handle non-finite values.
Results may differ from the reference program's by a relative error of at most 0.033.
Values may be sent and summed in bfloat16 or wider, within the bound.
No kernel may reach another device: no remote copies, remote signals or barrier semaphores. Data moves between devices by JAX's collectives and lax.ppermute only.
A program may use at most 192 MiB of HBM per device.

```python
import jax
import jax.numpy as jnp
from jax import lax

D = 1024
FF = 4096
HD = 64
LEN = 1024
ENC = 256
MICRO = 2
BATCH = 8


def draw_source_lengths(key, part):
    key = jax.random.fold_in(key, 11)
    first_key, second_key = jax.random.split(key)
    lengths = jax.random.randint(first_key, (MICRO, BATCH), ENC // 4, ENC + 1)
    batch_keys = jax.random.split(second_key, MICRO)
    ranks = jax.vmap(lambda one_key: jax.random.permutation(one_key, BATCH))(batch_keys)
    lengths = jnp.where(ranks == 0, ENC, lengths)
    lengths = jnp.where(ranks == 1, ENC // 4, lengths)
    return lengths.astype(jnp.int32)


def block_levels(own_key, extent, cuts, least, high):
    factor_of, own = 1.0, jax.random.fold_in(own_key, 6)
    for position, blocks in cuts:
        steps = jnp.exp(jax.random.uniform(jax.random.fold_in(own, position), (blocks,), jnp.float32, least / len(cuts), high / len(cuts)))
        factor_of = factor_of * jnp.repeat(steps, extent[position] // blocks).reshape([-1 if axis == position else 1 for axis in range(len(extent))])
    return factor_of


def gaussian(rng, dims, scale, reach, cuts=(), held_as=jnp.bfloat16):
    level = block_levels(rng, dims, cuts, -0.22, 0.18) if cuts else 1.0
    result = jax.random.normal(rng, dims, jnp.float32) * scale * level
    return jnp.minimum(jnp.maximum(result, -reach), reach).astype(held_as)


def setup_inputs(seed: int = 0) -> dict:
    key_list = jax.random.split(jax.random.key(seed), 14)
    return {
        "inputs": gaussian(key_list[0], (MICRO, LEN, BATCH, D), 1.0, 6.0, ((1, 8), (2, 8))),
        "memory_states": gaussian(key_list[1], (MICRO, ENC, BATCH, D), 1.0, 6.0, ((1, 8), (2, 8))),
        "source_lengths": draw_source_lengths(jax.random.fold_in(key_list[13], 71), 0),
        "cotangent": gaussian(key_list[3], (MICRO, LEN, BATCH, D), 1.0, 6.0, ((1, 8), (2, 8))),
        "norm_gain": jnp.clip(1.0 + 0.1 * jax.random.normal(key_list[4], (2, 3, D), jnp.float32), 0.5, 1.5),
        "norm_bias": gaussian(key_list[5], (2, 3, D), 0.3, 2.0, ((0, 2),), jnp.float32),
        "w_self": gaussian(key_list[6], (2, D, 3, D), D ** -0.5, 0.1875, ((0, 2), (3, 8))),
        "w_self_out": gaussian(key_list[7], (2, D, D), (max(1, 8 * D // LEN)) ** -0.5, 2.0, ((0, 2), (1, 8))),
        "w_cross_q": gaussian(key_list[8], (2, D, D), D ** -0.5, 0.1875, ((0, 2), (2, 8))),
        "w_cross_kv": gaussian(key_list[9], (2, D, 2, D), D ** -0.5, 0.1875, ((0, 2), (3, 8))),
        "w_cross_out": gaussian(key_list[10], (2, D, D), (max(1, 2 * D // ENC)) ** -0.5, 2.0, ((0, 2), (1, 8))),
        "up_weight": gaussian(key_list[11], (2, D, FF), D ** -0.5, 0.1875, ((0, 2), (2, 8))),
        "down_weight": gaussian(key_list[12], (2, FF, D), FF ** -0.5, 0.09375, ((0, 2), (1, 8))),
    }


@jax.custom_vjp
def low(v):
    return lax.optimization_barrier(v.astype(jnp.bfloat16)).astype(jnp.float32)

@jax.custom_vjp
def low_back(v):
    return v

def low_keep(v):
    return (low(v), None)

def low_pass(kept, grad):
    return (grad,)

def back_keep(v):
    return (v, None)

def back_low(kept, grad):
    return (low(grad),)
low.defvjp(low_keep, low_pass)
low_back.defvjp(back_keep, back_low)
EPSILON = 1e-05
NEG_FILL = -1000000000.0
EXACT = lax.Precision.HIGHEST

def normalize(residual_stream, gain_row, bias_row):
    average = lax.optimization_barrier(jnp.mean(residual_stream, axis=-1, keepdims=True))
    centred = residual_stream - average
    return centred * lax.rsqrt(lax.optimization_barrier(jnp.mean(centred * centred, axis=-1, keepdims=True)) + EPSILON) * gain_row + bias_row

def one_block(query_in, key_in, value_in, bounds, offset):
    qblock = min(512, query_in.shape[0])
    factor = query_in.shape[2] ** (-0.5)
    row_slice = lax.dynamic_slice_in_dim(query_in, offset, qblock, 0)
    limits = lax.dynamic_slice_in_dim(bounds, offset, qblock, 0)
    slots = jnp.arange(key_in.shape[0], dtype=jnp.int32)
    scores = jnp.einsum('qhe,khe->hqk', row_slice, key_in, precision=EXACT) * factor
    scores = low_back(jnp.where(slots[None, :] < limits[:, None], scores, NEG_FILL))
    chances = jax.nn.softmax(scores, axis=-1)
    mixed = jnp.einsum('hqk,khe->qhe', low(chances), value_in, precision=EXACT)
    return low(low_back(mixed.reshape(qblock, -1)))

def attend(query_in, key_in, value_in, bounds):
    length = query_in.shape[0]
    qblock = min(512, length)
    starts = jnp.arange(length // qblock, dtype=jnp.int32) * qblock
    checked = jax.checkpoint(one_block)
    mixed = lax.map(lambda offset: checked(query_in, key_in, value_in, bounds, offset), starts)
    return mixed.reshape(length, -1)

def layer(params, which, residual_stream, memory, length):
    norm_gain, norm_bias, w_self, w_self_out, w_cross_q, w_cross_kv, w_cross_out, up_weight, down_weight = params
    tokens = residual_stream.shape[0]
    normed = low(normalize(residual_stream, norm_gain[which, 0], norm_bias[which, 0]))
    packed = low(low_back(jnp.einsum('ld,dkh->lkh', normed, w_self[which], precision=EXACT)))
    divided = packed.reshape(tokens, 3, -1, HD)
    causal = jnp.arange(tokens, dtype=jnp.int32) + 1
    mixed = attend(divided[:, 0], divided[:, 1], divided[:, 2], causal)
    residual_stream = residual_stream + low_back(jnp.dot(mixed, w_self_out[which], precision=EXACT))
    normed = low(normalize(residual_stream, norm_gain[which, 1], norm_bias[which, 1]))
    cross_query = low(low_back(jnp.dot(normed, w_cross_q[which], precision=EXACT)))
    cross_pair = low(low_back(jnp.einsum('ed,dkh->ekh', memory, w_cross_kv[which], precision=EXACT)))
    cross_pair = cross_pair.reshape(memory.shape[0], 2, -1, HD)
    visible = jnp.zeros((tokens,), jnp.int32) + length
    mixed = attend(cross_query.reshape(tokens, -1, HD), cross_pair[:, 0], cross_pair[:, 1], visible)
    residual_stream = residual_stream + low_back(jnp.dot(mixed, w_cross_out[which], precision=EXACT))
    normed = low(normalize(residual_stream, norm_gain[which, 2], norm_bias[which, 2]))
    hidden = low(jax.nn.gelu(low_back(jnp.dot(normed, up_weight[which], precision=EXACT))))
    return residual_stream + low_back(jnp.dot(hidden, down_weight[which], precision=EXACT))

def reference(inputs, memory_states, source_lengths, cotangent, norm_gain, norm_bias, w_self, w_self_out, w_cross_q, w_cross_kv, w_cross_out, up_weight, down_weight):

    def flatten_seq(array):
        return jnp.transpose(array.astype(jnp.float32), (0, 2, 1, 3)).reshape(MICRO * BATCH, array.shape[1], D)

    def unflatten_seq(array):
        return jnp.transpose(array.reshape(MICRO, BATCH, LEN, D), (0, 2, 1, 3))
    seq_inputs = flatten_seq(inputs)
    seq_memory = flatten_seq(memory_states)
    seq_lengths = source_lengths.reshape(MICRO * BATCH).astype(jnp.int32)
    params = tuple((member.astype(jnp.float32) for member in (norm_gain, norm_bias, w_self, w_self_out, w_cross_q, w_cross_kv, w_cross_out, up_weight, down_weight)))
    zero_grad = jnp.zeros_like(seq_inputs)

    def forward(params, seq_inputs, zero_grad):

        def per_sequence(element):
            start_rows, memory, length, offset_rows = element
            text_out = low(low_back(layer(params, 0, start_rows, memory, length)))
            return (text_out, layer(params, 1, text_out + offset_rows, memory, length))
        return lax.map(per_sequence, (seq_inputs, seq_memory, seq_lengths, zero_grad))
    (text_out, unit_out), pullback = jax.vjp(forward, params, seq_inputs, zero_grad)
    gradients, grad_inputs, grad_text = pullback((jnp.zeros_like(text_out), flatten_seq(cotangent)))
    states = jnp.stack([unflatten_seq(text_out), unflatten_seq(unit_out)]).astype(jnp.bfloat16)
    input_grads = jnp.stack([unflatten_seq(grad_inputs), unflatten_seq(grad_text)]).astype(jnp.bfloat16)
    ffn_norm = jnp.stack([gradients[0][:, 2], gradients[1][:, 2]], axis=1)
    return (states, input_grads, gradients[0][:, :2], gradients[1][:, :2], ffn_norm, gradients[2], gradients[3], gradients[4], gradients[5], gradients[6], gradients[7], gradients[8])
```

```python
import functools

import jax
import jax.numpy as jnp
from jax import lax
from jax.experimental import pallas as pl
from jax.experimental.pallas import tpu as pltpu
from jax.sharding import Mesh, PartitionSpec as P

HD = 64
EPSILON = 1e-05
NEG_FILL = -1000000000.0
BLOCK = 128
RING = 4
BF16 = jnp.bfloat16
F32 = jnp.float32


def shift(value, axis, steps):
    count = lax.axis_size(axis)
    return lax.ppermute(value, axis, [(i, (i + steps) % count) for i in range(count)])


def swap(value, axis):
    return shift(value, axis, 1)


def gather_x(value):
    return [value] + [shift(value, "tx", k) for k in range(1, RING)]


def scatter_x(own, others):
    arrived = [shift(block, "tx", -k) for k, block in enumerate(others, 1)]
    total = own
    for block in arrived:
        total = total + block.astype(F32)
    return total


def dot(a, b, dims):
    return lax.dot_general(a, b, ((dims[0], dims[1]), ((), ())), preferred_element_type=F32)


def mm(a, b):
    return dot(a, b, ((1,), (0,)))


def mm_nt(a, b):
    return dot(a, b, ((1,), (1,)))


def mm_tn(a, b):
    return dot(a, b, ((0,), (0,)))


def normalize(v, gain, bias):
    average = jnp.mean(v, axis=-1, keepdims=True)
    centred = v - average
    inv = lax.rsqrt(jnp.mean(centred * centred, axis=-1, keepdims=True) + EPSILON)
    standard = centred * inv
    return (standard * gain + bias).astype(BF16), standard, inv


def normalize_back(incoming, standard, inv, gain):
    scaled = incoming * gain
    inner = (
        scaled
        - jnp.mean(scaled, axis=-1, keepdims=True)
        - standard * jnp.mean(scaled * standard, axis=-1, keepdims=True)
    )
    return inner * inv, jnp.sum(incoming * standard, axis=0), jnp.sum(incoming, axis=0)


def block_of(place, b):
    return lax.rem(place[0] - b + RING, RING)


def lay_out_keys(place, own_ref, other_ref, kbuf, vbuf):
    core = place[1]
    for b in range(RING):
        j = block_of(place, b)
        own_at = pl.ds(pl.multiple_of((2 * b + core) * BLOCK, BLOCK), BLOCK)
        other_at = pl.ds(pl.multiple_of((2 * b + 1 - core) * BLOCK, BLOCK), BLOCK)
        for pair in range(2):
            here = slice(pair * 128, pair * 128 + 128)
            kbuf[own_at, here] = own_ref[j, :, 256 * pair : 256 * pair + 128]
            vbuf[own_at, here] = own_ref[j, :, 256 * pair + 128 : 256 * pair + 256]
            theirs = 1 - pair
            kbuf[other_at, here] = other_ref[j, :, 256 * theirs : 256 * theirs + 128]
            vbuf[other_at, here] = other_ref[j, :, 256 * theirs + 128 : 256 * theirs + 256]


def causal_tail(scores, core):
    key_at = lax.broadcasted_iota(jnp.int32, scores.shape, 0)
    query_at = lax.broadcasted_iota(jnp.int32, scores.shape, 1) + core * BLOCK
    return jnp.where(key_at <= query_at, scores, NEG_FILL)


def self_forward_kernel(place, q_ref, own_ref, other_ref, o_ref, lse_ref, kbuf, vbuf):
    lay_out_keys(place, own_ref, other_ref, kbuf, vbuf)
    core = place[1]
    for b in range(RING):
        j = block_of(place, b)
        span = 2 * BLOCK * (b + 1)
        head = span - 2 * BLOCK
        for pair in range(2):
            outs = []
            for h in (2 * pair, 2 * pair + 1):
                cols = slice(HD * h, HD * h + HD)
                q = q_ref[j, :, cols] * 0.125
                last = causal_tail(mm_nt(kbuf[head:span, cols], q), core)
                top = jnp.max(last, axis=0, keepdims=True)
                if head:
                    early = mm_nt(kbuf[0:head, cols], q)
                    top = jnp.maximum(top, jnp.max(early, axis=0, keepdims=True))
                    early = jnp.exp(early - top)
                last = jnp.exp(last - top)
                total = jnp.sum(last, axis=0, keepdims=True)
                mixed = mm_tn(vbuf[head:span, cols], last.astype(BF16))
                if head:
                    total = total + jnp.sum(early, axis=0, keepdims=True)
                    mixed = mixed + mm_tn(vbuf[0:head, cols], early.astype(BF16))
                outs.append(mixed / total)
                lse_ref[h, j] = top + jnp.log(total)
            both = jnp.concatenate(outs, axis=0)
            o_ref[j, :, 128 * pair : 128 * pair + 128] = both.T.astype(BF16)


def self_back_kernel(
    place, q_ref, own_ref, other_ref, do_ref, lse_ref, dq_ref, down_ref, dother_ref, kbuf, vbuf, dk, dv
):
    lay_out_keys(place, own_ref, other_ref, kbuf, vbuf)
    core = place[1]
    for b in reversed(range(RING)):
        j = block_of(place, b)
        span = 2 * BLOCK * (b + 1)
        head = span - 2 * BLOCK
        for pair in range(2):
            lanes = slice(128 * pair, 128 * pair + 128)
            dqs, dks, dvs = [], [], []
            for h in (2 * pair, 2 * pair + 1):
                cols = slice(HD * h, HD * h + HD)
                q = q_ref[j, :, cols] * 0.125
                do = do_ref[j, :, cols]
                k = kbuf[0:span, cols]
                scores = mm_nt(k, q)
                last = causal_tail(scores[head:span], core)
                scores = jnp.concatenate([scores[0:head], last], axis=0) if head else last
                probs = jnp.exp(scores - lse_ref[h, j])
                dprobs = mm_nt(vbuf[0:span, cols], do)
                delta = jnp.sum(probs * dprobs, axis=0, keepdims=True)
                dscores = (probs * (dprobs - delta)).astype(BF16)
                dqs.append(mm_tn(k, dscores) * 0.125)
                dks.append(mm(dscores, q))
                dvs.append(mm(probs.astype(BF16), do))
            dq_ref[j, :, lanes] = jnp.concatenate(dqs, axis=0).T.astype(BF16)
            dk_new = jnp.concatenate(dks, axis=1)
            dv_new = jnp.concatenate(dvs, axis=1)
            if b == RING - 1:
                dk[0:span, lanes] = dk_new
                dv[0:span, lanes] = dv_new
            else:
                dk[0:span, lanes] += dk_new
                dv[0:span, lanes] += dv_new
    for b in range(RING):
        j = block_of(place, b)
        own_at = pl.ds(pl.multiple_of((2 * b + core) * BLOCK, BLOCK), BLOCK)
        other_at = pl.ds(pl.multiple_of((2 * b + 1 - core) * BLOCK, BLOCK), BLOCK)
        for pair in range(2):
            here = slice(pair * 128, pair * 128 + 128)
            theirs = 1 - pair
            down_ref[j, :, 256 * pair : 256 * pair + 128] = dk[own_at, here]
            down_ref[j, :, 256 * pair + 128 : 256 * pair + 256] = dv[own_at, here]
            dother_ref[j, :, 256 * theirs : 256 * theirs + 128] = dk[other_at, here].astype(BF16)
            dother_ref[j, :, 256 * theirs + 128 : 256 * theirs + 256] = dv[other_at, here].astype(BF16)


def cross_mask(scores, length):
    slots = lax.broadcasted_iota(jnp.int32, scores.shape, 0)
    return jnp.where(slots < length, scores, NEG_FILL)


def cross_forward_kernel(length, q_ref, kv_ref, o_ref, lse_ref):
    for g in range(RING):
        outs = []
        for p in range(2):
            h = 2 * g + p
            q = q_ref[:, HD * h : HD * h + HD] * 0.125
            k = kv_ref[g, :, HD * p : HD * p + HD]
            v = kv_ref[g, :, 128 + HD * p : 128 + HD * p + HD]
            scores = cross_mask(mm_nt(k, q), length[0])
            top = jnp.max(scores, axis=0, keepdims=True)
            raised = jnp.exp(scores - top)
            total = jnp.sum(raised, axis=0, keepdims=True)
            outs.append(mm_tn(v, raised.astype(BF16)) / total)
            lse_ref[h] = top + jnp.log(total)
        o_ref[:, 128 * g : 128 * g + 128] = jnp.concatenate(outs, axis=0).T.astype(BF16)


def cross_back_kernel(length, q_ref, kv_ref, do_ref, lse_ref, dq_ref, dkv_ref):
    for g in range(RING):
        dqs, dks, dvs = [], [], []
        for p in range(2):
            h = 2 * g + p
            q = q_ref[:, HD * h : HD * h + HD] * 0.125
            do = do_ref[:, HD * h : HD * h + HD]
            k = kv_ref[g, :, HD * p : HD * p + HD]
            v = kv_ref[g, :, 128 + HD * p : 128 + HD * p + HD]
            probs = jnp.exp(cross_mask(mm_nt(k, q), length[0]) - lse_ref[h])
            dprobs = mm_nt(v, do)
            delta = jnp.sum(probs * dprobs, axis=0, keepdims=True)
            dscores = (probs * (dprobs - delta)).astype(BF16)
            dqs.append(mm_tn(k, dscores) * 0.125)
            dks.append(mm(dscores, q))
            dvs.append(mm(probs.astype(BF16), do))
        dq_ref[:, 128 * g : 128 * g + 128] = jnp.concatenate(dqs, axis=0).T.astype(BF16)
        dkv_ref[g] = jnp.concatenate(dks + dvs, axis=1).astype(BF16)


SMEM = pl.BlockSpec(memory_space=pltpu.SMEM)
VMEM = pl.BlockSpec(memory_space=pltpu.VMEM)
LIMIT = 48 * 1024 * 1024


def call(kernel, outs, scratch, flops, *operands):
    moved = sum(o.size * o.dtype.itemsize for o in operands) + sum(
        o.size * o.dtype.itemsize for o in outs
    )
    return pl.pallas_call(
        kernel,
        out_shape=outs,
        in_specs=[SMEM] + [VMEM] * (len(operands) - 1),
        out_specs=[VMEM] * len(outs),
        scratch_shapes=scratch,
        compiler_params=pltpu.CompilerParams(vmem_limit_bytes=LIMIT),
        cost_estimate=pl.CostEstimate(flops=flops, bytes_accessed=moved, transcendentals=0),
    )(*operands)


def struct(shape, dtype):
    return jax.ShapeDtypeStruct(shape, dtype)


KEYS = 2 * RING * BLOCK


def self_forward(place, q, kv, kv_other):
    return call(
        self_forward_kernel,
        [struct((RING, BLOCK, 256), BF16), struct((4, RING, 1, BLOCK), F32)],
        [pltpu.VMEM((KEYS, 256), BF16), pltpu.VMEM((KEYS, 256), BF16)],
        4 * 2 * 2 * 512 * 1024 * HD,
        place,
        q,
        kv,
        kv_other,
    )


def self_back(place, q, kv, kv_other, do, lse):
    return call(
        self_back_kernel,
        [
            struct((RING, BLOCK, 256), BF16),
            struct((RING, BLOCK, 512), F32),
            struct((RING, BLOCK, 512), BF16),
        ],
        [
            pltpu.VMEM((KEYS, 256), BF16),
            pltpu.VMEM((KEYS, 256), BF16),
            pltpu.VMEM((KEYS, 256), F32),
            pltpu.VMEM((KEYS, 256), F32),
        ],
        4 * 5 * 2 * 512 * 1024 * HD,
        place,
        q,
        kv,
        kv_other,
        do,
        lse,
    )


def cross_forward(length, q, kv):
    return call(
        cross_forward_kernel,
        [struct(q.shape, BF16), struct((2 * RING, 1, q.shape[0]), F32)],
        [],
        8 * 2 * 2 * 256 * 256 * HD,
        length,
        q,
        kv,
    )


def cross_back(length, q, kv, do, lse):
    return call(
        cross_back_kernel,
        [struct(q.shape, BF16), struct(kv.shape, BF16)],
        [],
        8 * 5 * 2 * 256 * 256 * HD,
        length,
        q,
        kv,
        do,
        lse,
    )


def rows_of(full):
    return [full[BLOCK * k : BLOCK * (k + 1)] for k in range(RING)]


def sum_rows(operands, weights, product):
    shares = [None] * RING
    for k in (2, 1, 3, 0):
        total = None
        for operand, weight in zip(operands, weights):
            part = product(operand[BLOCK * k : BLOCK * (k + 1)], weight)
            total = part if total is None else total + part
        shares[k] = total
    return scatter_x(shares[0], [share.astype(BF16) for share in shares[1:]])


def gelu_both(pre):
    root = 0.7978845608028654
    square = pre * pre
    t = jnp.tanh(root * (pre + 0.044715 * pre * square))
    half = 0.5 * (1.0 + t)
    slope = half + 0.5 * pre * (1.0 - t * t) * (root * (1.0 + 3 * 0.044715 * square))
    return (pre * half).astype(BF16), slope


def layer_forward(v, weights, kv, place, length, gain, bias):
    a1, s1, r1 = normalize(v, gain[0], bias[0])
    full1 = jnp.concatenate(gather_x(a1), axis=0)
    kv_self = mm(full1, weights["kv"]).astype(BF16).reshape(RING, BLOCK, 512)
    kv_other = swap(kv_self, "core")
    q = mm(full1, weights["q"]).astype(BF16).reshape(RING, BLOCK, 256)
    mixed1, lse1 = self_forward(place, q, kv_self, kv_other)
    mixed1 = mixed1.reshape(RING * BLOCK, 256)
    v1 = v + sum_rows([mixed1], [weights["out"]], mm)
    a2, s2, r2 = normalize(v1, gain[1], bias[1])
    pair2 = jnp.concatenate([a2, swap(a2, "core")], axis=0)
    cq = mm(pair2, weights["cq"]).astype(BF16)
    mixed2, lse2 = cross_forward(length, cq, kv)
    far = mm(mixed2[BLOCK:], weights["co"]).astype(BF16)
    near = mm(mixed2[:BLOCK], weights["co"])
    v2 = v1 + (near + swap(far, "core").astype(F32))
    a3, s3, r3 = normalize(v2, gain[2], bias[2])
    full3 = jnp.concatenate(gather_x(a3), axis=0)
    hidden, slope = gelu_both(mm(full3, weights["up"]))
    v3 = v2 + sum_rows([hidden], [weights["down"]], mm)
    stored = (
        (s1, r1, full1, q, kv_self, kv_other, mixed1, lse1),
        (s2, r2, pair2, cq, mixed2, lse2),
        (s3, r3, full3, hidden, slope),
    )
    return v3, stored


def pair_sum(left, right):
    half = left.shape[1] // 2
    theirs = mm_tn(left[:, half:], right).astype(BF16)
    ours = mm_tn(left[:, :half], right)
    return (ours + swap(theirs, "core").astype(F32)).astype(BF16)


def layer_back(dv, full_g3, stored, weights, kv, memory, place, length, gain):
    (s1, r1, full1, q, kv_self, kv_other, mixed1, lse1), second, third = stored
    s2, r2, pair2, cq, mixed2, lse2 = second
    s3, r3, full3, hidden, slope = third
    dpre = (mm_nt(full_g3, weights["down"]) * slope).astype(BF16)
    da3 = sum_rows([dpre], [weights["up"]], mm_nt)
    delta, gain3, bias3 = normalize_back(da3, s3, r3, gain[2])
    dv2 = dv + delta
    grad_down = pair_sum(hidden, full_g3)
    grad_up = pair_sum(dpre, full3)

    g2 = dv2.astype(BF16)
    pair_g2 = jnp.concatenate([g2, swap(g2, "core")], axis=0)
    dmixed2 = mm_nt(pair_g2, weights["co"]).astype(BF16)
    dcq, dkv = cross_back(length, cq, kv, dmixed2, lse2)
    far = mm_nt(dcq[BLOCK:], weights["cq"]).astype(BF16)
    near = mm_nt(dcq[:BLOCK], weights["cq"])
    da2 = near + swap(far, "core").astype(F32)
    delta, gain2, bias2 = normalize_back(da2, s2, r2, gain[1])
    dv1 = dv2 + delta

    g1 = dv1.astype(BF16)
    full_g1 = jnp.concatenate(gather_x(g1), axis=0)
    dmixed1 = mm_nt(full_g1, weights["out"]).astype(BF16).reshape(RING, BLOCK, 256)
    dq, dkv_own, dkv_theirs = self_back(place, q, kv_self, kv_other, dmixed1, lse1)
    dkv_self = dkv_own + swap(dkv_theirs, "core").astype(F32)
    dkv_self = dkv_self.astype(BF16).reshape(RING * BLOCK, 512)
    dq = dq.reshape(RING * BLOCK, 256)
    da1 = sum_rows([dq, dkv_self], [weights["q"], weights["kv"]], mm_nt)
    delta, gain1, bias1 = normalize_back(da1, s1, r1, gain[0])
    dv0 = dv1 + delta

    dwco = mm_tn(mixed2, pair_g2)
    grad_co = scatter_x(dwco[:128], [dwco[128 * k : 128 * k + 128].astype(BF16) for k in (1, 2, 3)])
    dwcq = mm_tn(dcq, pair2)
    grad_cq = scatter_x(dwcq[:128], [dwcq[128 * k : 128 * k + 128].astype(BF16) for k in (1, 2, 3)])
    dkv_sum = scatter_x(dkv[0].astype(F32), [dkv[k] for k in (1, 2, 3)]).astype(BF16)
    grad_ckv = mm_tn(dkv_sum, memory)
    grad_out = pair_sum(mixed1, full_g1)
    grad_q = pair_sum(dq, full1)
    grad_kv = pair_sum(dkv_self, full1)
    late = jnp.concatenate(
        [grad_co.astype(BF16), grad_cq.astype(BF16), grad_ckv.astype(BF16), grad_out, grad_q, grad_kv], axis=0
    )
    early = jnp.concatenate([grad_down, grad_up], axis=0)
    norms = jnp.stack([gain1, gain2, gain3, bias1, bias2, bias3])
    return dv0, early, late, norms


def sum_over_mesh(value):
    value = value + swap(value, "core")
    for axis in ("tx", "dy"):
        value = value + sum(shift(value, axis, k) for k in range(1, RING))
    value = value + swap(value, "dz")
    return value + swap(value, "section")


def reduce_dp(grads):
    return lax.psum_scatter(grads, ("dz", "dy"), scatter_dimension=0, tiled=True)


def finish(is_first, first_layer, second_layer):
    mine = jnp.where(is_first, first_layer, second_layer).astype(F32)
    theirs = jnp.where(is_first, second_layer, first_layer)
    total = (mine + swap(theirs, "section").astype(F32)).astype(BF16)
    return lax.all_gather(total, ("dz", "dy"), axis=0, tiled=True).astype(F32)


def shards(
    inputs,
    memory_states,
    source_lengths,
    cotangent,
    norm_gain,
    norm_bias,
    w_self,
    w_self_out,
    w_cross_q,
    w_cross_kv,
    w_cross_out,
    up_weight,
    down_weight,
):
    section = lax.axis_index("section")
    is_first = section == 0
    place = jnp.stack([lax.axis_index("tx"), lax.axis_index("core")]).astype(jnp.int32)

    def pick(array):
        return lax.dynamic_index_in_dim(array, section, 0, keepdims=False)

    def both_layers(mine, other):
        return jnp.where(is_first, mine, other), jnp.where(is_first, other, mine)

    x = pick(inputs)[:, 0]
    g_top = pick(cotangent)[:, 0]
    length = pick(source_lengths)
    memory = lax.all_gather(pick(memory_states)[:, 0], ("tx", "core"), axis=0, tiled=True)

    ws = w_self[0].reshape(w_self.shape[1], -1)
    mine = {
        "self": ws,
        "out": w_self_out[0],
        "cq": w_cross_q[0],
        "co": w_cross_out[0],
        "ckv": w_cross_kv[0].reshape(w_cross_kv.shape[1], -1),
        "up": up_weight[0],
        "down": down_weight[0],
    }
    other = {name: swap(value, "section") for name, value in mine.items()}
    gains = both_layers(norm_gain[0], swap(norm_gain[0], "section"))
    biases = both_layers(norm_bias[0], swap(norm_bias[0], "section"))

    layers = [{}, {}]
    for name, axis in (("self", 1), ("out", 0), ("up", 1), ("down", 0)):
        own = both_layers(mine[name], other[name])
        far = both_layers(swap(mine[name], "core"), swap(other[name], "core"))
        for i in range(2):
            if name == "self":
                layers[i]["q"] = jnp.concatenate([own[i][:, :128], far[i][:, :128]], axis=1)
                layers[i]["kv"] = jnp.concatenate([own[i][:, 128:], far[i][:, 128:]], axis=1)
            else:
                layers[i][name] = jnp.concatenate([own[i], far[i]], axis=axis)
    for name, axis in (("cq", 1), ("co", 0)):
        for i, value in enumerate(both_layers(mine[name], other[name])):
            layers[i][name] = jnp.concatenate(gather_x(value), axis=axis)
    ckv = both_layers(mine["ckv"], other["ckv"])
    pairs = [mm(memory, ckv[i]).astype(BF16) for i in range(2)]
    kvs = [jnp.stack(gather_x(pair)) for pair in pairs]

    text, stored0 = layer_forward(x.astype(F32), layers[0], kvs[0], place, length, gains[0], biases[0])
    text = text.astype(BF16)
    unit, stored1 = layer_forward(text.astype(F32), layers[1], kvs[1], place, length, gains[1], biases[1])
    unit = unit.astype(BF16)

    full_top = jnp.concatenate(gather_x(g_top), axis=0)
    dv, early1, late1, norms1 = layer_back(
        g_top.astype(F32), full_top, stored1, layers[1], kvs[1], memory, place, length, gains[1]
    )
    early1 = reduce_dp(early1)
    late1 = reduce_dp(late1)
    text_grad = dv.astype(BF16)
    full_text = jnp.concatenate(gather_x(text_grad), axis=0)
    dv, early0, late0, norms0 = layer_back(
        text_grad.astype(F32), full_text, stored0, layers[0], kvs[0], memory, place, length, gains[0]
    )
    input_grad = dv.astype(BF16)
    early = finish(is_first, reduce_dp(early0), early1)
    late = finish(is_first, reduce_dp(late0), late1)

    def by_layer(first, second):
        keep = jnp.where(is_first, first, second)
        came = swap(jnp.where(is_first, second, first), "section")
        return jnp.stack([jnp.where(is_first, keep, came), jnp.where(is_first, came, keep)])[None, :, :, None]

    states = by_layer(text, unit)
    input_grads = by_layer(input_grad, text_grad)
    norms = pick(sum_over_mesh(jnp.stack([norms0, norms1])))

    half = down_weight.shape[1]
    grad_down, grad_up = early[:half], early[half:].T
    grad_co, grad_cq = late[:128], late[128:256].T
    grad_ckv = late[256:512].T.reshape(-1, 2, 128)
    grad_out = late[512:640]
    grad_self = late[640:1024].T.reshape(-1, 3, 128)
    return (
        states,
        input_grads,
        norms[None, 0:2],
        norms[None, 3:5],
        jnp.stack([norms[2], norms[5]])[None],
        grad_self[None],
        grad_out[None],
        grad_cq[None],
        grad_ckv[None],
        grad_co[None],
        grad_up[None],
        grad_down[None],
    )


def solution(mesh):
    sections = mesh.devices.shape[0]
    fine = Mesh(
        mesh.devices.reshape(sections, 2, RING, RING, 2), ("section", "dz", "dy", "tx", "core")
    )
    dp, tensor = ("dz", "dy"), ("tx", "core")
    rows = P(None, tensor, dp, None)
    return jax.shard_map(
        shards,
        mesh=fine,
        in_specs=(
            rows,
            rows,
            P(None, dp),
            rows,
            P("section", None, None),
            P("section", None, None),
            P("section", None, None, tensor),
            P("section", tensor, None),
            P("section", None, tensor),
            P("section", None, None, tensor),
            P("section", tensor, None),
            P("section", None, tensor),
            P("section", tensor, None),
        ),
        out_specs=(
            P("section", None, tensor, dp, None),
            P("section", None, tensor, dp, None),
            P("section", None, None),
            P("section", None, None),
            P("section", None, None),
            P("section", None, None, tensor),
            P("section", tensor, None),
            P("section", None, tensor),
            P("section", None, None, tensor),
            P("section", tensor, None),
            P("section", None, tensor),
            P("section", tensor, None),
        ),
        check_vma=False,
    )
```

```python
import functools
import math

import jax
import jax.numpy as jnp
from jax import lax
from jax.experimental import pallas as pl
from jax.experimental.pallas import tpu as pltpu
from jax.sharding import Mesh, PartitionSpec as P

HD = 64
EPSILON = 1e-05
NEG_FILL = -1000000000.0
BLOCK = 128
RING = 4
BF16 = jnp.bfloat16
F32 = jnp.float32


def shift(value, axis, steps):
    count = lax.axis_size(axis)
    return lax.ppermute(value, axis, [(i, (i + steps) % count) for i in range(count)])


def swap(value, axis):
    return shift(value, axis, 1)


def dot(a, b, dims):
    return lax.dot_general(a, b, ((dims[0], dims[1]), ((), ())), preferred_element_type=F32)


def mm(a, b):
    return dot(a, b, ((1,), (0,)))


def mm_nt(a, b):
    return dot(a, b, ((1,), (1,)))


def mm_tn(a, b):
    return dot(a, b, ((0,), (0,)))


def gather_x(value):
    return [value] + [shift(value, "tx", k) for k in range(1, RING)]


def send_x(others):
    return [shift(block, "tx", -k) for k, block in enumerate(others, 1)]


SMEM = pl.BlockSpec(memory_space=pltpu.SMEM)
VMEM = pl.BlockSpec(memory_space=pltpu.VMEM)
ANY = pl.BlockSpec(memory_space=pl.ANY)
HBM = pl.BlockSpec(memory_space=pltpu.HBM)
CHUNK = 256


def struct(shape, dtype):
    return jax.ShapeDtypeStruct(shape, dtype)


class Cold:
    def __init__(self, array):
        self.array = array


def cold(*arrays):
    return [Cold(array) for array in arrays]


def cold_if(flag, *arrays):
    return cold(*arrays) if flag else list(arrays)


def vmem(o):
    return pltpu.VMEM(o.shape, o.dtype)


class Place:
    axes = ("tx", "core", "dy", "dz", "section")

    def __getitem__(self, at):
        return lax.axis_index(self.axes[at])


PLACE = Place()


def settled(array):
    return pltpu.with_memory_space_constraint(array, pltpu.HBM)


def call(kernel, outs, operands, scalars=(), scratch=(), after=(), room=8, token=False):
    ins = [o if isinstance(o, Cold) else None for o in operands]
    arrays = [o.array if isinstance(o, Cold) else o for o in operands]
    puts = [o if isinstance(o, Cold) else None for o in outs]
    shapes = [o.array if isinstance(o, Cold) else o for o in outs]
    if token:
        puts.append(None)
        shapes.append(struct((8, 128), F32))
    placed = any(o is PLACE for o in scalars)
    scalars = [o for o in scalars if o is not PLACE]
    first, waits = len(scalars), len(after)
    last = first + len(arrays)
    brought = [vmem(o.array) for o in ins if o]
    taken = [vmem(o.array) for o in puts if o]
    held = sum(math.prod(o.shape) * o.dtype.itemsize for o in (*scratch, *brought, *taken))
    name = kernel.func.__name__ if isinstance(kernel, functools.partial) else kernel.__name__

    def body(*refs):
        given = list(refs[first:last])
        results = list(refs[last + waits : last + waits + len(shapes)])
        rest = list(refs[last + waits + len(shapes) :])
        semaphores = rest.pop() if brought or taken else None
        buffers = rest[len(scratch) :]
        moves, stores = [], []
        for at, o in enumerate(ins):
            if o:
                buffer = buffers[len(moves)]
                moves.append(
                    pltpu.make_async_copy(given[at], buffer, semaphores.at[len(moves)])
                )
                moves[-1].start()
                given[at] = buffer
        for at, o in enumerate(puts):
            if o:
                n = len(moves) + len(stores)
                stores.append(pltpu.make_async_copy(buffers[n], results[at], semaphores.at[n]))
                results[at] = buffers[n]
        for move in moves:
            move.wait()
        if token:
            results.pop()[...] = jnp.zeros((8, 128), F32)
        lead = [PLACE] if placed else []
        kernel(*lead, *refs[:first], *given, *results, *rest[: len(scratch)])
        for store in stores:
            store.start()
        for store in stores:
            store.wait()

    kept = [*scratch, *brought, *taken]
    if brought or taken:
        kept.append(pltpu.SemaphoreType.DMA((len(brought) + len(taken),)))
    return pl.pallas_call(
        body,
        name=name,
        out_shape=[pltpu.HBM(o.shape, o.dtype) if c else o for o, c in zip(shapes, puts)],
        in_specs=[SMEM] * first + [HBM if o else VMEM for o in ins] + [ANY] * waits,
        out_specs=[HBM if o else VMEM for o in puts],
        scratch_shapes=kept,
        compiler_params=pltpu.CompilerParams(vmem_limit_bytes=held + room * 1024 * 1024),
    )(*scalars, *(settled(a) if c else a for a, c in zip(arrays, ins)), *after)


ROW = struct((BLOCK, 1024), F32)
ROW16 = struct((BLOCK, 1024), BF16)
COLUMN = struct((BLOCK, 1), F32)
SENT = [ROW] + [ROW16] * (RING - 1)


def stack_rows(refs, cols=slice(None)):
    return jnp.concatenate([ref[:, cols] for ref in refs], axis=0)


def split_rows(total, outs, cols):
    outs[0][:, cols] = total[0:BLOCK]
    for k in range(1, len(outs)):
        outs[k][:, cols] = total[BLOCK * k : BLOCK * (k + 1)].astype(BF16)


def chunks(width=1024):
    return [slice(at, at + CHUNK) for at in range(0, width, CHUNK)]


def norm(v, gain, bias, a_ref, s_ref, r_ref):
    average = jnp.mean(v, axis=-1, keepdims=True)
    centred = v - average
    inv = lax.rsqrt(jnp.mean(centred * centred, axis=-1, keepdims=True) + EPSILON)
    standard = centred * inv
    s_ref[...] = standard
    r_ref[...] = inv
    a_ref[...] = (standard * gain + bias).astype(BF16)


def total_of(v_ref, near, far):
    total = v_ref[...].astype(F32) + near[...]
    for ref in far:
        total = total + ref[...].astype(F32)
    return total


def sum_norm_kernel(j, count, v_ref, near, *refs):
    far, (rows, v_out, a_ref, s_ref, r_ref) = refs[:count], refs[count:]
    v = total_of(v_ref, near, far)
    v_out[...] = v.astype(v_out.dtype)
    v = v_out[...].astype(F32)
    norm(v, rows[j : j + 1], rows[3 + j : 4 + j], a_ref, s_ref, r_ref)


def sum_norm(j, v, near, far, rows, kept, after=(), old=False, new=False):
    outs = [*cold_if(new, kept), ROW16, *cold_if(new, ROW, COLUMN)]
    return call(
        functools.partial(sum_norm_kernel, j, len(far)),
        outs,
        [*cold_if(old, v), near, *far, rows],
        after=after,
    )


def sum_last_kernel(v_ref, near, r1, r2, r3, v_out):
    v_out[...] = total_of(v_ref, near, (r1, r2, r3)).astype(BF16)


def sum_back_kernel(j, count, dv_ref, near, *refs):
    far, (s_ref, r_ref, rows, dv_out, g_out, norms) = refs[:count], refs[count:]
    da = near[...]
    for ref in far:
        da = da + ref[...].astype(F32)
    standard = s_ref[...]
    scaled = da * rows[j : j + 1]
    inner = (
        scaled
        - jnp.mean(scaled, axis=-1, keepdims=True)
        - standard * jnp.mean(scaled * standard, axis=-1, keepdims=True)
    )
    dv = dv_ref[...].astype(F32) + inner * r_ref[...]
    dv_out[...] = dv
    g_out[...] = dv.astype(BF16)
    norms[0:1] = jnp.sum(da * standard, axis=0, keepdims=True)
    norms[1:2] = jnp.sum(da, axis=0, keepdims=True)


def sum_back(j, dv, near, far, s, r, rows, after=(), old=False, new=False):
    return call(
        functools.partial(sum_back_kernel, j, len(far)),
        [*cold_if(new, ROW), ROW16, *cold_if(new, struct((2, 1024), F32))],
        [*cold_if(old, dv), near, *far, *cold_if(old, s, r, rows)],
        after=after,
    )


KEYS = 2 * RING * BLOCK


def block_of(place, b):
    return lax.rem(place[0] - b + RING, RING)


def lay_out_keys(place, own_ref, other_ref, kbuf, vbuf):
    core = place[1]
    for b in range(RING):
        j = block_of(place, b)
        own_at = pl.ds(pl.multiple_of((2 * b + core) * BLOCK, BLOCK), BLOCK)
        other_at = pl.ds(pl.multiple_of((2 * b + 1 - core) * BLOCK, BLOCK), BLOCK)
        for pair in range(2):
            here = slice(pair * 128, pair * 128 + 128)
            kbuf[own_at, here] = own_ref[j, :, 256 * pair : 256 * pair + 128]
            vbuf[own_at, here] = own_ref[j, :, 256 * pair + 128 : 256 * pair + 256]
            theirs = 1 - pair
            kbuf[other_at, here] = other_ref[j, :, 256 * theirs : 256 * theirs + 128]
            vbuf[other_at, here] = other_ref[j, :, 256 * theirs + 128 : 256 * theirs + 256]


def causal_tail(scores, core):
    key_at = lax.broadcasted_iota(jnp.int32, scores.shape, 0)
    query_at = lax.broadcasted_iota(jnp.int32, scores.shape, 1) + core * BLOCK
    return jnp.where(key_at <= query_at, scores, NEG_FILL)


class Tall:
    def __init__(self, *halves):
        self.halves = halves

    def __getitem__(self, key):
        rows, cols = key
        if rows.start is None:
            return jnp.concatenate([half[:, cols] for half in self.halves], axis=0)
        return self.halves[rows.start // 512][rows.start % 512 : rows.stop - 512 * (rows.start // 512), cols]


def qkv_rows(rows, own, far, q_ref, kv_ref):
    weights = (
        jnp.concatenate([own[:, 0:128], far[:, 0:128]], axis=1),
        own[:, 128:384],
        far[:, 128:384],
    )
    for n, weight in enumerate(weights):
        out = mm(rows, weight).astype(BF16)
        for k in range(RING):
            block = out[BLOCK * k : BLOCK * (k + 1)]
            if n == 0:
                q_ref[k] = block
            else:
                kv_ref[k, :, 256 * n - 256 : 256 * n] = block


def qkv_kernel(a0, a1, a2, a3, own0, own1, far0, far1, q_ref, kv_ref):
    own, far = Tall(own0, own1), Tall(far0, far1)
    qkv_rows(stack_rows((a0, a1, a2, a3)), own, far, q_ref, kv_ref)


def first_qkv_kernel(
    x0, x1, x2, x3, own0, own1, far0, far1, norms, q_ref, kv_ref, *refs
):
    outs, (s_ref, r_ref, all_ref) = refs[0:4], refs[4:7]
    own, far = Tall(own0, own1), Tall(far0, far1)
    for k, x_ref in enumerate((x0, x1, x2, x3)):
        x = x_ref[0:BLOCK].astype(F32)
        centred = x - jnp.mean(x, axis=-1, keepdims=True)
        inv = lax.rsqrt(jnp.mean(centred * centred, axis=-1, keepdims=True) + EPSILON)
        standard = centred * inv
        if k == 0:
            s_ref[...] = standard
            r_ref[...] = inv
        all_ref[BLOCK * k : BLOCK * (k + 1)] = standard.astype(BF16)
        outs[k][...] = (standard * norms[0:1] + norms[3:4]).astype(BF16)
    qkv_rows(stack_rows(outs), own, far, q_ref, kv_ref)


def lane_blocks(ref, at, cols):
    return jnp.concatenate(
        [ref[c : c + 128, at : at + 128] for c in range(cols.start, cols.stop, 128)], axis=1
    )


ALL_COLS = slice(0, 1024)


def self_forward_kernel(
    place, q_ref, own_ref, other_ref, w0, w1, w2, w3, o_ref, lse_ref, near, f1, f2, f3, kbuf, vbuf
):
    lay_out_keys(place, own_ref, other_ref, kbuf, vbuf)
    core = place[1]
    for b in range(RING):
        j = block_of(place, b)
        span = 2 * BLOCK * (b + 1)
        head = span - 2 * BLOCK
        for pair in range(2):
            outs = []
            for h in (2 * pair, 2 * pair + 1):
                cols = slice(HD * h, HD * h + HD)
                q = q_ref[j, :, cols] * 0.125
                last = causal_tail(mm_nt(kbuf[head:span, cols], q), core)
                top = jnp.max(last, axis=0, keepdims=True)
                if head:
                    early = mm_nt(kbuf[0:head, cols], q)
                    top = jnp.maximum(top, jnp.max(early, axis=0, keepdims=True))
                    early = jnp.exp(early - top)
                last = jnp.exp(last - top)
                total = jnp.sum(last, axis=0, keepdims=True)
                mixed = mm_tn(vbuf[head:span, cols], last.astype(BF16))
                if head:
                    total = total + jnp.sum(early, axis=0, keepdims=True)
                    mixed = mixed + mm_tn(vbuf[0:head, cols], early.astype(BF16))
                outs.append(mixed / total)
                lse_ref[h, j] = top + jnp.log(total)
            both = jnp.concatenate(outs, axis=0)
            o_ref[j, :, 128 * pair : 128 * pair + 128] = both.T.astype(BF16)
    rows = jnp.concatenate([o_ref[k] for k in range(RING)], axis=0)
    for cols in chunks():
        weight = jnp.concatenate([lane_blocks(w, 384, cols) for w in (Tall(w0, w1), Tall(w2, w3))], axis=0)
        split_rows(mm(rows, weight), (near, f1, f2, f3), cols)


def self_back_kernel(
    place, g0, g1, g2, g3, w0, w1, w2, w3, q_ref, own_ref, other_ref, lse_ref,
    dq_ref, down_ref, dother_ref, kbuf, vbuf, dobuf, dk, dv,
):
    rows = stack_rows((g0, g1, g2, g3))
    weight = jnp.concatenate([lane_blocks(w, 384, ALL_COLS) for w in (Tall(w0, w1), Tall(w2, w3))], axis=0)
    dobuf[...] = mm_nt(rows, weight).astype(BF16).reshape(dobuf.shape)
    lay_out_keys(place, own_ref, other_ref, kbuf, vbuf)
    core = place[1]
    for b in reversed(range(RING)):
        j = block_of(place, b)
        span = 2 * BLOCK * (b + 1)
        head = span - 2 * BLOCK
        for pair in range(2):
            lanes = slice(128 * pair, 128 * pair + 128)
            dqs, dks, dvs = [], [], []
            for h in (2 * pair, 2 * pair + 1):
                cols = slice(HD * h, HD * h + HD)
                q = q_ref[j, :, cols] * 0.125
                do = dobuf[j, :, cols]
                k = kbuf[0:span, cols]
                scores = mm_nt(k, q)
                last = causal_tail(scores[head:span], core)
                scores = jnp.concatenate([scores[0:head], last], axis=0) if head else last
                probs = jnp.exp(scores - lse_ref[h, j])
                dprobs = mm_nt(vbuf[0:span, cols], do)
                delta = jnp.sum(probs * dprobs, axis=0, keepdims=True)
                dscores = (probs * (dprobs - delta)).astype(BF16)
                dqs.append(mm_tn(k, dscores) * 0.125)
                dks.append(mm(dscores, q))
                dvs.append(mm(probs.astype(BF16), do))
            dq_ref[j, :, lanes] = jnp.concatenate(dqs, axis=0).T.astype(BF16)
            dk_new = jnp.concatenate(dks, axis=1)
            dv_new = jnp.concatenate(dvs, axis=1)
            if b == RING - 1:
                dk[0:span, lanes] = dk_new
                dv[0:span, lanes] = dv_new
            else:
                dk[0:span, lanes] += dk_new
                dv[0:span, lanes] += dv_new
    for b in range(RING):
        j = block_of(place, b)
        own_at = pl.ds(pl.multiple_of((2 * b + core) * BLOCK, BLOCK), BLOCK)
        other_at = pl.ds(pl.multiple_of((2 * b + 1 - core) * BLOCK, BLOCK), BLOCK)
        for pair in range(2):
            here = slice(pair * 128, pair * 128 + 128)
            theirs = 1 - pair
            down_ref[j, :, 256 * pair : 256 * pair + 128] = dk[own_at, here]
            down_ref[j, :, 256 * pair + 128 : 256 * pair + 256] = dv[own_at, here]
            dother_ref[j, :, 256 * theirs : 256 * theirs + 128] = dk[other_at, here].astype(BF16)
            dother_ref[j, :, 256 * theirs + 128 : 256 * theirs + 256] = dv[other_at, here].astype(BF16)


def keys_total(down_ref, dother_ref):
    total = [down_ref[k] + dother_ref[k].astype(F32) for k in range(RING)]
    return jnp.concatenate(total, axis=0).astype(BF16)


def self_rows_back_kernel(
    dq_ref, down_ref, dother_ref, own0, own1, far0, far1, near, f1, f2, f3
):
    own, far = Tall(own0, own1), Tall(far0, far1)
    dq = jnp.concatenate([dq_ref[k] for k in range(RING)], axis=0)
    rows = jnp.concatenate([dq, keys_total(down_ref, dother_ref)], axis=1)
    for cols in chunks():
        weight = jnp.concatenate(
            [own[cols, 0:128], far[cols, 0:128], own[cols, 128:384], far[cols, 128:384]], axis=1
        )
        split_rows(mm_nt(rows, weight), (near, f1, f2, f3), cols)


def last_rows_back_kernel(
    dq_ref, down_ref, dother_ref, own0, own1, far0, far1, all_ref, n0, n1, n2, n3, n4,
    near, f1, f2, f3, norms,
):
    own, far = Tall(own0, own1), Tall(far0, far1)
    dq = jnp.concatenate([dq_ref[k] for k in range(RING)], axis=0)
    rows = jnp.concatenate([dq, keys_total(down_ref, dother_ref)], axis=1)
    for n, ref in enumerate((n0, n1, n2, n3, n4), 1):
        norms[2 * n : 2 * n + 2] = ref[...]
    norms[12:16] = jnp.zeros((4, 1024), F32)
    for cols in chunks():
        weight = jnp.concatenate(
            [own[cols, 0:128], far[cols, 0:128], own[cols, 128:384], far[cols, 128:384]], axis=1
        )
        total = mm_nt(rows, weight)
        near[:, cols] = total[0:BLOCK]
        for k, out in enumerate((f1, f2, f3), 1):
            out[0:BLOCK, cols] = total[BLOCK * k : BLOCK * (k + 1)].astype(BF16)
        norms[0:1, cols] = jnp.sum(total * all_ref[:, cols].astype(F32), axis=0, keepdims=True)
        norms[1:2, cols] = jnp.sum(total, axis=0, keepdims=True)
    for out in (f1, f2, f3):
        out[BLOCK : BLOCK + 16] = norms[...].astype(BF16)


def last_sum_back_kernel(dv_ref, near, r1, r2, r3, s_ref, r_ref, rows, norms, g_out, total):
    da = near[...]
    for ref in (r1, r2, r3):
        da = da + ref[0:BLOCK].astype(F32)
    standard = s_ref[...]
    scaled = da * rows[0:1]
    inner = (
        scaled
        - jnp.mean(scaled, axis=-1, keepdims=True)
        - standard * jnp.mean(scaled * standard, axis=-1, keepdims=True)
    )
    g_out[...] = (dv_ref[...].astype(F32) + inner * r_ref[...]).astype(BF16)
    total[...] = norms[...] + sum(ref[BLOCK : BLOCK + 16].astype(F32) for ref in (r1, r2, r3))


def cross_cols(w, layer, place, g, at, rows):
    first = RING * block_of(place, g)
    parts = [
        w[2 * (first + y) + layer, :, at : at + 128]
        for y in range(rows.start // 256, rows.stop // 256)
    ]
    return parts[0] if len(parts) == 1 else jnp.concatenate(parts, axis=0)


def cross_blocks(w, layer, place, g, cols):
    first = RING * block_of(place, g)
    parts = []
    for c in range(cols.start, cols.stop, 128):
        at = c % 256
        parts.append(w[2 * (first + c // 256) + layer, at : at + 128, 128:256])
    return jnp.concatenate(parts, axis=1)


def cross_mask(scores, length):
    slots = lax.broadcasted_iota(jnp.int32, scores.shape, 0)
    return jnp.where(slots < length, scores, NEG_FILL)


def cross_forward_kernel(layer, place, lengths, mine, theirs, *refs):
    w, kv, (q_ref, o_ref, lse_ref, near, far) = refs[0], refs[1:5], refs[5:]
    rows = stack_rows((mine, theirs))
    for g in range(RING):
        lanes = slice(128 * g, 128 * g + 128)
        q_ref[:, lanes] = mm(rows, cross_cols(w, layer, place, g, 0, slice(0, 1024))).astype(BF16)
        outs = []
        for p in range(2):
            h = 2 * g + p
            q = q_ref[:, HD * h : HD * h + HD] * 0.125
            k = kv[g][layer, :, HD * p : HD * p + HD]
            v = kv[g][layer, :, 128 + HD * p : 128 + HD * p + HD]
            scores = cross_mask(mm_nt(k, q), lengths[place[4], 0])
            top = jnp.max(scores, axis=0, keepdims=True)
            raised = jnp.exp(scores - top)
            total = jnp.sum(raised, axis=0, keepdims=True)
            outs.append(mm_tn(v, raised.astype(BF16)) / total)
            lse_ref[h] = top + jnp.log(total)
        o_ref[:, lanes] = jnp.concatenate(outs, axis=0).T.astype(BF16)
    for cols in chunks():
        weight = jnp.concatenate([cross_blocks(w, layer, place, g, cols) for g in range(RING)], axis=0)
        split_rows(mm(o_ref[...], weight), (near, far), cols)


def cross_back_kernel(layer, place, lengths, mine, theirs, *refs):
    w, kv, (q_ref, lse_ref) = refs[0], refs[1:5], refs[5:7]
    dq_ref, dkv, (near, far) = refs[7], refs[8:12], refs[12:14]
    rows = stack_rows((mine, theirs))
    for g in range(RING):
        lanes = slice(128 * g, 128 * g + 128)
        dmixed = mm_nt(rows, cross_blocks(w, layer, place, g, ALL_COLS)).astype(BF16)
        dqs, dks, dvs = [], [], []
        for p in range(2):
            h = 2 * g + p
            q = q_ref[:, HD * h : HD * h + HD] * 0.125
            do = dmixed[:, HD * p : HD * p + HD]
            k = kv[g][layer, :, HD * p : HD * p + HD]
            v = kv[g][layer, :, 128 + HD * p : 128 + HD * p + HD]
            probs = jnp.exp(cross_mask(mm_nt(k, q), lengths[place[4], 0]) - lse_ref[h])
            dprobs = mm_nt(v, do)
            delta = jnp.sum(probs * dprobs, axis=0, keepdims=True)
            dscores = (probs * (dprobs - delta)).astype(BF16)
            dqs.append(mm_tn(k, dscores) * 0.125)
            dks.append(mm(dscores, q))
            dvs.append(mm(probs.astype(BF16), do))
        dq_ref[:, lanes] = jnp.concatenate(dqs, axis=0).T.astype(BF16)
        dkv[g][...] = jnp.concatenate(dks + dvs, axis=1).astype(BF16)
    for cols in chunks():
        weight = jnp.concatenate([cross_cols(w, layer, place, g, 0, cols) for g in range(RING)], axis=1)
        split_rows(mm_nt(dq_ref[...], weight), (near, far), cols)


def up_cols(own, far, at):
    refs, at = (own, at) if at < 512 else (far, at - 512)
    return jnp.concatenate([ref[:, at : at + CHUNK] for ref in refs], axis=0)


def up_rows(own, far, cols):
    half, rows = cols.start // 512, slice(cols.start % 512, cols.start % 512 + CHUNK)
    return jnp.concatenate([own[half][rows, 0:512], far[half][rows, 0:512]], axis=1)


def down_rows(own, far, at):
    refs, at = (own, at) if at < 512 else (far, at - 512)
    return jnp.concatenate([ref[at : at + CHUNK, 512:1024] for ref in refs], axis=1)


def down_cols(own, far, at):
    half, lanes = at // 512, slice(512 + at % 512, 512 + at % 512 + CHUNK)
    return jnp.concatenate([own[half][:, lanes], far[half][:, lanes]], axis=0)


def ffn_forward_kernel(
    a0, a1, a2, a3, own0, own1, far0, far1, hidden_ref, slope_ref, near, f1, f2, f3
):
    own, far = (own0, own1), (far0, far1)
    root = 0.7978845608028654
    rows = stack_rows((a0, a1, a2, a3))
    for cols in chunks():
        pre = mm(rows, up_cols(own, far, cols.start))
        square = pre * pre
        t = jnp.tanh(root * (pre + 0.044715 * pre * square))
        half = 0.5 * (1.0 + t)
        hidden_ref[:, cols] = (pre * half).astype(BF16)
        slope_ref[:, cols] = half + 0.5 * pre * (1.0 - t * t) * (root * (1.0 + 3 * 0.044715 * square))
    for cols in chunks():
        split_rows(mm(hidden_ref[...], down_cols(own, far, cols.start)), (near, f1, f2, f3), cols)


def ffn_back_kernel(
    g0, g1, g2, g3, own0, own1, far0, far1, slope_ref, dpre_ref, near, f1, f2, f3
):
    own, far = (own0, own1), (far0, far1)
    rows = stack_rows((g0, g1, g2, g3))
    for cols in chunks():
        dhidden = mm_nt(rows, down_rows(own, far, cols.start))
        dpre_ref[:, cols] = (dhidden * slope_ref[:, cols]).astype(BF16)
    for cols in chunks():
        split_rows(mm_nt(dpre_ref[...], up_rows(own, far, cols)), (near, f1, f2, f3), cols)


def ffn_grads_kernel(hidden, g0, g1, g2, g3, dpre, a0, a1, a2, a3, ours, t0, t1, t2, t3):
    theirs = (t0, t1, t2, t3)
    g = stack_rows((g0, g1, g2, g3))
    a = stack_rows((a0, a1, a2, a3))
    for n in (2, 3, 0, 1):
        down = mm_tn(hidden[:, CHUNK * n : CHUNK * n + CHUNK], g)
        if n >= 2:
            theirs[n - 2][...] = down.astype(BF16)
        else:
            ours[CHUNK * n : CHUNK * n + CHUNK] = down
    for half in (1, 0):
        for n in range(4):
            up = mm_tn(a[:, CHUNK * n : CHUNK * n + CHUNK], dpre[:, 512 * half : 512 * half + 512])
            lanes = slice(512 * (n // 2), 512 * (n // 2) + 512)
            if half:
                theirs[2 + n % 2][:, lanes] = up.astype(BF16)
            else:
                ours[512 + CHUNK * (n % 2) : 512 + CHUNK * (n % 2) + CHUNK, lanes] = up


def ffn_total(ours, came, rows):
    n, at = rows.start // CHUNK, rows.start % CHUNK
    return ours[rows] + came[n][at : at + rows.stop - rows.start].astype(F32)


def cross_shares(k, g, a, mixed, dq, keys, memory):
    lanes = slice(128 * k, 128 * k + 128)
    return mm_tn(dq[:, lanes], a), mm_tn(mixed[:, lanes], g), mm_tn(keys[...], memory)


def cross_grads_kernel(
    mixed, g_mine, g_theirs, dq, a_mine, a_theirs, k0, k1, k2, k3, b0, b1, b2, b3
):
    g = stack_rows((g_mine, g_theirs))
    a = stack_rows((a_mine, a_theirs))
    for k, (key, out) in enumerate(zip((k0, k1, k2, k3), (b0, b1, b2, b3))):
        lanes = slice(128 * k, 128 * k + 128)
        out[0:128] = mm_tn(dq[:, lanes], a).astype(out.dtype)
        out[128:256] = mm_tn(mixed[:, lanes], g).astype(out.dtype)
        for i in range(4):
            out[256:320, 256 * i : 256 * i + 256] = key[64 * i : 64 * i + 64].astype(out.dtype)


def cross_first_kernel(
    place, ours, q0, q1, q2, q3, mixed, g_mine, g_theirs, dq, a_mine, a_theirs, k0, k1, k2, k3,
    memory, out,
):
    g = stack_rows((g_mine, g_theirs))
    a = stack_rows((a_mine, a_theirs))
    for i in range(8):
        rows = slice(128 * i, 128 * i + 128)
        out[i, 0:128] = ffn_total(ours, (q0, q1, q2, q3), rows).astype(BF16)
    for k, key in enumerate((k0, k1, k2, k3)):
        queries, outs, keys = cross_shares(k, g, a, mixed, dq, key, memory[...])
        for i in range(8):
            part, at = (queries, outs)[i // 4], 32 * (i % 4)
            to = pl.multiple_of(128 + 64 * block_of(place, k), 64)
            out[i, pl.ds(to, 32)] = part[at : at + 32].astype(BF16)
            out[i, pl.ds(pl.multiple_of(to + 32, 32), 32)] = keys[32 * i : 32 * i + 32].astype(BF16)


def self_grads_kernel(
    mixed, g0, g1, g2, g3, dq, down_ref, dother_ref, a0, a1, a2, a3, ours, t0, t1, t2, t3
):
    g = stack_rows((g0, g1, g2, g3))
    a = stack_rows((a0, a1, a2, a3))
    keys = keys_total(down_ref, dother_ref)
    outs, queries = [jnp.concatenate([r[k] for k in range(RING)], axis=0) for r in (mixed, dq)]
    t0[...] = mm_tn(outs[:, 128:256], g).astype(BF16)
    t1[...] = mm_tn(queries[:, 128:256], a).astype(BF16)
    t2[...] = mm_tn(keys[:, 256:384], a).astype(BF16)
    t3[...] = mm_tn(keys[:, 384:512], a).astype(BF16)
    ours[0:128] = mm_tn(outs[:, 0:128], g)
    ours[128:256] = mm_tn(queries[:, 0:128], a)
    ours[256:512] = mm_tn(keys[:, 0:256], a)


def rows_kernel(place, x_ref, memory_ref, g_ref, x, both, g):
    mine = place[4]
    x[...] = x_ref[mine]
    both[0:BLOCK] = x_ref[mine]
    both[BLOCK : BLOCK + 32] = memory_ref[mine]
    g[...] = g_ref[mine]


def norm_rows_kernel(gain, bias, out):
    out[0:3] = gain[0]
    out[3:6] = bias[0]


def both_norms_kernel(place, mine, other, first, second):
    first[...] = jnp.where(place[4] == 0, mine[...], other[...])
    second[...] = jnp.where(place[4] == 0, other[...], mine[...])


def memory_blocks_kernel(x0, x1, x2, x3, out):
    for k, ref in enumerate((x0, x1, x2, x3)):
        out[32 * k : 32 * k + 32] = ref[BLOCK : BLOCK + 32]


def pack_kernel(place, w_ref, out_ref, q_ref, cross_ref, kv_ref, first, second, part, whole):
    for i in range(3):
        whole[:, 128 * i : 128 * i + 128] = w_ref[i]
    for i in range(8):
        rows = slice(128 * i, 128 * i + 128)
        whole[rows, 384:512] = out_ref[:, rows]
        whole[rows, 640:768] = cross_ref[:, rows]
    whole[:, 512:640] = q_ref[...]
    whole[:, 768:1024] = kv_ref[...]
    first[...] = whole[0:512, 0:512]
    second[...] = whole[512:1024, 0:512]
    part[...] = whole[pl.ds(pl.multiple_of(place[2] * 256, 256), 256)]


def pack_ffn_kernel(up_ref, down_ref, out):
    out[:, 0:512] = up_ref[...]
    out[0:512, 512:1024] = down_ref[:, 0:512]
    out[512:1024, 512:1024] = down_ref[:, 512:1024]


def quarter(place, k):
    return pl.ds(pl.multiple_of(lax.rem(place[2] - k + RING, RING) * 256, 256), 256)


def by_section(place, write):
    pl.when(place[4] == 0)(lambda: write(0, 1))
    pl.when(place[4] == 1)(lambda: write(1, 0))


def fill_halves(place, parts, halves, cols):
    for k, ref in enumerate(parts):
        y = lax.rem(place[2] - k + RING, RING)
        rows = pl.ds(pl.multiple_of(lax.rem(y, 2) * 256, 256), 256)

        def put(half, ref=ref, rows=rows):
            halves[half][rows] = ref[:, cols]

        pl.when(y < 2)(functools.partial(put, 0))
        pl.when(y >= 2)(functools.partial(put, 1))


def both_selfs_kernel(
    place, mine0, mine1, r0, r1, r2, r3, a0, a1, b0, b1
):
    def write(own, far):
        halves = ((a0, a1), (b0, b1))
        halves[own][0][...] = mine0[...]
        halves[own][1][...] = mine1[...]
        fill_halves(place, (r0, r1, r2, r3), halves[far], slice(0, 512))

    by_section(place, write)


def rest_kernel(place, mine, other, out, parts):
    def write(own, far):
        parts[own] = mine[:, 512:768]
        parts[far] = other[:, 512:768]

    by_section(place, write)
    out[:, 0:512] = other[:, 0:512]
    out[:, 512:768] = other[:, 768:1024]


def keys_kernel(place, kv_ref, k0, k1, k2, k3, x0, x1, x2, x3, e_far, out, memory, pair):
    for k, ref in enumerate((x0, x1, x2, x3)):
        at = 64 * block_of(place, k)
        memory[pl.ds(pl.multiple_of(at + 32 * place[1], 32), 32)] = ref[BLOCK : BLOCK + 32]
        memory[pl.ds(pl.multiple_of(at + 32 - 32 * place[1], 32), 32)] = e_far[32 * k : 32 * k + 32]
    for k, ref in enumerate((k0, k1, k2, k3)):
        pair[quarter(place, k)] = ref[:, 512:768]
    mine = mm(memory[...], kv_ref[...]).astype(BF16)
    other = mm(memory[...], pair[...]).astype(BF16)

    def write(own, far):
        out[own] = mine
        out[far] = other

    by_section(place, write)


def both_ffns_kernel(place, mine, other, a0, a1, b0, b1):
    def write(own, far):
        halves = ((a0, a1), (b0, b1))
        for half in range(2):
            rows = slice(512 * half, 512 * half + 512)
            halves[own][half][...] = mine[rows]
            halves[far][half][...] = other[rows]

    by_section(place, write)


def cut_chunks(place, total, outs):
    rows = total.shape[0] // 8
    for k, out in enumerate(outs):
        y = lax.rem(place[2] - k + RING, RING)
        for z in range(2):
            at = pl.ds(pl.multiple_of((RING * z + y) * rows, rows), rows)
            out[z] = total[at].astype(out.dtype)


def join_kernel(f, q0, q1, q2, q3, ours, t0, t1, t2, t3, out):
    for i in range(8):
        out[i, 0:128] = ffn_total(f, (q0, q1, q2, q3), slice(128 * i, 128 * i + 128)).astype(BF16)
        theirs = (t0, t1, t2, t3)[i // 2]
        at = 64 * (i % 2)
        out[i, 128:192] = (ours[64 * i : 64 * i + 64] + theirs[at : at + 64].astype(F32)).astype(BF16)


def rest_chunk_kernel(
    place, ours, t0, t1, t2, t3, w0, w1, w2, w3, memory, c0, c1, c2, c3, total
):
    cross = w0[...] + sum(w[...].astype(F32) for w in (w1, w2, w3))
    keys = jnp.concatenate([cross[256:320, 256 * i : 256 * i + 256] for i in range(4)], axis=0)
    keys = mm_tn(keys.astype(BF16), memory[...])
    for i in range(8):
        theirs = (t0, t1, t2, t3)[i // 2]
        at, to = 64 * (i % 2), 128 * i
        total[to : to + 64] = ours[64 * i : 64 * i + 64] + theirs[at : at + 64].astype(F32)
        total[to + 64 : to + 96] = cross[32 * i : 32 * i + 32]
        total[to + 96 : to + 128] = keys[32 * i : 32 * i + 32]
    cut_chunks(place, total, (c0, c1, c2, c3))


def split_kernel(grads, ffn, cross):
    ffn[...] = grads[0:128]
    cross[...] = grads[128:384]


def chunk_shapes(rows):
    return [Cold(struct((2, rows, 1024), F32))] + [struct((2, rows, 1024), BF16)] * 3


def sum_y_kernel(place, c0, r1, r2, r3, first, ffn, cross, keep, over_z, over_s):
    z = place[3]

    def half(n):
        return c0[n] + sum(r[n].astype(F32) for r in (r1, r2, r3))

    over_z[...] = half(1 - z).astype(BF16)
    rest = half(z)

    def write_first():
        keep[0:128] = rest
        keep[128:256] = first[0:128].astype(F32)
        over_s[0:64] = first[128:192]
        over_s[64:128] = cross[...]
        over_s[128:256] = ffn[...]

    def write_second():
        keep[0:64] = first[128:192].astype(F32)
        keep[64:128] = cross[...].astype(F32)
        keep[128:256] = ffn[...].astype(F32)
        over_s[0:128] = rest.astype(BF16)
        over_s[128:256] = first[0:128]

    pl.when(place[4] == 0)(write_first)
    pl.when(place[4] == 1)(write_second)


def sum_rest_kernel(place, keep, from_z, from_s, from_both, norms, came, out):
    rest = keep[0:128] + from_s[0:128].astype(F32)
    other = from_z[...].astype(F32) + from_both[...].astype(F32)
    out[0:128] = jnp.where(place[4] == 0, rest + other, rest).astype(BF16)
    out[128:144] = (norms[...] + came[...]).astype(BF16)
    out[144:272] = (keep[128:256] + from_s[128:256].astype(F32)).astype(BF16)


def exchange(over_z, over_s):
    from_both = lax.ppermute(over_z, ("section", "dz"), [(2, 1), (3, 0)])
    return swap(over_z, "dz"), swap(over_s, "section"), from_both


def norms_kernel(place, all_ref, keep, over_s):
    total = sum(all_ref[272 * i + 128 : 272 * i + 144].astype(F32) for i in range(8))
    first, second = total[0:6], total[6:12]
    keep[0:6] = jnp.where(place[4] == 0, first, second)
    over_s[0:6] = jnp.where(place[4] == 0, second, first)
    keep[6:8] = jnp.zeros((2, 1024), F32)
    over_s[6:8] = jnp.zeros((2, 1024), F32)


def last_norms_kernel(mine, came, gains, biases, ffn):
    norms = mine[...] + came[...]
    for j in range(2):
        gains[j : j + 1] = norms[2 * j : 2 * j + 1]
        biases[j : j + 1] = norms[2 * j + 1 : 2 * j + 2]
    ffn[...] = norms[4:6]


def last_kernel(
    all_ref, out_ref, self_ref, q_ref, cross_ref, kv_ref, up_ref, down_ref
):
    def rows(at, count, span):
        return jnp.concatenate(
            [all_ref[272 * i + at : 272 * i + at + span] for i in range(count, count + 128 // span)],
            axis=0,
        ).astype(F32)

    out_ref[...] = rows(0, 0, 64)
    for i in range(3):
        self_ref[i] = rows(0, 2 + 2 * i, 64).T
    q_ref[...] = rows(64, 0, 32).T
    cross_ref[...] = rows(64, 4, 32)
    kv_ref[pl.ds(0, 1024, stride=2)] = rows(96, 0, 32).T
    kv_ref[pl.ds(1, 1024, stride=2)] = rows(96, 4, 32).T
    for i in range(4):
        here = slice(128 * i, 128 * i + 128)
        down_ref[here] = rows(144, i, 128)
        up = rows(144, 4 + i, 128)
        up_ref[here] = up[:, 0:512]
        up_ref[512 + 128 * i : 640 + 128 * i] = up[:, 512:1024]


def other_layer_kernel(place, first, second, out):
    out[...] = jnp.where(place[4] == 0, second[...], first[...])


def both_batches_kernel(place, first, second, came, out):
    mine = place[4]
    out[mine] = jnp.where(mine == 0, first[...], second[...])
    out[1 - mine] = came[...]


def last_ffn_kernel(whole, up_ref, down_ref):
    down_ref[...] = whole[0:512].astype(F32)
    up_ref[0:512] = whole[512:1024, 0:512].astype(F32)
    up_ref[512:1024] = whole[512:1024, 512:1024].astype(F32)


def layer_forward(layer, v, first, weights, ffns, place, lengths, rows, after):
    own, far, cross, kv = weights
    heads = [struct((RING, BLOCK, 256), BF16), struct((RING, BLOCK, 512), BF16)]
    if layer == 0:
        q, kv_self, *rest = call(
            first_qkv_kernel,
            heads + cold(*[ROW16] * RING, ROW, COLUMN, struct((RING * BLOCK, 1024), BF16)),
            [*cold(*first, *own, *far), rows],
            after=after.get("qkv", ()),
        )
        full1, (s1, r1, all1) = rest[0:4], rest[4:7]
    else:
        a1, s1, r1, all1 = *first, None
        full1 = gather_x(a1)
        q, kv_self = call(qkv_kernel, heads, [*full1, *cold(*own, *far)], after=after.get("qkv", ()))
    kv_other = swap(kv_self, "core")
    if "keys" in after:
        after["keys"](q)
    mixed1, lse1, *sent = call(
        self_forward_kernel,
        cold_if(not layer, struct((RING, BLOCK, 256), BF16), struct((4, RING, 1, BLOCK), F32)) + SENT,
        [q, kv_self, kv_other, *cold(*own, *far)],
        scalars=[place],
        scratch=[pltpu.VMEM((KEYS, 256), BF16), pltpu.VMEM((KEYS, 256), BF16)],
        after=after.get("self", ()),
    )
    waits = after["sum1"](mixed1) if "sum1" in after else ()
    v1, a2, s2, r2 = sum_norm(1, v, sent[0], send_x(sent[1:]), rows, ROW, after=waits, new=not layer)
    a2_theirs = swap(a2, "core")
    cq, mixed2, lse2, near, far2 = call(
        functools.partial(cross_forward_kernel, layer),
        [
            struct((2 * BLOCK, 512), BF16),
            struct((2 * BLOCK, 512), BF16),
            struct((2 * RING, 1, 2 * BLOCK), F32),
            ROW,
            ROW16,
        ],
        [a2, a2_theirs, *cold(cross, *kv[0:4])],
        scalars=[place, lengths],
        after=after.get("cross", ()),
    )
    v2, a3, s3, r3 = sum_norm(
        2, v1, near, [swap(far2, "core")], rows, ROW, after=after.get("sum2", ()), old=not layer
    )
    full3 = gather_x(a3)
    hidden, slope, *sent = call(
        ffn_forward_kernel,
        [struct((RING * BLOCK, 1024), BF16), struct((RING * BLOCK, 1024), F32)] + SENT,
        [*full3, *cold(*ffns[layer])],
        after=after.get("ffn", ()),
    )
    stored = (
        (s1, r1, full1, q, kv_self, kv_other, mixed1, lse1, all1),
        (s2, r2, a2, a2_theirs, cq, mixed2, lse2),
        (s3, r3, full3, hidden, slope),
    )
    return v2, sent[0], send_x(sent[1:]), stored


def layer_back(layer, dv, full_g3, stored, weights, ffns, place, lengths, rows, steps):
    own, far, cross, kv = weights
    (s1, r1, full1, q, kv_self, kv_other, mixed1, lse1, all1), second, third = stored
    s2, r2, a2, a2_theirs, cq, mixed2, lse2 = second
    s3, r3, full3, hidden, slope = third
    old = layer == 0
    dpre, *sent = call(
        ffn_back_kernel,
        [struct((RING * BLOCK, 1024), BF16)] + SENT,
        [*full_g3, *cold(*ffns[layer]), *cold_if(old, slope)],
        after=steps.get("ffn", ()),
    )
    ffn_ours, *ffn_theirs = call(
        ffn_grads_kernel,
        [struct((1024, 1024), F32)] + [struct((CHUNK, 1024), BF16)] * 4,
        [*cold_if(old, hidden), *full_g3, dpre, *cold_if(old, *full3)],
    )
    ffn_parts = [ffn_ours, *(swap(part, "core") for part in ffn_theirs)]
    dv2, g2, norms3 = sum_back(
        2, dv, sent[0], send_x(sent[1:]), s3, r3, rows,
        after=[ffn_theirs[0], *steps.get("sum3", ())], old=old, new=old,
    )
    g2_theirs = swap(g2, "core")
    pair_keys = struct((2 * BLOCK, 256), BF16)
    dcq, *rest = call(
        functools.partial(cross_back_kernel, layer),
        [struct((2 * BLOCK, 512), BF16)] + [pair_keys] * RING + [ROW, ROW16],
        [g2, g2_theirs, *cold(cross, *kv[0:4]), *cold_if(old, cq, lse2)],
        scalars=[place, lengths],
        after=steps.get("cross", lambda parts, g2: ())(ffn_parts, g2),
    )
    dkv_cross, (near, far2) = rest[:RING], rest[RING:]
    dv1, g1, norms2 = sum_back(1, dv2, near, [swap(far2, "core")], s2, r2, rows, old=old, new=True)
    full_g1 = gather_x(g1)
    cross_grads = [*cold_if(old, mixed2), g2, g2_theirs, dcq, *cold_if(old, a2, a2_theirs), *dkv_cross]
    middle, waits = steps["middle"](ffn_parts, cross_grads, g1)
    dq, dkv_own, dkv_theirs = call(
        self_back_kernel,
        [
            struct((RING, BLOCK, 256), BF16),
            struct((RING, BLOCK, 512), F32),
            struct((RING, BLOCK, 512), BF16),
        ],
        [*full_g1, *cold(*own, *far, q, kv_self, kv_other, lse1)],
        scalars=[place],
        scratch=[
            pltpu.VMEM((KEYS, 256), BF16),
            pltpu.VMEM((KEYS, 256), BF16),
            pltpu.VMEM((RING, BLOCK, 256), BF16),
            pltpu.VMEM((KEYS, 256), F32),
            pltpu.VMEM((KEYS, 256), F32),
        ],
        after=waits,
    )
    back = [dq, dkv_own, swap(dkv_theirs, "core")]

    def self_grads(waits=()):
        ours, *theirs = call(
            self_grads_kernel,
            [struct((512, 1024), F32)] + [struct((BLOCK, 1024), BF16)] * 4,
            [*cold(mixed1), *full_g1, *back, *cold(*full1)],
            after=waits,
        )
        return [ours, *(swap(part, "core") for part in theirs)], theirs

    if layer == 0:
        self_parts, theirs = self_grads([*middle[1:4], *steps["before"]])
        waits = steps["late"](middle, self_parts, theirs)
        tall = struct((BLOCK + 16, 1024), BF16)
        near, *others, sums = call(
            last_rows_back_kernel,
            [ROW, tall, tall, tall, struct((16, 1024), F32)],
            [*back, *cold(*own, *far, all1, norms2, norms3, *steps["norms"])],
            after=waits,
        )
        steps["tail"]["near"] = near
        g0, sums = call(
            last_sum_back_kernel,
            [ROW16, struct((16, 1024), F32)],
            [*cold(dv1), near, *send_x(others), *cold(s1, r1, rows, sums)],
        )
        return g0, middle, self_parts, sums
    else:
        sent = call(self_rows_back_kernel, SENT, [*back, *cold(*own, *far)])
        self_parts, theirs = self_grads()
        waits = [theirs[0], *steps["late"]()]
    dv0, g0, norms1 = sum_back(
        0, dv1, sent[0], send_x(sent[1:]), s1, r1, rows, after=waits, old=True
    )
    return g0, middle, self_parts, (norms1, norms2, norms3)


def reduce_dp(grads):
    total = lax.psum_scatter(grads, ("dz", "dy"), scatter_dimension=0, tiled=True)
    return total.reshape(grads.shape[1:])


def shards(
    inputs,
    memory_states,
    source_lengths,
    cotangent,
    norm_gain,
    norm_bias,
    w_self,
    w_self_out,
    w_cross_q,
    w_cross_kv,
    w_cross_out,
    up_weight,
    down_weight,
):
    place = PLACE

    def along_y(part):
        return [part] + [shift(part, "dy", k) for k in range(1, RING)]

    row16 = struct((BLOCK, 1024), BF16)
    kv_mine = w_cross_kv[0].reshape(w_cross_kv.shape[1], -1)
    half = struct((512, 512), BF16)
    *self_mine, mine = call(
        pack_kernel,
        [*cold(half, half), struct((256, 1024), BF16)],
        cold(w_self[0].transpose(1, 0, 2), w_self_out[0], w_cross_q[0], w_cross_out[0], kv_mine),
        scalars=[place],
        scratch=[pltpu.VMEM((1024, 1024), BF16)],
    )
    other = swap(mine, "section")
    x, rows_first, g_top = call(
        rows_kernel,
        cold(row16, struct((BLOCK + 32, 1024), BF16), row16),
        cold(inputs[:, :, 0], memory_states[:, :, 0], cotangent[:, :, 0]),
        scalars=[place],
        after=[mine],
    )
    norms = call(
        norm_rows_kernel, [struct((6, 1024), F32)], [norm_gain, norm_bias], after=[mine]
    )[0]
    norms_other = swap(norms, "section")
    rows_first = gather_x(rows_first)
    ffn_half = struct((512, 1024), BF16)
    ffn_mine, ffn_done = call(
        pack_ffn_kernel,
        cold(struct((1024, 1024), BF16)),
        cold(up_weight[0], down_weight[0]),
        after=[other, *rows_first[1:]],
        token=True,
    )
    ffn_other = swap(ffn_mine, "section")
    norms = call(
        both_norms_kernel, [struct((6, 1024), F32)] * 2, [norms, norms_other], scalars=[place]
    )

    rest, parts = call(
        rest_kernel,
        [struct((256, 768), BF16), Cold(struct((2, 256, 256), BF16))],
        [mine, other],
        scalars=[place],
        after=[norms_other, *rows_first[1:]],
    )
    rests = along_y(rest)
    e_far = swap(call(memory_blocks_kernel, [row16], rows_first)[0], "core")
    a0, a1, b0, b1 = call(
        both_selfs_kernel,
        [half, half, *cold(half, half)],
        [*cold(*self_mine), *rests],
        scalars=[place],
        after=[e_far, norms[0], ffn_done],
    )
    selfs = [(a0, a1), (b0, b1)]
    selfs_far = [tuple(swap(w, "core") for w in pair) for pair in selfs]
    crosses = lax.all_gather(parts, ("tx", "dy"), axis=0, tiled=True)
    ffns, kvs = [], []

    def make_keys(q):
        keyed, memory = call(
            keys_kernel,
            cold(struct((2, 256, 256), BF16), struct((256, 1024), BF16)),
            cold(kv_mine, *rests, *rows_first, e_far),
            scalars=[place],
            scratch=[pltpu.VMEM((1024, 256), BF16)],
            after=[q],
        )
        kvs.extend(gather_x(keyed))
        kvs.append(memory)


    def made(mixed):
        a0, a1, b0, b1, done = call(
            both_ffns_kernel,
            cold(*[ffn_half] * 4),
            cold(ffn_mine, ffn_other),
            scalars=[place],
            after=[mixed],
            token=True,
        )
        for first, second in ((a0, a1), (b0, b1)):
            ffns.append((first, second, swap(first, "core"), swap(second, "core")))
        return [done]

    weights = [(selfs[i], selfs_far[i], crosses, kvs) for i in range(2)]

    v, near, far, stored0 = layer_forward(
        0, x, rows_first, weights[0], ffns, place, source_lengths, norms[0], {"keys": make_keys, "sum1": lambda mixed: [*kvs[1:4], *made(mixed)]}
    )
    text, *normed = sum_norm(0, v, near, far, norms[1], ROW16)
    v, near, far, stored1 = layer_forward(
        1, text, normed, weights[1], ffns, place, source_lengths, norms[1], {}
    )
    memory = kvs[4]
    full_top = gather_x(g_top)
    unit = call(sum_last_kernel, cold(ROW16), [*cold(v), near, *far])[0]

    def middle_second(ffn_parts, cross_grads, after):
        out, done = call(
            cross_first_kernel,
            cold(struct((8, 384, 1024), BF16)),
            [*ffn_parts, *cross_grads, *cold(memory)],
            scalars=[place],
            after=[after],
            token=True,
        )
        return out, [done]

    def by_layer(first, second, after=()):
        lacks = call(other_layer_kernel, [row16], cold(first, second), scalars=[place], after=after)[0]
        return [*cold(first, second), swap(lacks, "section")]

    def both_batches(parts, after=()):
        return call(
            both_batches_kernel,
            cold(struct((2, BLOCK, 1024), BF16)),
            parts,
            scalars=[place],
            after=after,
        )[0]

    states = by_layer(text, unit, ())
    text_grad, grads_a, self1, norms1 = layer_back(
        1, g_top, full_top, stored1, weights[1], ffns, place, source_lengths, norms[1],
        {
            "ffn": full_top[1:],
            "sum3": [unit],
            "middle": middle_second,
            "late": lambda: (),
        },
    )
    grads_a = reduce_dp(grads_a)

    tail = {}

    def join(ffn_parts, g2):
        tail["joined"], done = call(
            join_kernel,
            cold(struct((8, 192, 1024), BF16)),
            [*ffn_parts, *self1],
            after=[g2],
            token=True,
        )
        return [done]

    def middle_first(ffn_parts, cross_grads, after):
        own, *sent = call(
            cross_grads_kernel,
            [struct((320, 1024), F32)] + [struct((320, 1024), BF16)] * 3,
            cross_grads,
            after=[after],
        )
        return [own, *send_x(sent)], [own]

    def late_first(cross_parts, self_parts, theirs):
        tail["chunks"] = call(
            rest_chunk_kernel,
            chunk_shapes(128),
            [*self_parts, *cross_parts, *cold(memory)],
            scalars=[place],
            scratch=[pltpu.VMEM((1024, 1024), F32)],
        )
        return [tail["chunks"][0]]

    input_grad, _, _, norms = layer_back(
        0, text_grad, gather_x(text_grad), stored0, weights[0], ffns, place, source_lengths, norms[0],
        {
            "cross": join,
            "middle": middle_first,
            "late": late_first,
            "norms": norms1,
            "tail": tail,
            "before": [states[2]],
        },
    )
    grads_b = reduce_dp(tail["joined"])
    ffn1, cross1 = call(
        split_kernel,
        cold(row16, struct((256, 1024), BF16)),
        cold(grads_a),
        after=[tail["near"]],
    )
    cross1 = lax.psum_scatter(cross1, "tx", scatter_dimension=0, tiled=True)
    chunks_of = tail["chunks"]
    arrived = [shift(c, "dy", -k) for k, c in enumerate(chunks_of[1:], 1)]
    two = struct((256, 1024), F32)
    keep, over_z, over_s = call(
        sum_y_kernel,
        [Cold(two), row16, struct((256, 1024), BF16)],
        [*cold(chunks_of[0]), *arrived, *cold(grads_b, ffn1, cross1)],
        scalars=[place],
        after=[tail["near"]],
    )
    last = call(
        sum_rest_kernel,
        cold(struct((272, 1024), BF16)),
        [*cold(keep), *exchange(over_z, over_s), norms, swap(norms, "core")],
        scalars=[place],
    )[0]
    whole = lax.all_gather(last, ("dz", "dy"), axis=0, tiled=True)
    states = both_batches(states)
    input_parts = by_layer(input_grad, text_grad, ())
    eight, pair32 = struct((8, 1024), F32), struct((2, 1024), F32)
    own, over_s = call(
        norms_kernel, [eight] * 2, cold(whole), scalars=[place], after=[states]
    )
    grad_out, grad_self, grad_cq, grad_co, grad_ckv, grad_up, grad_down, done = call(
        last_kernel,
        cold(
            struct((128, 1024), F32),
            struct((3, 1024, 128), F32),
            struct((1024, 128), F32),
            struct((128, 1024), F32),
            struct((2048, 128), F32),
            struct((1024, 512), F32),
            struct((512, 1024), F32),
        ),
        cold(whole),
        after=[own],
        token=True,
    )
    input_grads = both_batches(input_parts, [done])
    grad_gain, grad_bias, grad_ffn = call(
        last_norms_kernel, [pair32] * 3, [own, swap(over_s, "section")], after=[done]
    )
    return (
        states[None, :, :, None],
        input_grads[None, :, :, None],
        grad_gain[None],
        grad_bias[None],
        grad_ffn[None],
        grad_self.transpose(1, 0, 2)[None],
        grad_out[None],
        grad_cq[None],
        grad_ckv.reshape(1, 1024, 2, 128),
        grad_co[None],
        grad_up[None],
        grad_down[None],
    )


def solution(mesh):
    sections = mesh.devices.shape[0]
    fine = Mesh(
        mesh.devices.reshape(sections, 2, RING, RING, 2), ("section", "dz", "dy", "tx", "core")
    )
    dp, tensor = ("dz", "dy"), ("tx", "core")
    rows = P(None, tensor, dp, None)
    return jax.shard_map(
        shards,
        mesh=fine,
        in_specs=(
            rows,
            rows,
            P(None, dp),
            rows,
            P("section", None, None),
            P("section", None, None),
            P("section", None, None, tensor),
            P("section", tensor, None),
            P("section", None, tensor),
            P("section", None, None, tensor),
            P("section", tensor, None),
            P("section", None, tensor),
            P("section", tensor, None),
        ),
        out_specs=(
            P("section", None, tensor, dp, None),
            P("section", None, tensor, dp, None),
            P("section", None, None),
            P("section", None, None),
            P("section", None, None),
            P("section", None, None, tensor),
            P("section", tensor, None),
            P("section", None, tensor),
            P("section", None, None, tensor),
            P("section", tensor, None),
            P("section", None, tensor),
            P("section", tensor, None),
        ),
        check_vma=False,
    )
```

```python
import functools
import math

import jax
import jax.numpy as jnp
from jax import lax
from jax.experimental import pallas as pl
from jax.experimental.pallas import tpu as pltpu
from jax.sharding import Mesh, PartitionSpec as P

HD = 64
EPSILON = 1e-05
NEG_FILL = -1000000000.0
BLOCK = 128
RING = 4
BF16 = jnp.bfloat16
F32 = jnp.float32


def shift(value, axis, steps):
    count = lax.axis_size(axis)
    return lax.ppermute(value, axis, [(i, (i + steps) % count) for i in range(count)])


def swap(value, axis):
    return shift(value, axis, 1)


def dot(a, b, dims):
    return lax.dot_general(a, b, ((dims[0], dims[1]), ((), ())), preferred_element_type=F32)


def mm(a, b):
    return dot(a, b, ((1,), (0,)))


def mm_nt(a, b):
    return dot(a, b, ((1,), (1,)))


def mm_tn(a, b):
    return dot(a, b, ((0,), (0,)))


def gather_x(value):
    return [value] + [shift(value, "tx", k) for k in range(1, RING)]


def send_x(others):
    return [shift(block, "tx", -k) for k, block in enumerate(others, 1)]


SMEM = pl.BlockSpec(memory_space=pltpu.SMEM)
VMEM = pl.BlockSpec(memory_space=pltpu.VMEM)
ANY = pl.BlockSpec(memory_space=pl.ANY)
HBM = pl.BlockSpec(memory_space=pltpu.HBM)
CHUNK = 256


def struct(shape, dtype):
    return jax.ShapeDtypeStruct(shape, dtype)


class Cold:
    def __init__(self, array):
        self.array = array


class Awaited:
    def __init__(self, buffer, move):
        self.buffer, self.move = buffer, move
        self.shape, self.dtype = buffer.shape, buffer.dtype

    def arrived(self):
        if self.move is not None:
            self.move.wait()
            self.move = None
        return self.buffer

    def __getitem__(self, key):
        return self.arrived()[key]


def cold(*arrays):
    return [Cold(array) for array in arrays]


def cold_if(flag, *arrays):
    return cold(*arrays) if flag else list(arrays)


def vmem(o):
    return pltpu.VMEM(o.shape, o.dtype)


class Place:
    axes = ("tx", "core", "dy", "dz", "section")

    def __getitem__(self, at):
        return lax.axis_index(self.axes[at])


PLACE = Place()


def settled(array):
    return pltpu.with_memory_space_constraint(array, pltpu.HBM)


def call(kernel, outs, operands, scalars=(), scratch=(), after=(), room=8, token=False, lazy=True):
    ins = [o if isinstance(o, Cold) else None for o in operands]
    arrays = [o.array if isinstance(o, Cold) else o for o in operands]
    puts = [o if isinstance(o, Cold) else None for o in outs]
    shapes = [o.array if isinstance(o, Cold) else o for o in outs]
    if token:
        puts.append(None)
        shapes.append(struct((8, 128), F32))
    placed = any(o is PLACE for o in scalars)
    scalars = [o for o in scalars if o is not PLACE]
    first, waits = len(scalars), len(after)
    large = [a.size * a.dtype.itemsize >= 2**21 for a in after]
    last = first + len(arrays)
    brought = [vmem(o.array) for o in ins if o]
    taken = [vmem(o.array) for o in puts if o]
    held = sum(math.prod(o.shape) * o.dtype.itemsize for o in (*scratch, *brought, *taken))
    name = kernel.func.__name__ if isinstance(kernel, functools.partial) else kernel.__name__

    def body(*refs):
        given = list(refs[first:last])
        results = list(refs[last + waits : last + waits + len(shapes)])
        rest = list(refs[last + waits + len(shapes) :])
        semaphores = rest.pop() if brought or taken else None
        buffers = rest[len(scratch) :]
        moves, stores = [], []
        for at, o in enumerate(ins):
            if o:
                buffer = buffers[len(moves)]
                moves.append(
                    pltpu.make_async_copy(given[at], buffer, semaphores.at[len(moves)])
                )
                moves[-1].start()
                given[at] = buffer
        for at, o in enumerate(puts):
            if o:
                n = len(moves) + len(stores)
                stores.append(pltpu.make_async_copy(buffers[n], results[at], semaphores.at[n]))
                results[at] = buffers[n]
        for at, o in enumerate(ins):
            if o and lazy:
                given[at] = Awaited(given[at], moves[sum(1 for p in ins[:at] if p)])
        for move in () if lazy else moves:
            move.wait()
        if token:
            results.pop()[...] = jnp.zeros((8, 128), F32)
        lead = [PLACE] if placed else []
        kernel(*lead, *refs[:first], *given, *results, *rest[: len(scratch)])
        for ref in given:
            if isinstance(ref, Awaited):
                ref.arrived()
        for store in stores:
            store.start()
        for store in stores:
            store.wait()

    kept = [*scratch, *brought, *taken]
    if brought or taken:
        kept.append(pltpu.SemaphoreType.DMA((len(brought) + len(taken),)))
    return pl.pallas_call(
        body,
        name=name,
        out_shape=[pltpu.HBM(o.shape, o.dtype) if c else o for o, c in zip(shapes, puts)],
        in_specs=[SMEM] * first + [HBM if o else VMEM for o in ins] + [HBM if b else ANY for b in large],
        out_specs=[HBM if o else VMEM for o in puts],
        scratch_shapes=kept,
        compiler_params=pltpu.CompilerParams(vmem_limit_bytes=held + room * 1024 * 1024),
    )(*scalars, *(settled(a) if c else a for a, c in zip(arrays, ins)),
      *(settled(a) if b else a for a, b in zip(after, large)))


ROW = struct((BLOCK, 1024), F32)
ROW16 = struct((BLOCK, 1024), BF16)
COLUMN = struct((BLOCK, 1), F32)
SENT = [ROW] + [ROW16] * (RING - 1)


def stack_rows(refs, cols=slice(None)):
    return jnp.concatenate([ref[:, cols] for ref in refs], axis=0)


def split_rows(total, outs, cols):
    outs[0][:, cols] = total[0:BLOCK]
    for k in range(1, len(outs)):
        outs[k][:, cols] = total[BLOCK * k : BLOCK * (k + 1)].astype(BF16)


def chunks(width=1024):
    return [slice(at, at + CHUNK) for at in range(0, width, CHUNK)]


def norm(v, gain, bias, a_ref, s_ref, r_ref):
    average = jnp.mean(v, axis=-1, keepdims=True)
    centred = v - average
    inv = lax.rsqrt(jnp.mean(centred * centred, axis=-1, keepdims=True) + EPSILON)
    standard = centred * inv
    s_ref[...] = standard
    r_ref[...] = inv
    a_ref[...] = (standard * gain + bias).astype(BF16)


def total_of(v_ref, near, far):
    total = v_ref[...].astype(F32) + near[...]
    for ref in far:
        total = total + ref[...].astype(F32)
    return total


def sum_norm_kernel(j, count, v_ref, near, *refs):
    far, (rows, v_out, a_ref, s_ref, r_ref) = refs[:count], refs[count:]
    v = total_of(v_ref, near, far)
    v_out[...] = v.astype(v_out.dtype)
    v = v_out[...].astype(F32)
    norm(v, rows[j : j + 1], rows[3 + j : 4 + j], a_ref, s_ref, r_ref)


def sum_norm(j, v, near, far, rows, kept, after=(), old=False, new=False):
    outs = [*cold_if(new, kept), ROW16, *cold_if(new, ROW, COLUMN)]
    return call(
        functools.partial(sum_norm_kernel, j, len(far)),
        outs,
        [*cold_if(old, v), near, *far, rows],
        after=after,
    )


def sum_last_kernel(v_ref, near, r1, r2, r3, v_out):
    v_out[...] = total_of(v_ref, near, (r1, r2, r3)).astype(BF16)


def sum_back_kernel(j, count, dv_ref, near, *refs):
    far, (s_ref, r_ref, rows, dv_out, g_out, norms) = refs[:count], refs[count:]
    da = near[...]
    for ref in far:
        da = da + ref[...].astype(F32)
    standard = s_ref[...]
    scaled = da * rows[j : j + 1]
    inner = (
        scaled
        - jnp.mean(scaled, axis=-1, keepdims=True)
        - standard * jnp.mean(scaled * standard, axis=-1, keepdims=True)
    )
    dv = dv_ref[...].astype(F32) + inner * r_ref[...]
    dv_out[...] = dv
    g_out[...] = dv.astype(BF16)
    norms[0:1] = jnp.sum(da * standard, axis=0, keepdims=True)
    norms[1:2] = jnp.sum(da, axis=0, keepdims=True)


def sum_back(j, dv, near, far, s, r, rows, after=(), old=False, new=False):
    return call(
        functools.partial(sum_back_kernel, j, len(far)),
        [*cold_if(new, ROW), ROW16, *cold_if(new, struct((2, 1024), F32))],
        [*cold_if(old, dv), near, *far, *cold_if(old, s, r, rows)],
        after=after,
    )


KEYS = 2 * RING * BLOCK


def block_of(place, b):
    return lax.rem(place[0] - b + RING, RING)


def lay_out_keys(place, own_ref, other_ref, kbuf, vbuf):
    core = place[1]
    for b in range(RING):
        j = block_of(place, b)
        own_at = pl.ds(pl.multiple_of((2 * b + core) * BLOCK, BLOCK), BLOCK)
        other_at = pl.ds(pl.multiple_of((2 * b + 1 - core) * BLOCK, BLOCK), BLOCK)
        for pair in range(2):
            here = slice(pair * 128, pair * 128 + 128)
            kbuf[own_at, here] = own_ref[j, :, 256 * pair : 256 * pair + 128]
            vbuf[own_at, here] = own_ref[j, :, 256 * pair + 128 : 256 * pair + 256]
            theirs = 1 - pair
            kbuf[other_at, here] = other_ref[j, :, 256 * theirs : 256 * theirs + 128]
            vbuf[other_at, here] = other_ref[j, :, 256 * theirs + 128 : 256 * theirs + 256]


def causal_tail(scores, core):
    key_at = lax.broadcasted_iota(jnp.int32, scores.shape, 0)
    query_at = lax.broadcasted_iota(jnp.int32, scores.shape, 1) + core * BLOCK
    return jnp.where(key_at <= query_at, scores, NEG_FILL)


class Tall:
    def __init__(self, *halves):
        self.halves = halves

    def __getitem__(self, key):
        rows, cols = key
        if rows.start is None:
            return jnp.concatenate([half[:, cols] for half in self.halves], axis=0)
        return self.halves[rows.start // 512][rows.start % 512 : rows.stop - 512 * (rows.start // 512), cols]


def qkv_rows(rows, own, far, q_ref, kv_ref):
    weights = (
        jnp.concatenate([own[:, 0:128], far[:, 0:128]], axis=1),
        own[:, 128:384],
        far[:, 128:384],
    )
    for n, weight in enumerate(weights):
        out = mm(rows, weight).astype(BF16)
        for k in range(RING):
            block = out[BLOCK * k : BLOCK * (k + 1)]
            if n == 0:
                q_ref[k] = block
            else:
                kv_ref[k, :, 256 * n - 256 : 256 * n] = block


def qkv_kernel(a0, a1, a2, a3, own0, own1, far0, far1, q_ref, kv_ref):
    own, far = Tall(own0, own1), Tall(far0, far1)
    qkv_rows(stack_rows((a0, a1, a2, a3)), own, far, q_ref, kv_ref)


def first_qkv_kernel(
    x0, x1, x2, x3, own0, own1, far0, far1, norms, q_ref, kv_ref, *refs
):
    outs, (s_ref, r_ref, all_ref) = refs[0:4], refs[4:7]
    own, far = Tall(own0, own1), Tall(far0, far1)
    for k, x_ref in enumerate((x0, x1, x2, x3)):
        x = x_ref[0:BLOCK].astype(F32)
        centred = x - jnp.mean(x, axis=-1, keepdims=True)
        inv = lax.rsqrt(jnp.mean(centred * centred, axis=-1, keepdims=True) + EPSILON)
        standard = centred * inv
        if k == 0:
            s_ref[...] = standard
            r_ref[...] = inv
        all_ref[BLOCK * k : BLOCK * (k + 1)] = standard.astype(BF16)
        outs[k][...] = (standard * norms[0:1] + norms[3:4]).astype(BF16)
    qkv_rows(stack_rows(outs), own, far, q_ref, kv_ref)


def lane_blocks(ref, at, cols):
    return jnp.concatenate(
        [ref[c : c + 128, at : at + 128] for c in range(cols.start, cols.stop, 128)], axis=1
    )


ALL_COLS = slice(0, 1024)


def self_forward_kernel(
    place, q_ref, own_ref, other_ref, w0, w1, w2, w3, o_ref, lse_ref, near, f1, f2, f3, kbuf, vbuf
):
    lay_out_keys(place, own_ref, other_ref, kbuf, vbuf)
    core = place[1]
    for b in range(RING):
        j = block_of(place, b)
        span = 2 * BLOCK * (b + 1)
        head = span - 2 * BLOCK
        for pair in range(2):
            outs = []
            for h in (2 * pair, 2 * pair + 1):
                cols = slice(HD * h, HD * h + HD)
                q = q_ref[j, :, cols] * 0.125
                last = causal_tail(mm_nt(kbuf[head:span, cols], q), core)
                top = jnp.max(last, axis=0, keepdims=True)
                if head:
                    early = mm_nt(kbuf[0:head, cols], q)
                    top = jnp.maximum(top, jnp.max(early, axis=0, keepdims=True))
                    early = jnp.exp(early - top)
                last = jnp.exp(last - top)
                total = jnp.sum(last, axis=0, keepdims=True)
                mixed = mm_tn(vbuf[head:span, cols], last.astype(BF16))
                if head:
                    total = total + jnp.sum(early, axis=0, keepdims=True)
                    mixed = mixed + mm_tn(vbuf[0:head, cols], early.astype(BF16))
                outs.append(mixed / total)
                lse_ref[h, j] = top + jnp.log(total)
            both = jnp.concatenate(outs, axis=0)
            o_ref[j, :, 128 * pair : 128 * pair + 128] = both.T.astype(BF16)
    rows = jnp.concatenate([o_ref[k] for k in range(RING)], axis=0)
    for cols in chunks():
        weight = jnp.concatenate([lane_blocks(w, 384, cols) for w in (Tall(w0, w1), Tall(w2, w3))], axis=0)
        split_rows(mm(rows, weight), (near, f1, f2, f3), cols)


def self_back_kernel(
    place, g0, g1, g2, g3, w0, w1, w2, w3, q_ref, own_ref, other_ref, lse_ref,
    dq_ref, down_ref, dother_ref, kbuf, vbuf, dobuf, dk, dv,
):
    rows = stack_rows((g0, g1, g2, g3))
    weight = jnp.concatenate([lane_blocks(w, 384, ALL_COLS) for w in (Tall(w0, w1), Tall(w2, w3))], axis=0)
    dobuf[...] = mm_nt(rows, weight).astype(BF16).reshape(dobuf.shape)
    lay_out_keys(place, own_ref, other_ref, kbuf, vbuf)
    core = place[1]
    for b in reversed(range(RING)):
        j = block_of(place, b)
        span = 2 * BLOCK * (b + 1)
        head = span - 2 * BLOCK
        for pair in range(2):
            lanes = slice(128 * pair, 128 * pair + 128)
            dqs, dks, dvs = [], [], []
            for h in (2 * pair, 2 * pair + 1):
                cols = slice(HD * h, HD * h + HD)
                q = q_ref[j, :, cols] * 0.125
                do = dobuf[j, :, cols]
                k = kbuf[0:span, cols]
                scores = mm_nt(k, q)
                last = causal_tail(scores[head:span], core)
                scores = jnp.concatenate([scores[0:head], last], axis=0) if head else last
                probs = jnp.exp(scores - lse_ref[h, j])
                dprobs = mm_nt(vbuf[0:span, cols], do)
                delta = jnp.sum(probs * dprobs, axis=0, keepdims=True)
                dscores = (probs * (dprobs - delta)).astype(BF16)
                dqs.append(mm_tn(k, dscores) * 0.125)
                dks.append(mm(dscores, q))
                dvs.append(mm(probs.astype(BF16), do))
            dq_ref[j, :, lanes] = jnp.concatenate(dqs, axis=0).T.astype(BF16)
            dk_new = jnp.concatenate(dks, axis=1)
            dv_new = jnp.concatenate(dvs, axis=1)
            if b == RING - 1:
                dk[0:span, lanes] = dk_new
                dv[0:span, lanes] = dv_new
            else:
                dk[0:span, lanes] += dk_new
                dv[0:span, lanes] += dv_new
    for b in range(RING):
        j = block_of(place, b)
        own_at = pl.ds(pl.multiple_of((2 * b + core) * BLOCK, BLOCK), BLOCK)
        other_at = pl.ds(pl.multiple_of((2 * b + 1 - core) * BLOCK, BLOCK), BLOCK)
        for pair in range(2):
            here = slice(pair * 128, pair * 128 + 128)
            theirs = 1 - pair
            down_ref[j, :, 256 * pair : 256 * pair + 128] = dk[own_at, here]
            down_ref[j, :, 256 * pair + 128 : 256 * pair + 256] = dv[own_at, here]
            dother_ref[j, :, 256 * theirs : 256 * theirs + 128] = dk[other_at, here].astype(BF16)
            dother_ref[j, :, 256 * theirs + 128 : 256 * theirs + 256] = dv[other_at, here].astype(BF16)


def keys_total(down_ref, dother_ref):
    total = [down_ref[k] + dother_ref[k].astype(F32) for k in range(RING)]
    return jnp.concatenate(total, axis=0).astype(BF16)


def self_rows_back_kernel(
    dq_ref, down_ref, dother_ref, own0, own1, far0, far1, near, f1, f2, f3
):
    own, far = Tall(own0, own1), Tall(far0, far1)
    dq = jnp.concatenate([dq_ref[k] for k in range(RING)], axis=0)
    rows = jnp.concatenate([dq, keys_total(down_ref, dother_ref)], axis=1)
    for cols in chunks():
        weight = jnp.concatenate(
            [own[cols, 0:128], far[cols, 0:128], own[cols, 128:384], far[cols, 128:384]], axis=1
        )
        split_rows(mm_nt(rows, weight), (near, f1, f2, f3), cols)


def last_rows_back_kernel(
    dq_ref, down_ref, dother_ref, own0, own1, far0, far1, all_ref, n0, n1, n2, n3, n4,
    near, f1, f2, f3, norms,
):
    own, far = Tall(own0, own1), Tall(far0, far1)
    dq = jnp.concatenate([dq_ref[k] for k in range(RING)], axis=0)
    rows = jnp.concatenate([dq, keys_total(down_ref, dother_ref)], axis=1)
    for n, ref in enumerate((n0, n1, n2, n3, n4), 1):
        norms[2 * n : 2 * n + 2] = ref[...]
    norms[12:16] = jnp.zeros((4, 1024), F32)
    for cols in chunks():
        weight = jnp.concatenate(
            [own[cols, 0:128], far[cols, 0:128], own[cols, 128:384], far[cols, 128:384]], axis=1
        )
        total = mm_nt(rows, weight)
        near[:, cols] = total[0:BLOCK]
        for k, out in enumerate((f1, f2, f3), 1):
            out[0:BLOCK, cols] = total[BLOCK * k : BLOCK * (k + 1)].astype(BF16)
        norms[0:1, cols] = jnp.sum(total * all_ref[:, cols].astype(F32), axis=0, keepdims=True)
        norms[1:2, cols] = jnp.sum(total, axis=0, keepdims=True)
    for out in (f1, f2, f3):
        out[BLOCK : BLOCK + 16] = norms[...].astype(BF16)


def last_sum_back_kernel(dv_ref, near, r1, r2, r3, s_ref, r_ref, rows, norms, g_out, total):
    da = near[...]
    for ref in (r1, r2, r3):
        da = da + ref[0:BLOCK].astype(F32)
    standard = s_ref[...]
    scaled = da * rows[0:1]
    inner = (
        scaled
        - jnp.mean(scaled, axis=-1, keepdims=True)
        - standard * jnp.mean(scaled * standard, axis=-1, keepdims=True)
    )
    g_out[...] = (dv_ref[...].astype(F32) + inner * r_ref[...]).astype(BF16)
    total[...] = norms[...] + sum(ref[BLOCK : BLOCK + 16].astype(F32) for ref in (r1, r2, r3))


def cross_cols(w, layer, place, g, at, rows):
    first = RING * block_of(place, g)
    parts = [
        w[first + y, :, at : at + 128]
        for y in range(rows.start // 256, rows.stop // 256)
    ]
    return parts[0] if len(parts) == 1 else jnp.concatenate(parts, axis=0)


def cross_blocks(w, layer, place, g, cols):
    first = RING * block_of(place, g)
    parts = []
    for c in range(cols.start, cols.stop, 128):
        at = c % 256
        parts.append(w[first + c // 256, at : at + 128, 128:256])
    return jnp.concatenate(parts, axis=1)


def cross_mask(scores, length):
    slots = lax.broadcasted_iota(jnp.int32, scores.shape, 0)
    return jnp.where(slots < length, scores, NEG_FILL)


def cross_forward_kernel(layer, place, lengths, mine, theirs, *refs):
    w, kv, (q_ref, o_ref, lse_ref, near, far) = refs[0], refs[1:5], refs[5:]
    rows = stack_rows((mine, theirs))
    for g in range(RING):
        lanes = slice(128 * g, 128 * g + 128)
        q_ref[:, lanes] = mm(rows, cross_cols(w, layer, place, g, 0, slice(0, 1024))).astype(BF16)
        outs = []
        for p in range(2):
            h = 2 * g + p
            q = q_ref[:, HD * h : HD * h + HD] * 0.125
            k = kv[g][layer, :, HD * p : HD * p + HD]
            v = kv[g][layer, :, 128 + HD * p : 128 + HD * p + HD]
            scores = cross_mask(mm_nt(k, q), lengths[place[4], 0])
            top = jnp.max(scores, axis=0, keepdims=True)
            raised = jnp.exp(scores - top)
            total = jnp.sum(raised, axis=0, keepdims=True)
            outs.append(mm_tn(v, raised.astype(BF16)) / total)
            lse_ref[h] = top + jnp.log(total)
        o_ref[:, lanes] = jnp.concatenate(outs, axis=0).T.astype(BF16)
    for cols in chunks():
        weight = jnp.concatenate([cross_blocks(w, layer, place, g, cols) for g in range(RING)], axis=0)
        split_rows(mm(o_ref[...], weight), (near, far), cols)


def cross_back_kernel(layer, place, lengths, mine, theirs, *refs):
    w, kv, (q_ref, lse_ref) = refs[0], refs[1:5], refs[5:7]
    dq_ref, dkv, (near, far) = refs[7], refs[8:12], refs[12:14]
    rows = stack_rows((mine, theirs))
    for g in range(RING):
        lanes = slice(128 * g, 128 * g + 128)
        dmixed = mm_nt(rows, cross_blocks(w, layer, place, g, ALL_COLS)).astype(BF16)
        dqs, dks, dvs = [], [], []
        for p in range(2):
            h = 2 * g + p
            q = q_ref[:, HD * h : HD * h + HD] * 0.125
            do = dmixed[:, HD * p : HD * p + HD]
            k = kv[g][layer, :, HD * p : HD * p + HD]
            v = kv[g][layer, :, 128 + HD * p : 128 + HD * p + HD]
            probs = jnp.exp(cross_mask(mm_nt(k, q), lengths[place[4], 0]) - lse_ref[h])
            dprobs = mm_nt(v, do)
            delta = jnp.sum(probs * dprobs, axis=0, keepdims=True)
            dscores = (probs * (dprobs - delta)).astype(BF16)
            dqs.append(mm_tn(k, dscores) * 0.125)
            dks.append(mm(dscores, q))
            dvs.append(mm(probs.astype(BF16), do))
        dq_ref[:, lanes] = jnp.concatenate(dqs, axis=0).T.astype(BF16)
        dkv[g][...] = jnp.concatenate(dks + dvs, axis=1).astype(BF16)
    for cols in chunks():
        weight = jnp.concatenate([cross_cols(w, layer, place, g, 0, cols) for g in range(RING)], axis=1)
        split_rows(mm_nt(dq_ref[...], weight), (near, far), cols)


def up_cols(own, far, at):
    refs, at = (own, at) if at < 512 else (far, at - 512)
    return jnp.concatenate([ref[:, at : at + CHUNK] for ref in refs], axis=0)


def up_rows(own, far, cols):
    half, rows = cols.start // 512, slice(cols.start % 512, cols.start % 512 + CHUNK)
    return jnp.concatenate([own[half][rows, 0:512], far[half][rows, 0:512]], axis=1)


def down_rows(own, far, at):
    refs, at = (own, at) if at < 512 else (far, at - 512)
    return jnp.concatenate([ref[at : at + CHUNK, 512:1024] for ref in refs], axis=1)


def down_cols(own, far, at):
    half, lanes = at // 512, slice(512 + at % 512, 512 + at % 512 + CHUNK)
    return jnp.concatenate([own[half][:, lanes], far[half][:, lanes]], axis=0)


def ffn_forward_kernel(
    a0, a1, a2, a3, own0, own1, far0, far1, hidden_ref, slope_ref, near, f1, f2, f3
):
    own, far = (own0, own1), (far0, far1)
    root = 0.7978845608028654
    rows = stack_rows((a0, a1, a2, a3))
    for cols in chunks():
        pre = mm(rows, up_cols(own, far, cols.start))
        square = pre * pre
        t = jnp.tanh(root * (pre + 0.044715 * pre * square))
        half = 0.5 * (1.0 + t)
        hidden_ref[:, cols] = (pre * half).astype(BF16)
        slope_ref[:, cols] = half + 0.5 * pre * (1.0 - t * t) * (root * (1.0 + 3 * 0.044715 * square))
    for cols in chunks():
        split_rows(mm(hidden_ref[...], down_cols(own, far, cols.start)), (near, f1, f2, f3), cols)


def ffn_back_kernel(
    g0, g1, g2, g3, own0, own1, far0, far1, slope_ref, dpre_ref, near, f1, f2, f3
):
    own, far = (own0, own1), (far0, far1)
    rows = stack_rows((g0, g1, g2, g3))
    for cols in chunks():
        dhidden = mm_nt(rows, down_rows(own, far, cols.start))
        dpre_ref[:, cols] = (dhidden * slope_ref[:, cols]).astype(BF16)
    for cols in chunks():
        split_rows(mm_nt(dpre_ref[...], up_rows(own, far, cols)), (near, f1, f2, f3), cols)


def ffn_grads_kernel(hidden, g0, g1, g2, g3, dpre, a0, a1, a2, a3, ours, t0, t1, t2, t3):
    theirs = (t0, t1, t2, t3)
    g = stack_rows((g0, g1, g2, g3))
    a = stack_rows((a0, a1, a2, a3))
    for n in (2, 3, 0, 1):
        down = mm_tn(hidden[:, CHUNK * n : CHUNK * n + CHUNK], g)
        if n >= 2:
            theirs[n - 2][...] = down.astype(BF16)
        else:
            ours[CHUNK * n : CHUNK * n + CHUNK] = down
    for half in (1, 0):
        for n in range(4):
            up = mm_tn(a[:, CHUNK * n : CHUNK * n + CHUNK], dpre[:, 512 * half : 512 * half + 512])
            lanes = slice(512 * (n // 2), 512 * (n // 2) + 512)
            if half:
                theirs[2 + n % 2][:, lanes] = up.astype(BF16)
            else:
                ours[512 + CHUNK * (n % 2) : 512 + CHUNK * (n % 2) + CHUNK, lanes] = up


def ffn_total(ours, came, rows):
    n, at = rows.start // CHUNK, rows.start % CHUNK
    return ours[rows] + came[n][at : at + rows.stop - rows.start].astype(F32)


def cross_shares(k, g, a, mixed, dq, keys, memory):
    lanes = slice(128 * k, 128 * k + 128)
    return mm_tn(dq[:, lanes], a), mm_tn(mixed[:, lanes], g), mm_tn(keys[...], memory)


def cross_chunk_kernel(place, mixed, g_mine, g_theirs, dq, a_mine, a_theirs, c0, c1, c2, c3, total):
    g = stack_rows((g_mine, g_theirs))
    a = stack_rows((a_mine, a_theirs))
    for k in range(RING):
        lanes = slice(128 * k, 128 * k + 128)
        parts = (mm_tn(dq[:, lanes], a), mm_tn(mixed[:, lanes], g))
        for i in range(8):
            at = 32 * (i % 4)
            total[128 * i + 32 * k : 128 * i + 32 * k + 32] = parts[i // 4][at : at + 32]
    cut_chunks(place, total, (c0, c1, c2, c3))


def cross_sum_kernel(c0, r1, r2, r3, k0, k1, k2, k3, *outs):
    sums = [c0[z] + sum(r[z].astype(F32) for r in (r1, r2, r3)) for z in range(2)]
    for k, (key, out) in enumerate(zip((k0, k1, k2, k3), outs)):
        for z in range(2):
            out[32 * z : 32 * z + 32] = sums[z][32 * k : 32 * k + 32].astype(out.dtype)
        for i in range(4):
            out[64:128, 256 * i : 256 * i + 256] = key[64 * i : 64 * i + 64].astype(out.dtype)


def cross_first_kernel(
    place, ours, q0, q1, q2, q3, mixed, g_mine, g_theirs, dq, a_mine, a_theirs, k0, k1, k2, k3,
    memory, out,
):
    g = stack_rows((g_mine, g_theirs))
    a = stack_rows((a_mine, a_theirs))
    for i in range(8):
        rows = slice(128 * i, 128 * i + 128)
        out[i, 0:128] = ffn_total(ours, (q0, q1, q2, q3), rows).astype(BF16)
    for k, key in enumerate((k0, k1, k2, k3)):
        queries, outs, keys = cross_shares(k, g, a, mixed, dq, key, memory[...])
        for i in range(8):
            part, at = (queries, outs)[i // 4], 32 * (i % 4)
            to = pl.multiple_of(128 + 64 * block_of(place, k), 64)
            out[i, pl.ds(to, 32)] = part[at : at + 32].astype(BF16)
            out[i, pl.ds(pl.multiple_of(to + 32, 32), 32)] = keys[32 * i : 32 * i + 32].astype(BF16)


def self_grads_kernel(
    mixed, g0, g1, g2, g3, dq, down_ref, dother_ref, a0, a1, a2, a3, ours, t0, t1
):
    g = stack_rows((g0, g1, g2, g3))
    a = stack_rows((a0, a1, a2, a3))
    keys = keys_total(down_ref, dother_ref)
    outs, queries = [jnp.concatenate([r[k] for k in range(RING)], axis=0) for r in (mixed, dq)]
    t0[0:128] = mm_tn(outs[:, 128:256], g).astype(BF16)
    t0[128:256] = mm_tn(queries[:, 128:256], a).astype(BF16)
    t1[...] = mm_tn(keys[:, 256:512], a).astype(BF16)
    ours[0:128] = mm_tn(outs[:, 0:128], g)
    ours[128:256] = mm_tn(queries[:, 0:128], a)
    ours[256:512] = mm_tn(keys[:, 0:256], a)


def rows_kernel(place, x_ref, memory_ref, g_ref, x, both, g):
    mine = place[4]
    x[...] = x_ref[mine]
    both[0:BLOCK] = x_ref[mine]
    both[BLOCK : BLOCK + 32] = memory_ref[mine]
    g[...] = g_ref[mine]


def norm_rows_kernel(gain, bias, out):
    out[0:3] = gain[0]
    out[3:6] = bias[0]


def both_norms_kernel(place, mine, other, first, second):
    first[...] = jnp.where(place[4] == 0, mine[...], other[...])
    second[...] = jnp.where(place[4] == 0, other[...], mine[...])


def memory_blocks_kernel(x0, x1, x2, x3, out):
    for k, ref in enumerate((x0, x1, x2, x3)):
        out[32 * k : 32 * k + 32] = ref[BLOCK : BLOCK + 32]


def pack_kernel(place, w_ref, out_ref, q_ref, cross_ref, kv_ref, first, second, part, whole):
    for i in range(3):
        whole[:, 128 * i : 128 * i + 128] = w_ref[i]
    for i in range(8):
        rows = slice(128 * i, 128 * i + 128)
        whole[rows, 384:512] = out_ref[:, rows]
        whole[rows, 640:768] = cross_ref[:, rows]
    whole[:, 512:640] = q_ref[...]
    whole[:, 768:1024] = kv_ref[...]
    first[...] = whole[0:512, 0:512]
    second[...] = whole[512:1024, 0:512]
    part[...] = whole[pl.ds(pl.multiple_of(place[2] * 256, 256), 256)]


def pack_ffn_kernel(up_ref, down_ref, out):
    out[:, 0:512] = up_ref[...]
    out[0:512, 512:1024] = down_ref[:, 0:512]
    out[512:1024, 512:1024] = down_ref[:, 512:1024]


def quarter(place, k):
    return pl.ds(pl.multiple_of(lax.rem(place[2] - k + RING, RING) * 256, 256), 256)


def by_section(place, write):
    pl.when(place[4] == 0)(lambda: write(0, 1))
    pl.when(place[4] == 1)(lambda: write(1, 0))


def fill_halves(place, parts, halves, cols):
    for k, ref in enumerate(parts):
        y = lax.rem(place[2] - k + RING, RING)
        rows = pl.ds(pl.multiple_of(lax.rem(y, 2) * 256, 256), 256)

        def put(half, ref=ref, rows=rows):
            halves[half][rows] = ref[:, cols]

        pl.when(y < 2)(functools.partial(put, 0))
        pl.when(y >= 2)(functools.partial(put, 1))


def both_selfs_kernel(
    place, mine0, mine1, r0, r1, r2, r3, a0, a1, b0, b1
):
    def write(own, far):
        halves = ((a0, a1), (b0, b1))
        halves[own][0][...] = mine0[...]
        halves[own][1][...] = mine1[...]
        fill_halves(place, (r0, r1, r2, r3), halves[far], slice(0, 512))

    by_section(place, write)


def rest_kernel(place, mine, other, out, part0, part1):
    def write(own, far):
        (part0, part1)[own][0] = mine[:, 512:768]
        (part0, part1)[far][0] = other[:, 512:768]

    by_section(place, write)
    out[:, 0:512] = other[:, 0:512]
    out[:, 512:768] = other[:, 768:1024]


def keys_kernel(place, kv_ref, k0, k1, k2, k3, x0, x1, x2, x3, e_far, out, memory, pair):
    for k, ref in enumerate((x0, x1, x2, x3)):
        at = 64 * block_of(place, k)
        memory[pl.ds(pl.multiple_of(at + 32 * place[1], 32), 32)] = ref[BLOCK : BLOCK + 32]
        memory[pl.ds(pl.multiple_of(at + 32 - 32 * place[1], 32), 32)] = e_far[32 * k : 32 * k + 32]
    for k, ref in enumerate((k0, k1, k2, k3)):
        pair[quarter(place, k)] = ref[:, 512:768]
    mine = mm(memory[...], kv_ref[...]).astype(BF16)
    other = mm(memory[...], pair[...]).astype(BF16)

    def write(own, far):
        out[own] = mine
        out[far] = other

    by_section(place, write)


def both_ffns_kernel(place, mine, other, a0, a1, b0, b1):
    def write(own, far):
        halves = ((a0, a1), (b0, b1))
        for half in range(2):
            rows = slice(512 * half, 512 * half + 512)
            halves[own][half][...] = mine[rows]
            halves[far][half][...] = other[rows]

    by_section(place, write)


def cut_chunks(place, total, outs):
    rows = total.shape[0] // 8
    for k, out in enumerate(outs):
        y = lax.rem(place[2] - k + RING, RING)
        for z in range(2):
            at = pl.ds(pl.multiple_of((RING * z + y) * rows, rows), rows)
            out[z] = total[at].astype(out.dtype)


def join_kernel(f, q0, q1, q2, q3, ours, t0, t1, out):
    for i in range(8):
        out[i, 0:128] = ffn_total(f, (q0, q1, q2, q3), slice(128 * i, 128 * i + 128)).astype(BF16)
        theirs = (t0, t1)[i // 4]
        at = 64 * (i % 4)
        out[i, 128:192] = (ours[64 * i : 64 * i + 64] + theirs[at : at + 64].astype(F32)).astype(BF16)


def rest_chunk_kernel(
    place, ours, t0, t1, w0, w1, w2, w3, memory, c0, c1, c2, c3, cross, total
):
    came = w0[...] + sum(w[...].astype(F32) for w in (w1, w2, w3))
    for z in range(2):
        cross[z] = came[32 * z : 32 * z + 32]
    keys = jnp.concatenate([came[64:128, 256 * i : 256 * i + 256] for i in range(4)], axis=0)
    keys = mm_tn(keys.astype(BF16), memory[...])
    for i in range(8):
        theirs = (t0, t1)[i // 4]
        at, to = 64 * (i % 4), 96 * i
        total[to : to + 64] = ours[64 * i : 64 * i + 64] + theirs[at : at + 64].astype(F32)
        total[to + 64 : to + 96] = keys[32 * i : 32 * i + 32]
    cut_chunks(place, total, (c0, c1, c2, c3))


def split_kernel(grads, ffn, cross):
    ffn[...] = grads[0:128]
    cross[...] = grads[128:384]


def chunk_shapes(rows):
    return [Cold(struct((2, rows, 1024), F32))] + [struct((2, rows, 1024), BF16)] * 3


def sum_y_kernel(place, c0, r1, r2, r3, mid, first, ffn, cross, keep, over_z, over_s):
    z = place[3]

    def half(n):
        rest = c0[n] + sum(r[n].astype(F32) for r in (r1, r2, r3))
        return jnp.concatenate([rest[0:64], mid[n], rest[64:96]], axis=0)

    over_z[...] = half(1 - z).astype(BF16)
    rest = half(z)

    def write_first():
        keep[0:128] = rest
        keep[128:256] = first[0:128].astype(F32)
        over_s[0:64] = first[128:192]
        over_s[64:128] = cross[...]
        over_s[128:256] = ffn[...]

    def write_second():
        keep[0:64] = first[128:192].astype(F32)
        keep[64:128] = cross[...].astype(F32)
        keep[128:256] = ffn[...].astype(F32)
        over_s[0:128] = rest.astype(BF16)
        over_s[128:256] = first[0:128]

    pl.when(place[4] == 0)(write_first)
    pl.when(place[4] == 1)(write_second)


def sum_rest_kernel(place, keep, from_z, from_s, from_both, norms, came, out):
    rest = keep[0:128] + from_s[0:128].astype(F32)
    other = from_z[...].astype(F32) + from_both[...].astype(F32)
    out[0:128] = jnp.where(place[4] == 0, rest + other, rest).astype(BF16)
    out[128:144] = (norms[...] + came[...]).astype(BF16)
    out[144:272] = (keep[128:256] + from_s[128:256].astype(F32)).astype(BF16)


def exchange(over_z, over_s):
    from_both = lax.ppermute(over_z, ("section", "dz"), [(2, 1), (3, 0)])
    return swap(over_z, "dz"), swap(over_s, "section"), from_both


def norms_kernel(place, all_ref, keep, over_s):
    total = sum(all_ref[272 * i + 128 : 272 * i + 144].astype(F32) for i in range(8))
    first, second = total[0:6], total[6:12]
    keep[0:6] = jnp.where(place[4] == 0, first, second)
    over_s[0:6] = jnp.where(place[4] == 0, second, first)
    keep[6:8] = jnp.zeros((2, 1024), F32)
    over_s[6:8] = jnp.zeros((2, 1024), F32)


def last_norms_kernel(mine, came, gains, biases, ffn):
    norms = mine[...] + came[...]
    for j in range(2):
        gains[j : j + 1] = norms[2 * j : 2 * j + 1]
        biases[j : j + 1] = norms[2 * j + 1 : 2 * j + 2]
    ffn[...] = norms[4:6]


def last_kernel(
    all_ref, out_ref, self_ref, q_ref, cross_ref, kv_ref, up_ref, down_ref
):
    def rows(at, count, span):
        return jnp.concatenate(
            [all_ref[272 * i + at : 272 * i + at + span] for i in range(count, count + 128 // span)],
            axis=0,
        ).astype(F32)

    out_ref[...] = rows(0, 0, 64)
    for i in range(3):
        self_ref[i] = rows(0, 2 + 2 * i, 64).T
    q_ref[...] = rows(64, 0, 32).T
    cross_ref[...] = rows(64, 4, 32)
    kv_ref[pl.ds(0, 1024, stride=2)] = rows(96, 0, 32).T
    kv_ref[pl.ds(1, 1024, stride=2)] = rows(96, 4, 32).T
    for i in range(4):
        here = slice(128 * i, 128 * i + 128)
        down_ref[here] = rows(144, i, 128)
        up = rows(144, 4 + i, 128)
        up_ref[here] = up[:, 0:512]
        up_ref[512 + 128 * i : 640 + 128 * i] = up[:, 512:1024]


def other_layer_kernel(place, text, unit, input_grad, text_grad, out):
    def write(rows, grads):
        out[0:BLOCK] = rows[...]
        out[BLOCK : 2 * BLOCK] = grads[...]

    pl.when(place[4] == 0)(lambda: write(unit, text_grad))
    pl.when(place[4] == 1)(lambda: write(text, input_grad))


def both_batches_kernel(place, text, unit, input_grad, text_grad, came, states, grads):
    mine = place[4]

    def write(rows, own):
        states[mine] = rows[...]
        grads[mine] = own[...]

    pl.when(mine == 0)(lambda: write(text, input_grad))
    pl.when(mine == 1)(lambda: write(unit, text_grad))
    states[1 - mine] = came[0:BLOCK]
    grads[1 - mine] = came[BLOCK : 2 * BLOCK]


def layer_forward(layer, v, first, weights, ffns, place, lengths, rows, after):
    own, far, cross, kv = weights
    heads = [struct((RING, BLOCK, 256), BF16), struct((RING, BLOCK, 512), BF16)]
    if layer == 0:
        q, kv_self, *rest = call(
            first_qkv_kernel,
            heads + cold(*[ROW16] * RING, ROW, COLUMN, struct((RING * BLOCK, 1024), BF16)),
            [*cold(*first, *own, *far), rows],
            after=after.get("qkv", ()),
        )
        full1, (s1, r1, all1) = rest[0:4], rest[4:7]
    else:
        a1, s1, r1, all1 = *first, None
        full1 = gather_x(a1)
        q, kv_self = call(qkv_kernel, heads, [*full1, *cold(*own, *far)], after=after.get("qkv", ()))
    kv_other = swap(kv_self, "core")
    if "keys" in after:
        after["keys"](q)
    mixed1, lse1, *sent = call(
        self_forward_kernel,
        cold_if(not layer, struct((RING, BLOCK, 256), BF16), struct((4, RING, 1, BLOCK), F32)) + SENT,
        [q, kv_self, kv_other, *cold(*own, *far)],
        scalars=[place],
        scratch=[pltpu.VMEM((KEYS, 256), BF16), pltpu.VMEM((KEYS, 256), BF16)],
        after=after.get("self", ()),
    )
    waits = after["sum1"](mixed1) if "sum1" in after else ()
    v1, a2, s2, r2 = sum_norm(1, v, sent[0], send_x(sent[1:]), rows, ROW, after=waits, new=not layer)
    a2_theirs = swap(a2, "core")
    cq, mixed2, lse2, near, far2 = call(
        functools.partial(cross_forward_kernel, layer),
        [
            struct((2 * BLOCK, 512), BF16),
            struct((2 * BLOCK, 512), BF16),
            struct((2 * RING, 1, 2 * BLOCK), F32),
            ROW,
            ROW16,
        ],
        [a2, a2_theirs, *cold(cross, *kv[0:4])],
        scalars=[place, lengths],
        after=after.get("cross", ()),
    )
    v2, a3, s3, r3 = sum_norm(
        2, v1, near, [swap(far2, "core")], rows, ROW, after=after.get("sum2", ()), old=not layer
    )
    full3 = gather_x(a3)
    hidden, slope, *sent = call(
        ffn_forward_kernel,
        [struct((RING * BLOCK, 1024), BF16), struct((RING * BLOCK, 1024), F32)] + SENT,
        [*full3, *cold(*ffns[layer])],
        after=after.get("ffn", ()),
    )
    stored = (
        (s1, r1, full1, q, kv_self, kv_other, mixed1, lse1, all1),
        (s2, r2, a2, a2_theirs, cq, mixed2, lse2),
        (s3, r3, full3, hidden, slope),
    )
    return v2, sent[0], send_x(sent[1:]), stored


def layer_back(layer, dv, full_g3, stored, weights, ffns, place, lengths, rows, steps):
    own, far, cross, kv = weights
    (s1, r1, full1, q, kv_self, kv_other, mixed1, lse1, all1), second, third = stored
    s2, r2, a2, a2_theirs, cq, mixed2, lse2 = second
    s3, r3, full3, hidden, slope = third
    old = layer == 0
    dpre, *sent = call(
        ffn_back_kernel,
        [struct((RING * BLOCK, 1024), BF16)] + SENT,
        [*full_g3, *cold(*ffns[layer]), *cold_if(old, slope)],
        after=steps.get("ffn", ()),
    )
    ffn_ours, *ffn_theirs = call(
        ffn_grads_kernel,
        [struct((1024, 1024), F32)] + [struct((CHUNK, 1024), BF16)] * 4,
        [*cold_if(old, hidden), *full_g3, dpre, *cold_if(old, *full3)],
    )
    ffn_parts = [ffn_ours, *(swap(part, "core") for part in ffn_theirs)]
    dv2, g2, norms3 = sum_back(
        2, dv, sent[0], send_x(sent[1:]), s3, r3, rows,
        after=[ffn_theirs[0], *steps.get("sum3", ())], old=old, new=old,
    )
    g2_theirs = swap(g2, "core")
    pair_keys = struct((2 * BLOCK, 256), BF16)
    dcq, *rest = call(
        functools.partial(cross_back_kernel, layer),
        [struct((2 * BLOCK, 512), BF16)] + [pair_keys] * RING + [ROW, ROW16],
        [g2, g2_theirs, *cold(cross, *kv[0:4]), *cold_if(old, cq, lse2)],
        scalars=[place, lengths],
        after=steps.get("cross", lambda parts, g2: ())(ffn_parts, g2),
    )
    dkv_cross, (near, far2) = rest[:RING], rest[RING:]
    dv1, g1, norms2 = sum_back(1, dv2, near, [swap(far2, "core")], s2, r2, rows, old=old, new=True)
    full_g1 = gather_x(g1)
    cross_grads = [*cold_if(old, mixed2), g2, g2_theirs, dcq, *cold_if(old, a2, a2_theirs)]
    middle, waits = steps["middle"](ffn_parts, cross_grads, dkv_cross, g1)
    dq, dkv_own, dkv_theirs = call(
        self_back_kernel,
        [
            struct((RING, BLOCK, 256), BF16),
            struct((RING, BLOCK, 512), F32),
            struct((RING, BLOCK, 512), BF16),
        ],
        [*full_g1, *cold(*own, *far, q, kv_self, kv_other, lse1)],
        scalars=[place],
        scratch=[
            pltpu.VMEM((KEYS, 256), BF16),
            pltpu.VMEM((KEYS, 256), BF16),
            pltpu.VMEM((RING, BLOCK, 256), BF16),
            pltpu.VMEM((KEYS, 256), F32),
            pltpu.VMEM((KEYS, 256), F32),
        ],
        after=waits,
    )
    back = [dq, dkv_own, swap(dkv_theirs, "core")]

    def self_grads(waits=()):
        ours, *theirs = call(
            self_grads_kernel,
            [struct((512, 1024), F32)] + [struct((2 * BLOCK, 1024), BF16)] * 2,
            [*cold(mixed1), *full_g1, *back, *cold(*full1)],
            after=waits,
        )
        return [ours, *(swap(part, "core") for part in theirs)], theirs

    if layer == 0:
        share, *others = call(cross_sum_kernel, [ROW, ROW16, ROW16, ROW16], middle)
        self_parts, theirs = self_grads([share])
        waits = steps["late"]([share, *send_x(others)], self_parts, theirs)
        tall = struct((BLOCK + 16, 1024), BF16)
        near, *others, sums = call(
            last_rows_back_kernel,
            [ROW, tall, tall, tall, struct((16, 1024), F32)],
            [*back, *cold(*own, *far, all1, norms2, norms3, *steps["norms"])],
            after=waits,
        )
        steps["tail"]["near"] = near
        g0, sums = call(
            last_sum_back_kernel,
            [ROW16, struct((16, 1024), F32)],
            [*cold(dv1), near, *send_x(others), *cold(s1, r1, rows, sums)],
        )
        return g0, middle, self_parts, sums
    else:
        sent = call(self_rows_back_kernel, SENT, [*back, *cold(*own, *far)])
        self_parts, theirs = self_grads()
        waits = [theirs[0], *steps["late"]()]
    dv0, g0, norms1 = sum_back(
        0, dv1, sent[0], send_x(sent[1:]), s1, r1, rows, after=waits, old=True
    )
    return g0, middle, self_parts, (norms1, norms2, norms3)


def reduce_dp(grads):
    total = lax.psum_scatter(grads, ("dz", "dy"), scatter_dimension=0, tiled=True)
    return total.reshape(grads.shape[1:])


def shards(
    inputs,
    memory_states,
    source_lengths,
    cotangent,
    norm_gain,
    norm_bias,
    w_self,
    w_self_out,
    w_cross_q,
    w_cross_kv,
    w_cross_out,
    up_weight,
    down_weight,
):
    place = PLACE

    def along_y(part):
        return [part] + [shift(part, "dy", k) for k in range(1, RING)]

    row16 = struct((BLOCK, 1024), BF16)
    kv_mine = w_cross_kv[0].reshape(w_cross_kv.shape[1], -1)
    half = struct((512, 512), BF16)
    *self_mine, mine = call(
        pack_kernel,
        [*cold(half, half), struct((256, 1024), BF16)],
        cold(w_self[0].transpose(1, 0, 2), w_self_out[0], w_cross_q[0], w_cross_out[0], kv_mine),
        scalars=[place],
        scratch=[pltpu.VMEM((1024, 1024), BF16)],
    )
    other = swap(mine, "section")
    x, rows_first, g_top = call(
        rows_kernel,
        cold(row16, struct((BLOCK + 32, 1024), BF16), row16),
        cold(inputs[:, :, 0], memory_states[:, :, 0], cotangent[:, :, 0]),
        scalars=[place],
        after=[mine],
    )
    norms = call(
        norm_rows_kernel, [struct((6, 1024), F32)], [norm_gain, norm_bias], after=[mine]
    )[0]
    norms_other = swap(norms, "section")
    rows_first = gather_x(rows_first)
    ffn_half = struct((512, 1024), BF16)
    ffn_mine, ffn_done = call(
        pack_ffn_kernel,
        cold(struct((1024, 1024), BF16)),
        cold(up_weight[0], down_weight[0]),
        after=[other, *rows_first[1:]],
        token=True,
    )
    ffn_other = swap(ffn_mine, "section")
    norms = call(
        both_norms_kernel, [struct((6, 1024), F32)] * 2, [norms, norms_other], scalars=[place]
    )

    rest, *parts = call(
        rest_kernel,
        [struct((256, 768), BF16), *cold(*[struct((1, 256, 256), BF16)] * 2)],
        [mine, other],
        scalars=[place],
        after=[norms_other, *rows_first[1:]], lazy=False)
    rests = along_y(rest)
    e_far = swap(call(memory_blocks_kernel, [row16], rows_first)[0], "core")
    a0, a1, b0, b1 = call(
        both_selfs_kernel,
        [half, half, *cold(half, half)],
        [*cold(*self_mine), *rests],
        scalars=[place],
        after=[e_far, norms[0], ffn_done], lazy=False)
    selfs = [(a0, a1), (b0, b1)]
    selfs_far = [tuple(swap(w, "core") for w in pair) for pair in selfs]
    crosses = [lax.all_gather(part, ("tx", "dy"), axis=0, tiled=True) for part in parts]
    ffns, kvs = [], []

    def make_keys(q):
        keyed, memory = call(
            keys_kernel,
            cold(struct((2, 256, 256), BF16), struct((256, 1024), BF16)),
            cold(kv_mine, *rests, *rows_first, e_far),
            scalars=[place],
            scratch=[pltpu.VMEM((1024, 256), BF16)],
            after=[q],
        )
        kvs.extend(gather_x(keyed))
        kvs.append(memory)


    def made(mixed):
        a0, a1, b0, b1, done = call(
            both_ffns_kernel,
            cold(*[ffn_half] * 4),
            cold(ffn_mine, ffn_other),
            scalars=[place],
            after=[mixed],
            token=True, lazy=False)
        for first, second in ((a0, a1), (b0, b1)):
            ffns.append((first, second, swap(first, "core"), swap(second, "core")))
        return [done]

    weights = [(selfs[i], selfs_far[i], crosses[i], kvs) for i in range(2)]

    v, near, far, stored0 = layer_forward(
        0, x, rows_first, weights[0], ffns, place, source_lengths, norms[0], {"keys": make_keys, "sum1": lambda mixed: [*kvs[1:4], *made(mixed)]}
    )
    text, *normed = sum_norm(0, v, near, far, norms[1], ROW16, after=[crosses[1]])
    v, near, far, stored1 = layer_forward(
        1, text, normed, weights[1], ffns, place, source_lengths, norms[1], {}
    )
    memory = kvs[4]
    full_top = gather_x(g_top)
    unit = call(sum_last_kernel, cold(ROW16), [*cold(v), near, *far])[0]

    def middle_second(ffn_parts, cross_grads, keys, after):
        out, done = call(
            cross_first_kernel,
            cold(struct((8, 384, 1024), BF16)),
            [*ffn_parts, *cross_grads, *keys, *cold(memory)],
            scalars=[place],
            after=[after],
            token=True,
        )
        return out, [done]

    text_grad, grads_a, self1, norms1 = layer_back(
        1, g_top, full_top, stored1, weights[1], ffns, place, source_lengths, norms[1],
        {
            "ffn": full_top[1:],
            "sum3": [unit],
            "middle": middle_second,
            "late": lambda: (),
        },
    )
    grads_a = reduce_dp(grads_a)

    tail = {}

    def join(ffn_parts, g2):
        tail["joined"], done = call(
            join_kernel,
            cold(struct((8, 192, 1024), BF16)),
            [*ffn_parts, *self1],
            after=[g2],
            token=True,
        )
        return [done]

    def middle_first(ffn_parts, cross_grads, keys, after):
        chunks_of = call(
            cross_chunk_kernel,
            chunk_shapes(128),
            cross_grads,
            scalars=[place],
            scratch=[pltpu.VMEM((1024, 1024), F32)],
            after=[after],
        )
        arrived = [shift(c, "dy", -k) for k, c in enumerate(chunks_of[1:], 1)]
        return [*cold(chunks_of[0]), *arrived, *keys], [chunks_of[1]]

    def late_first(cross_parts, self_parts, theirs):
        *tail["chunks"], tail["cross"] = call(
            rest_chunk_kernel,
            chunk_shapes(96) + cold(struct((2, 32, 1024), F32)),
            [*self_parts, *cross_parts, *cold(memory)],
            scalars=[place],
            scratch=[pltpu.VMEM((768, 1024), F32)],
        )
        return [tail["chunks"][1]]

    input_grad, _, _, norms = layer_back(
        0, text_grad, gather_x(text_grad), stored0, weights[0], ffns, place, source_lengths, norms[0],
        {
            "cross": join,
            "middle": middle_first,
            "late": late_first,
            "norms": norms1,
            "tail": tail,
        },
    )
    grads_b = reduce_dp(tail["joined"])
    ffn1, cross1 = call(
        split_kernel,
        cold(row16, struct((256, 1024), BF16)),
        cold(grads_a),
        after=[tail["near"]],
    )
    cross1 = lax.psum_scatter(cross1, "tx", scatter_dimension=0, tiled=True)
    chunks_of = tail["chunks"]
    arrived = [shift(c, "dy", -k) for k, c in enumerate(chunks_of[1:], 1)]
    two = struct((256, 1024), F32)
    keep, over_z, over_s = call(
        sum_y_kernel,
        [Cold(two), row16, struct((256, 1024), BF16)],
        [*cold(chunks_of[0]), *arrived, *cold(tail["cross"], grads_b, ffn1, cross1)],
        scalars=[place],
        after=[tail["near"]], lazy=False)
    last = call(
        sum_rest_kernel,
        cold(struct((272, 1024), BF16)),
        [*cold(keep), *exchange(over_z, over_s), norms, swap(norms, "core")],
        scalars=[place],
    )[0]
    whole = lax.all_gather(last, ("dz", "dy"), axis=0, tiled=True)
    rows = cold(text, unit, input_grad, text_grad)
    lacks = call(
        other_layer_kernel, [struct((256, 1024), BF16)], rows, scalars=[place], after=[last], lazy=False)[0]
    lacks = swap(lacks, "section")
    eight, pair32 = struct((8, 1024), F32), struct((2, 1024), F32)
    own, over_s = call(
        norms_kernel, [eight] * 2, cold(whole), scalars=[place]
    )
    grad_out, grad_self, grad_cq, grad_co, grad_ckv, grad_up, grad_down, done = call(
        last_kernel,
        cold(
            struct((128, 1024), F32),
            struct((3, 1024, 128), F32),
            struct((1024, 128), F32),
            struct((128, 1024), F32),
            struct((2048, 128), F32),
            struct((1024, 512), F32),
            struct((512, 1024), F32),
        ),
        cold(whole),
        after=[own],
        token=True,
    )
    both = struct((2, BLOCK, 1024), BF16)
    states, input_grads = call(
        both_batches_kernel, cold(both, both), [*rows, lacks], scalars=[place], after=[done], lazy=False)
    grad_gain, grad_bias, grad_ffn = call(
        last_norms_kernel, [pair32] * 3, [own, swap(over_s, "section")], after=[done]
    )
    return (
        states[None, :, :, None],
        input_grads[None, :, :, None],
        grad_gain[None],
        grad_bias[None],
        grad_ffn[None],
        grad_self.transpose(1, 0, 2)[None],
        grad_out[None],
        grad_cq[None],
        grad_ckv.reshape(1, 1024, 2, 128),
        grad_co[None],
        grad_up[None],
        grad_down[None],
    )


def solution(mesh):
    sections = mesh.devices.shape[0]
    fine = Mesh(
        mesh.devices.reshape(sections, 2, RING, RING, 2), ("section", "dz", "dy", "tx", "core")
    )
    dp, tensor = ("dz", "dy"), ("tx", "core")
    rows = P(None, tensor, dp, None)
    return jax.shard_map(
        shards,
        mesh=fine,
        in_specs=(
            rows,
            rows,
            P(None, dp),
            rows,
            P("section", None, None),
            P("section", None, None),
            P("section", None, None, tensor),
            P("section", tensor, None),
            P("section", None, tensor),
            P("section", None, None, tensor),
            P("section", tensor, None),
            P("section", None, tensor),
            P("section", tensor, None),
        ),
        out_specs=(
            P("section", None, tensor, dp, None),
            P("section", None, tensor, dp, None),
            P("section", None, None),
            P("section", None, None),
            P("section", None, None),
            P("section", None, None, tensor),
            P("section", tensor, None),
            P("section", None, tensor),
            P("section", None, None, tensor),
            P("section", tensor, None),
            P("section", None, tensor),
            P("section", tensor, None),
        ),
        check_vma=False,
    )
```

```python
import functools
import math

import jax
import jax.numpy as jnp
from jax import lax
from jax.experimental import pallas as pl
from jax.experimental.pallas import tpu as pltpu
from jax.sharding import Mesh, PartitionSpec as P

HD = 64
EPSILON = 1e-05
NEG_FILL = -1000000000.0
BLOCK = 128
RING = 4
BF16 = jnp.bfloat16
F32 = jnp.float32


def shift(value, axis, steps):
    count = lax.axis_size(axis)
    return lax.ppermute(value, axis, [(i, (i + steps) % count) for i in range(count)])


def swap(value, axis):
    return shift(value, axis, 1)


def dot(a, b, dims):
    return lax.dot_general(a, b, ((dims[0], dims[1]), ((), ())), preferred_element_type=F32)


def mm(a, b):
    return dot(a, b, ((1,), (0,)))


def mm_nt(a, b):
    return dot(a, b, ((1,), (1,)))


def mm_tn(a, b):
    return dot(a, b, ((0,), (0,)))


def gather_x(value):
    return [value] + [shift(value, "tx", k) for k in range(1, RING)]


def send_x(others):
    return [shift(block, "tx", -k) for k, block in enumerate(others, 1)]


SMEM = pl.BlockSpec(memory_space=pltpu.SMEM)
VMEM = pl.BlockSpec(memory_space=pltpu.VMEM)
ANY = pl.BlockSpec(memory_space=pl.ANY)
HBM = pl.BlockSpec(memory_space=pltpu.HBM)
CHUNK = 256


def struct(shape, dtype):
    return jax.ShapeDtypeStruct(shape, dtype)


class Cold:
    def __init__(self, array):
        self.array = array


class Awaited:
    def __init__(self, buffer, move):
        self.buffer, self.move = buffer, move
        self.shape, self.dtype = buffer.shape, buffer.dtype

    def arrived(self):
        if self.move is not None:
            self.move.wait()
            self.move = None
        return self.buffer

    def __getitem__(self, key):
        return self.arrived()[key]


def cold(*arrays):
    return [Cold(array) for array in arrays]


def cold_if(flag, *arrays):
    return cold(*arrays) if flag else list(arrays)


def vmem(o):
    return pltpu.VMEM(o.shape, o.dtype)


class Place:
    axes = ("tx", "core", "dy", "dz", "section")

    def __getitem__(self, at):
        return lax.axis_index(self.axes[at])


PLACE = Place()


def settled(array):
    return pltpu.with_memory_space_constraint(array, pltpu.HBM)


def call(kernel, outs, operands, scalars=(), scratch=(), after=(), room=8, token=False, lazy=True):
    ins = [o if isinstance(o, Cold) else None for o in operands]
    arrays = [o.array if isinstance(o, Cold) else o for o in operands]
    puts = [o if isinstance(o, Cold) else None for o in outs]
    shapes = [o.array if isinstance(o, Cold) else o for o in outs]
    if token:
        puts.append(None)
        shapes.append(struct((8, 128), F32))
    placed = any(o is PLACE for o in scalars)
    scalars = [o for o in scalars if o is not PLACE]
    first, waits = len(scalars), len(after)
    last = first + len(arrays)
    brought = [vmem(o.array) for o in ins if o]
    taken = [vmem(o.array) for o in puts if o]
    held = sum(math.prod(o.shape) * o.dtype.itemsize for o in (*scratch, *brought, *taken))
    name = kernel.func.__name__ if isinstance(kernel, functools.partial) else kernel.__name__

    def body(*refs):
        given = list(refs[first:last])
        results = list(refs[last + waits : last + waits + len(shapes)])
        rest = list(refs[last + waits + len(shapes) :])
        semaphores = rest.pop() if brought or taken else None
        buffers = rest[len(scratch) :]
        moves, stores = [], []
        for at, o in enumerate(ins):
            if o:
                buffer = buffers[len(moves)]
                moves.append(
                    pltpu.make_async_copy(given[at], buffer, semaphores.at[len(moves)])
                )
                moves[-1].start()
                given[at] = buffer
        for at, o in enumerate(puts):
            if o:
                n = len(moves) + len(stores)
                stores.append(pltpu.make_async_copy(buffers[n], results[at], semaphores.at[n]))
                results[at] = buffers[n]
        for at, o in enumerate(ins):
            if o and lazy:
                given[at] = Awaited(given[at], moves[sum(1 for p in ins[:at] if p)])
        for move in () if lazy else moves:
            move.wait()
        if token:
            results.pop()[...] = jnp.zeros((8, 128), F32)
        lead = [PLACE] if placed else []
        kernel(*lead, *refs[:first], *given, *results, *rest[: len(scratch)])
        for ref in given:
            if isinstance(ref, Awaited):
                ref.arrived()
        for store in stores:
            store.start()
        for store in stores:
            store.wait()

    kept = [*scratch, *brought, *taken]
    if brought or taken:
        kept.append(pltpu.SemaphoreType.DMA((len(brought) + len(taken),)))
    return pl.pallas_call(
        body,
        name=name,
        out_shape=[pltpu.HBM(o.shape, o.dtype) if c else o for o, c in zip(shapes, puts)],
        in_specs=[SMEM] * first + [HBM if o else VMEM for o in ins] + [ANY] * waits,
        out_specs=[HBM if o else VMEM for o in puts],
        scratch_shapes=kept,
        compiler_params=pltpu.CompilerParams(vmem_limit_bytes=held + room * 1024 * 1024),
    )(*scalars, *(settled(a) if c else a for a, c in zip(arrays, ins)), *after)


ROW = struct((BLOCK, 1024), F32)
ROW16 = struct((BLOCK, 1024), BF16)
COLUMN = struct((BLOCK, 1), F32)
SENT = [ROW] + [ROW16] * (RING - 1)


def stack_rows(refs, cols=slice(None)):
    return jnp.concatenate([ref[:, cols] for ref in refs], axis=0)


def split_rows(total, outs, cols):
    outs[0][:, cols] = total[0:BLOCK]
    for k in range(1, len(outs)):
        outs[k][:, cols] = total[BLOCK * k : BLOCK * (k + 1)].astype(BF16)


def chunks(width=1024):
    return [slice(at, at + CHUNK) for at in range(0, width, CHUNK)]


def norm(v, gain, bias, a_ref, s_ref, r_ref):
    average = jnp.mean(v, axis=-1, keepdims=True)
    centred = v - average
    inv = lax.rsqrt(jnp.mean(centred * centred, axis=-1, keepdims=True) + EPSILON)
    standard = centred * inv
    s_ref[...] = standard
    r_ref[...] = inv
    a_ref[...] = (standard * gain + bias).astype(BF16)


def total_of(v_ref, near, far):
    total = v_ref[...].astype(F32) + near[...]
    for ref in far:
        total = total + ref[...].astype(F32)
    return total


def sum_norm_kernel(j, count, v_ref, near, *refs):
    far, (rows, v_out, a_ref, s_ref, r_ref) = refs[:count], refs[count:]
    v = total_of(v_ref, near, far)
    v_out[...] = v.astype(v_out.dtype)
    v = v_out[...].astype(F32)
    norm(v, rows[j : j + 1], rows[3 + j : 4 + j], a_ref, s_ref, r_ref)


def sum_norm(j, v, near, far, rows, kept, after=(), old=False, new=False):
    outs = [*cold_if(new, kept), ROW16, *cold_if(new, ROW, COLUMN)]
    return call(
        functools.partial(sum_norm_kernel, j, len(far)),
        outs,
        [*cold_if(old, v), near, *far, rows],
        after=after,
    )


def sum_last_kernel(v_ref, near, r1, r2, r3, v_out):
    v_out[...] = total_of(v_ref, near, (r1, r2, r3)).astype(BF16)


def sum_back_kernel(j, count, dv_ref, near, *refs):
    far, (s_ref, r_ref, rows, dv_out, g_out, norms) = refs[:count], refs[count:]
    da = near[...]
    for ref in far:
        da = da + ref[...].astype(F32)
    standard = s_ref[...]
    scaled = da * rows[j : j + 1]
    inner = (
        scaled
        - jnp.mean(scaled, axis=-1, keepdims=True)
        - standard * jnp.mean(scaled * standard, axis=-1, keepdims=True)
    )
    dv = dv_ref[...].astype(F32) + inner * r_ref[...]
    dv_out[...] = dv
    g_out[...] = dv.astype(BF16)
    norms[0:1] = jnp.sum(da * standard, axis=0, keepdims=True)
    norms[1:2] = jnp.sum(da, axis=0, keepdims=True)


def sum_back(j, dv, near, far, s, r, rows, after=(), old=False, new=False):
    return call(
        functools.partial(sum_back_kernel, j, len(far)),
        [*cold_if(new, ROW), ROW16, *cold_if(new, struct((2, 1024), F32))],
        [*cold_if(old, dv), near, *far, *cold_if(old, s, r, rows)],
        after=after,
    )


KEYS = 2 * RING * BLOCK


def block_of(place, b):
    return lax.rem(place[0] - b + RING, RING)


def lay_out_keys(place, own_ref, other_ref, kbuf, vbuf):
    core = place[1]
    for b in range(RING):
        j = block_of(place, b)
        own_at = pl.ds(pl.multiple_of((2 * b + core) * BLOCK, BLOCK), BLOCK)
        other_at = pl.ds(pl.multiple_of((2 * b + 1 - core) * BLOCK, BLOCK), BLOCK)
        for pair in range(2):
            here = slice(pair * 128, pair * 128 + 128)
            kbuf[own_at, here] = own_ref[j, :, 256 * pair : 256 * pair + 128]
            vbuf[own_at, here] = own_ref[j, :, 256 * pair + 128 : 256 * pair + 256]
            theirs = 1 - pair
            kbuf[other_at, here] = other_ref[j, :, 256 * theirs : 256 * theirs + 128]
            vbuf[other_at, here] = other_ref[j, :, 256 * theirs + 128 : 256 * theirs + 256]


def causal_tail(scores, core):
    key_at = lax.broadcasted_iota(jnp.int32, scores.shape, 0)
    query_at = lax.broadcasted_iota(jnp.int32, scores.shape, 1) + core * BLOCK
    return jnp.where(key_at <= query_at, scores, NEG_FILL)


class Tall:
    def __init__(self, *halves):
        self.halves = halves

    def __getitem__(self, key):
        rows, cols = key
        if rows.start is None:
            return jnp.concatenate([half[:, cols] for half in self.halves], axis=0)
        return self.halves[rows.start // 512][rows.start % 512 : rows.stop - 512 * (rows.start // 512), cols]


def qkv_rows(rows, own, far, q_ref, kv_ref):
    weights = (
        jnp.concatenate([own[:, 0:128], far[:, 0:128]], axis=1),
        own[:, 128:384],
        far[:, 128:384],
    )
    for n, weight in enumerate(weights):
        out = mm(rows, weight).astype(BF16)
        for k in range(RING):
            block = out[BLOCK * k : BLOCK * (k + 1)]
            if n == 0:
                q_ref[k] = block
            else:
                kv_ref[k, :, 256 * n - 256 : 256 * n] = block


def qkv_kernel(a0, a1, a2, a3, own0, own1, far0, far1, q_ref, kv_ref):
    own, far = Tall(own0, own1), Tall(far0, far1)
    qkv_rows(stack_rows((a0, a1, a2, a3)), own, far, q_ref, kv_ref)


def first_qkv_kernel(
    x0, x1, x2, x3, own0, own1, far0, far1, norms, q_ref, kv_ref, *refs
):
    outs, (s_ref, r_ref, all_ref) = refs[0:4], refs[4:7]
    own, far = Tall(own0, own1), Tall(far0, far1)
    for k, x_ref in enumerate((x0, x1, x2, x3)):
        x = x_ref[0:BLOCK].astype(F32)
        centred = x - jnp.mean(x, axis=-1, keepdims=True)
        inv = lax.rsqrt(jnp.mean(centred * centred, axis=-1, keepdims=True) + EPSILON)
        standard = centred * inv
        if k == 0:
            s_ref[...] = standard
            r_ref[...] = inv
        all_ref[BLOCK * k : BLOCK * (k + 1)] = standard.astype(BF16)
        outs[k][...] = (standard * norms[0:1] + norms[3:4]).astype(BF16)
    qkv_rows(stack_rows(outs), own, far, q_ref, kv_ref)


def lane_blocks(ref, at, cols):
    return jnp.concatenate(
        [ref[c : c + 128, at : at + 128] for c in range(cols.start, cols.stop, 128)], axis=1
    )


ALL_COLS = slice(0, 1024)


def self_forward_kernel(
    place, q_ref, own_ref, other_ref, w0, w1, w2, w3, o_ref, lse_ref, near, f1, f2, f3, kbuf, vbuf
):
    lay_out_keys(place, own_ref, other_ref, kbuf, vbuf)
    core = place[1]
    for b in range(RING):
        j = block_of(place, b)
        span = 2 * BLOCK * (b + 1)
        head = span - 2 * BLOCK
        for pair in range(2):
            outs = []
            for h in (2 * pair, 2 * pair + 1):
                cols = slice(HD * h, HD * h + HD)
                q = q_ref[j, :, cols] * 0.125
                last = causal_tail(mm_nt(kbuf[head:span, cols], q), core)
                top = jnp.max(last, axis=0, keepdims=True)
                if head:
                    early = mm_nt(kbuf[0:head, cols], q)
                    top = jnp.maximum(top, jnp.max(early, axis=0, keepdims=True))
                    early = jnp.exp(early - top)
                last = jnp.exp(last - top)
                total = jnp.sum(last, axis=0, keepdims=True)
                mixed = mm_tn(vbuf[head:span, cols], last.astype(BF16))
                if head:
                    total = total + jnp.sum(early, axis=0, keepdims=True)
                    mixed = mixed + mm_tn(vbuf[0:head, cols], early.astype(BF16))
                outs.append(mixed / total)
                lse_ref[h, j] = top + jnp.log(total)
            both = jnp.concatenate(outs, axis=0)
            o_ref[j, :, 128 * pair : 128 * pair + 128] = both.T.astype(BF16)
    rows = jnp.concatenate([o_ref[k] for k in range(RING)], axis=0)
    for cols in chunks():
        weight = jnp.concatenate([lane_blocks(w, 384, cols) for w in (Tall(w0, w1), Tall(w2, w3))], axis=0)
        split_rows(mm(rows, weight), (near, f1, f2, f3), cols)


def self_back_kernel(
    place, g0, g1, g2, g3, w0, w1, w2, w3, q_ref, own_ref, other_ref, lse_ref,
    dq_ref, down_ref, dother_ref, kbuf, vbuf, dobuf, dk, dv,
):
    rows = stack_rows((g0, g1, g2, g3))
    weight = jnp.concatenate([lane_blocks(w, 384, ALL_COLS) for w in (Tall(w0, w1), Tall(w2, w3))], axis=0)
    dobuf[...] = mm_nt(rows, weight).astype(BF16).reshape(dobuf.shape)
    lay_out_keys(place, own_ref, other_ref, kbuf, vbuf)
    core = place[1]
    for b in reversed(range(RING)):
        j = block_of(place, b)
        span = 2 * BLOCK * (b + 1)
        head = span - 2 * BLOCK
        for pair in range(2):
            lanes = slice(128 * pair, 128 * pair + 128)
            dqs, dks, dvs = [], [], []
            for h in (2 * pair, 2 * pair + 1):
                cols = slice(HD * h, HD * h + HD)
                q = q_ref[j, :, cols] * 0.125
                do = dobuf[j, :, cols]
                k = kbuf[0:span, cols]
                scores = mm_nt(k, q)
                last = causal_tail(scores[head:span], core)
                scores = jnp.concatenate([scores[0:head], last], axis=0) if head else last
                probs = jnp.exp(scores - lse_ref[h, j])
                dprobs = mm_nt(vbuf[0:span, cols], do)
                delta = jnp.sum(probs * dprobs, axis=0, keepdims=True)
                dscores = (probs * (dprobs - delta)).astype(BF16)
                dqs.append(mm_tn(k, dscores) * 0.125)
                dks.append(mm(dscores, q))
                dvs.append(mm(probs.astype(BF16), do))
            dq_ref[j, :, lanes] = jnp.concatenate(dqs, axis=0).T.astype(BF16)
            dk_new = jnp.concatenate(dks, axis=1)
            dv_new = jnp.concatenate(dvs, axis=1)
            if b == RING - 1:
                dk[0:span, lanes] = dk_new
                dv[0:span, lanes] = dv_new
            else:
                dk[0:span, lanes] += dk_new
                dv[0:span, lanes] += dv_new
    for b in range(RING):
        j = block_of(place, b)
        own_at = pl.ds(pl.multiple_of((2 * b + core) * BLOCK, BLOCK), BLOCK)
        other_at = pl.ds(pl.multiple_of((2 * b + 1 - core) * BLOCK, BLOCK), BLOCK)
        for pair in range(2):
            here = slice(pair * 128, pair * 128 + 128)
            theirs = 1 - pair
            down_ref[j, :, 256 * pair : 256 * pair + 128] = dk[own_at, here]
            down_ref[j, :, 256 * pair + 128 : 256 * pair + 256] = dv[own_at, here]
            dother_ref[j, :, 256 * theirs : 256 * theirs + 128] = dk[other_at, here].astype(BF16)
            dother_ref[j, :, 256 * theirs + 128 : 256 * theirs + 256] = dv[other_at, here].astype(BF16)


def keys_total(down_ref, dother_ref):
    total = [down_ref[k] + dother_ref[k].astype(F32) for k in range(RING)]
    return jnp.concatenate(total, axis=0).astype(BF16)


def self_rows_back_kernel(
    dq_ref, down_ref, dother_ref, own0, own1, far0, far1, near, f1, f2, f3
):
    own, far = Tall(own0, own1), Tall(far0, far1)
    dq = jnp.concatenate([dq_ref[k] for k in range(RING)], axis=0)
    rows = jnp.concatenate([dq, keys_total(down_ref, dother_ref)], axis=1)
    for cols in chunks():
        weight = jnp.concatenate(
            [own[cols, 0:128], far[cols, 0:128], own[cols, 128:384], far[cols, 128:384]], axis=1
        )
        split_rows(mm_nt(rows, weight), (near, f1, f2, f3), cols)


def last_rows_back_kernel(
    dq_ref, down_ref, dother_ref, own0, own1, far0, far1, all_ref, n0, n1, n2, n3, n4,
    near, f1, f2, f3, norms,
):
    own, far = Tall(own0, own1), Tall(far0, far1)
    dq = jnp.concatenate([dq_ref[k] for k in range(RING)], axis=0)
    rows = jnp.concatenate([dq, keys_total(down_ref, dother_ref)], axis=1)
    for n, ref in enumerate((n0, n1, n2, n3, n4), 1):
        norms[2 * n : 2 * n + 2] = ref[...]
    norms[12:16] = jnp.zeros((4, 1024), F32)
    for cols in chunks():
        weight = jnp.concatenate(
            [own[cols, 0:128], far[cols, 0:128], own[cols, 128:384], far[cols, 128:384]], axis=1
        )
        total = mm_nt(rows, weight)
        near[:, cols] = total[0:BLOCK]
        for k, out in enumerate((f1, f2, f3), 1):
            out[0:BLOCK, cols] = total[BLOCK * k : BLOCK * (k + 1)].astype(BF16)
        norms[0:1, cols] = jnp.sum(total * all_ref[:, cols].astype(F32), axis=0, keepdims=True)
        norms[1:2, cols] = jnp.sum(total, axis=0, keepdims=True)
    for out in (f1, f2, f3):
        out[BLOCK : BLOCK + 16] = norms[...].astype(BF16)


def last_sum_back_kernel(dv_ref, near, r1, r2, r3, s_ref, r_ref, rows, norms, g_out, total):
    da = near[...]
    for ref in (r1, r2, r3):
        da = da + ref[0:BLOCK].astype(F32)
    standard = s_ref[...]
    scaled = da * rows[0:1]
    inner = (
        scaled
        - jnp.mean(scaled, axis=-1, keepdims=True)
        - standard * jnp.mean(scaled * standard, axis=-1, keepdims=True)
    )
    g_out[...] = (dv_ref[...].astype(F32) + inner * r_ref[...]).astype(BF16)
    total[...] = norms[...] + sum(ref[BLOCK : BLOCK + 16].astype(F32) for ref in (r1, r2, r3))


def cross_cols(w, layer, place, g, at, rows):
    first = RING * block_of(place, g)
    parts = [
        w[2 * (first + y) + layer, :, at : at + 128]
        for y in range(rows.start // 256, rows.stop // 256)
    ]
    return parts[0] if len(parts) == 1 else jnp.concatenate(parts, axis=0)


def cross_blocks(w, layer, place, g, cols):
    first = RING * block_of(place, g)
    parts = []
    for c in range(cols.start, cols.stop, 128):
        at = c % 256
        parts.append(w[2 * (first + c // 256) + layer, at : at + 128, 128:256])
    return jnp.concatenate(parts, axis=1)


def cross_mask(scores, length):
    slots = lax.broadcasted_iota(jnp.int32, scores.shape, 0)
    return jnp.where(slots < length, scores, NEG_FILL)


def cross_forward_kernel(layer, place, lengths, mine, theirs, *refs):
    w, kv, (q_ref, o_ref, lse_ref, near, far) = refs[0], refs[1:5], refs[5:]
    rows = stack_rows((mine, theirs))
    for g in range(RING):
        lanes = slice(128 * g, 128 * g + 128)
        q_ref[:, lanes] = mm(rows, cross_cols(w, layer, place, g, 0, slice(0, 1024))).astype(BF16)
        outs = []
        for p in range(2):
            h = 2 * g + p
            q = q_ref[:, HD * h : HD * h + HD] * 0.125
            k = kv[g][layer, :, HD * p : HD * p + HD]
            v = kv[g][layer, :, 128 + HD * p : 128 + HD * p + HD]
            scores = cross_mask(mm_nt(k, q), lengths[place[4], 0])
            top = jnp.max(scores, axis=0, keepdims=True)
            raised = jnp.exp(scores - top)
            total = jnp.sum(raised, axis=0, keepdims=True)
            outs.append(mm_tn(v, raised.astype(BF16)) / total)
            lse_ref[h] = top + jnp.log(total)
        o_ref[:, lanes] = jnp.concatenate(outs, axis=0).T.astype(BF16)
    for cols in chunks():
        weight = jnp.concatenate([cross_blocks(w, layer, place, g, cols) for g in range(RING)], axis=0)
        split_rows(mm(o_ref[...], weight), (near, far), cols)


def cross_back_kernel(layer, place, lengths, mine, theirs, *refs):
    w, kv, (q_ref, lse_ref) = refs[0], refs[1:5], refs[5:7]
    dq_ref, dkv, (near, far) = refs[7], refs[8:12], refs[12:14]
    rows = stack_rows((mine, theirs))
    for g in range(RING):
        lanes = slice(128 * g, 128 * g + 128)
        dmixed = mm_nt(rows, cross_blocks(w, layer, place, g, ALL_COLS)).astype(BF16)
        dqs, dks, dvs = [], [], []
        for p in range(2):
            h = 2 * g + p
            q = q_ref[:, HD * h : HD * h + HD] * 0.125
            do = dmixed[:, HD * p : HD * p + HD]
            k = kv[g][layer, :, HD * p : HD * p + HD]
            v = kv[g][layer, :, 128 + HD * p : 128 + HD * p + HD]
            probs = jnp.exp(cross_mask(mm_nt(k, q), lengths[place[4], 0]) - lse_ref[h])
            dprobs = mm_nt(v, do)
            delta = jnp.sum(probs * dprobs, axis=0, keepdims=True)
            dscores = (probs * (dprobs - delta)).astype(BF16)
            dqs.append(mm_tn(k, dscores) * 0.125)
            dks.append(mm(dscores, q))
            dvs.append(mm(probs.astype(BF16), do))
        dq_ref[:, lanes] = jnp.concatenate(dqs, axis=0).T.astype(BF16)
        dkv[g][...] = jnp.concatenate(dks + dvs, axis=1).astype(BF16)
    for cols in chunks():
        weight = jnp.concatenate([cross_cols(w, layer, place, g, 0, cols) for g in range(RING)], axis=1)
        split_rows(mm_nt(dq_ref[...], weight), (near, far), cols)


def up_cols(own, far, at):
    refs, at = (own, at) if at < 512 else (far, at - 512)
    return jnp.concatenate([ref[:, at : at + CHUNK] for ref in refs], axis=0)


def up_rows(own, far, cols):
    half, rows = cols.start // 512, slice(cols.start % 512, cols.start % 512 + CHUNK)
    return jnp.concatenate([own[half][rows, 0:512], far[half][rows, 0:512]], axis=1)


def down_rows(own, far, at):
    refs, at = (own, at) if at < 512 else (far, at - 512)
    return jnp.concatenate([ref[at : at + CHUNK, 512:1024] for ref in refs], axis=1)


def down_cols(own, far, at):
    half, lanes = at // 512, slice(512 + at % 512, 512 + at % 512 + CHUNK)
    return jnp.concatenate([own[half][:, lanes], far[half][:, lanes]], axis=0)


def ffn_forward_kernel(
    a0, a1, a2, a3, own0, own1, far0, far1, hidden_ref, slope_ref, near, f1, f2, f3
):
    own, far = (own0, own1), (far0, far1)
    root = 0.7978845608028654
    rows = stack_rows((a0, a1, a2, a3))
    for cols in chunks():
        pre = mm(rows, up_cols(own, far, cols.start))
        square = pre * pre
        t = jnp.tanh(root * (pre + 0.044715 * pre * square))
        half = 0.5 * (1.0 + t)
        hidden_ref[:, cols] = (pre * half).astype(BF16)
        slope_ref[:, cols] = half + 0.5 * pre * (1.0 - t * t) * (root * (1.0 + 3 * 0.044715 * square))
    for cols in chunks():
        split_rows(mm(hidden_ref[...], down_cols(own, far, cols.start)), (near, f1, f2, f3), cols)


def ffn_back_kernel(
    g0, g1, g2, g3, own0, own1, far0, far1, slope_ref, dpre_ref, near, f1, f2, f3
):
    own, far = (own0, own1), (far0, far1)
    rows = stack_rows((g0, g1, g2, g3))
    for cols in chunks():
        dhidden = mm_nt(rows, down_rows(own, far, cols.start))
        dpre_ref[:, cols] = (dhidden * slope_ref[:, cols]).astype(BF16)
    for cols in chunks():
        split_rows(mm_nt(dpre_ref[...], up_rows(own, far, cols)), (near, f1, f2, f3), cols)


def ffn_grads_kernel(hidden, g0, g1, g2, g3, dpre, a0, a1, a2, a3, ours, t0, t1, t2, t3):
    theirs = (t0, t1, t2, t3)
    g = stack_rows((g0, g1, g2, g3))
    a = stack_rows((a0, a1, a2, a3))
    for n in (2, 3, 0, 1):
        down = mm_tn(hidden[:, CHUNK * n : CHUNK * n + CHUNK], g)
        if n >= 2:
            theirs[n - 2][...] = down.astype(BF16)
        else:
            ours[CHUNK * n : CHUNK * n + CHUNK] = down
    for half in (1, 0):
        for n in range(4):
            up = mm_tn(a[:, CHUNK * n : CHUNK * n + CHUNK], dpre[:, 512 * half : 512 * half + 512])
            lanes = slice(512 * (n // 2), 512 * (n // 2) + 512)
            if half:
                theirs[2 + n % 2][:, lanes] = up.astype(BF16)
            else:
                ours[512 + CHUNK * (n % 2) : 512 + CHUNK * (n % 2) + CHUNK, lanes] = up


def ffn_total(ours, came, rows):
    n, at = rows.start // CHUNK, rows.start % CHUNK
    return ours[rows] + came[n][at : at + rows.stop - rows.start].astype(F32)


def cross_shares(k, g, a, mixed, dq, keys, memory):
    lanes = slice(128 * k, 128 * k + 128)
    return mm_tn(dq[:, lanes], a), mm_tn(mixed[:, lanes], g), mm_tn(keys[...], memory)


def cross_chunk_kernel(place, mixed, g_mine, g_theirs, dq, a_mine, a_theirs, c0, c1, c2, c3, total):
    g = stack_rows((g_mine, g_theirs))
    a = stack_rows((a_mine, a_theirs))
    for k in range(RING):
        lanes = slice(128 * k, 128 * k + 128)
        parts = (mm_tn(dq[:, lanes], a), mm_tn(mixed[:, lanes], g))
        for i in range(8):
            at = 32 * (i % 4)
            total[128 * i + 32 * k : 128 * i + 32 * k + 32] = parts[i // 4][at : at + 32]
    cut_chunks(place, total, (c0, c1, c2, c3))


def cross_sum_kernel(c0, r1, r2, r3, k0, k1, k2, k3, *outs):
    sums = [c0[z] + sum(r[z].astype(F32) for r in (r1, r2, r3)) for z in range(2)]
    for k, (key, out) in enumerate(zip((k0, k1, k2, k3), outs)):
        for z in range(2):
            out[32 * z : 32 * z + 32] = sums[z][32 * k : 32 * k + 32].astype(out.dtype)
        for i in range(4):
            out[64:128, 256 * i : 256 * i + 256] = key[64 * i : 64 * i + 64].astype(out.dtype)


def cross_first_kernel(
    place, ours, q0, q1, q2, q3, mixed, g_mine, g_theirs, dq, a_mine, a_theirs, k0, k1, k2, k3,
    memory, out,
):
    g = stack_rows((g_mine, g_theirs))
    a = stack_rows((a_mine, a_theirs))
    for i in range(8):
        rows = slice(128 * i, 128 * i + 128)
        out[i, 0:128] = ffn_total(ours, (q0, q1, q2, q3), rows).astype(BF16)
    for k, key in enumerate((k0, k1, k2, k3)):
        queries, outs, keys = cross_shares(k, g, a, mixed, dq, key, memory[...])
        for i in range(8):
            part, at = (queries, outs)[i // 4], 32 * (i % 4)
            to = pl.multiple_of(128 + 64 * block_of(place, k), 64)
            out[i, pl.ds(to, 32)] = part[at : at + 32].astype(BF16)
            out[i, pl.ds(pl.multiple_of(to + 32, 32), 32)] = keys[32 * i : 32 * i + 32].astype(BF16)


def self_grads_kernel(
    mixed, g0, g1, g2, g3, dq, down_ref, dother_ref, a0, a1, a2, a3, ours, t0, t1
):
    g = stack_rows((g0, g1, g2, g3))
    a = stack_rows((a0, a1, a2, a3))
    keys = keys_total(down_ref, dother_ref)
    outs, queries = [jnp.concatenate([r[k] for k in range(RING)], axis=0) for r in (mixed, dq)]
    t0[0:128] = mm_tn(outs[:, 128:256], g).astype(BF16)
    t0[128:256] = mm_tn(queries[:, 128:256], a).astype(BF16)
    t1[...] = mm_tn(keys[:, 256:512], a).astype(BF16)
    ours[0:128] = mm_tn(outs[:, 0:128], g)
    ours[128:256] = mm_tn(queries[:, 0:128], a)
    ours[256:512] = mm_tn(keys[:, 0:256], a)


def rows_kernel(place, x_ref, memory_ref, g_ref, x, both, g):
    mine = place[4]
    x[...] = x_ref[mine]
    both[0:BLOCK] = x_ref[mine]
    both[BLOCK : BLOCK + 32] = memory_ref[mine]
    g[...] = g_ref[mine]


def norm_rows_kernel(gain, bias, out):
    out[0:3] = gain[0]
    out[3:6] = bias[0]


def both_norms_kernel(place, mine, other, first, second):
    first[...] = jnp.where(place[4] == 0, mine[...], other[...])
    second[...] = jnp.where(place[4] == 0, other[...], mine[...])


def memory_blocks_kernel(x0, x1, x2, x3, out):
    for k, ref in enumerate((x0, x1, x2, x3)):
        out[32 * k : 32 * k + 32] = ref[BLOCK : BLOCK + 32]


def pack_kernel(place, w_ref, out_ref, q_ref, cross_ref, kv_ref, first, second, part, whole):
    for i in range(3):
        whole[:, 128 * i : 128 * i + 128] = w_ref[i]
    for i in range(8):
        rows = slice(128 * i, 128 * i + 128)
        whole[rows, 384:512] = out_ref[:, rows]
        whole[rows, 640:768] = cross_ref[:, rows]
    whole[:, 512:640] = q_ref[...]
    whole[:, 768:1024] = kv_ref[...]
    first[...] = whole[0:512, 0:512]
    second[...] = whole[512:1024, 0:512]
    part[...] = whole[pl.ds(pl.multiple_of(place[2] * 256, 256), 256)]


def pack_ffn_kernel(up_ref, down_ref, out):
    out[:, 0:512] = up_ref[...]
    out[0:512, 512:1024] = down_ref[:, 0:512]
    out[512:1024, 512:1024] = down_ref[:, 512:1024]


def quarter(place, k):
    return pl.ds(pl.multiple_of(lax.rem(place[2] - k + RING, RING) * 256, 256), 256)


def by_section(place, write):
    pl.when(place[4] == 0)(lambda: write(0, 1))
    pl.when(place[4] == 1)(lambda: write(1, 0))


def fill_halves(place, parts, halves, cols):
    for k, ref in enumerate(parts):
        y = lax.rem(place[2] - k + RING, RING)
        rows = pl.ds(pl.multiple_of(lax.rem(y, 2) * 256, 256), 256)

        def put(half, ref=ref, rows=rows):
            halves[half][rows] = ref[:, cols]

        pl.when(y < 2)(functools.partial(put, 0))
        pl.when(y >= 2)(functools.partial(put, 1))


def both_selfs_kernel(
    place, mine0, mine1, r0, r1, r2, r3, a0, a1, b0, b1
):
    def write(own, far):
        halves = ((a0, a1), (b0, b1))
        halves[own][0][...] = mine0[...]
        halves[own][1][...] = mine1[...]
        fill_halves(place, (r0, r1, r2, r3), halves[far], slice(0, 512))

    by_section(place, write)


def rest_kernel(place, mine, other, out, parts):
    def write(own, far):
        parts[own] = mine[:, 512:768]
        parts[far] = other[:, 512:768]

    by_section(place, write)
    out[:, 0:512] = other[:, 0:512]
    out[:, 512:768] = other[:, 768:1024]


def keys_kernel(place, kv_ref, k0, k1, k2, k3, x0, x1, x2, x3, e_far, out, memory, pair):
    for k, ref in enumerate((x0, x1, x2, x3)):
        at = 64 * block_of(place, k)
        memory[pl.ds(pl.multiple_of(at + 32 * place[1], 32), 32)] = ref[BLOCK : BLOCK + 32]
        memory[pl.ds(pl.multiple_of(at + 32 - 32 * place[1], 32), 32)] = e_far[32 * k : 32 * k + 32]
    for k, ref in enumerate((k0, k1, k2, k3)):
        pair[quarter(place, k)] = ref[:, 512:768]
    mine = mm(memory[...], kv_ref[...]).astype(BF16)
    other = mm(memory[...], pair[...]).astype(BF16)

    def write(own, far):
        out[own] = mine
        out[far] = other

    by_section(place, write)


def both_ffns_kernel(place, mine, other, a0, a1, b0, b1):
    def write(own, far):
        halves = ((a0, a1), (b0, b1))
        for half in range(2):
            rows = slice(512 * half, 512 * half + 512)
            halves[own][half][...] = mine[rows]
            halves[far][half][...] = other[rows]

    by_section(place, write)


def cut_chunks(place, total, outs):
    rows = total.shape[0] // 8
    for k, out in enumerate(outs):
        y = lax.rem(place[2] - k + RING, RING)
        for z in range(2):
            at = pl.ds(pl.multiple_of((RING * z + y) * rows, rows), rows)
            out[z] = total[at].astype(out.dtype)


def join_kernel(f, q0, q1, q2, q3, ours, t0, t1, out):
    for i in range(8):
        out[i, 0:128] = ffn_total(f, (q0, q1, q2, q3), slice(128 * i, 128 * i + 128)).astype(BF16)
        theirs = (t0, t1)[i // 4]
        at = 64 * (i % 4)
        out[i, 128:192] = (ours[64 * i : 64 * i + 64] + theirs[at : at + 64].astype(F32)).astype(BF16)


def rest_chunk_kernel(
    place, ours, t0, t1, w0, w1, w2, w3, memory, c0, c1, c2, c3, cross, total
):
    came = w0[...] + sum(w[...].astype(F32) for w in (w1, w2, w3))
    for z in range(2):
        cross[z] = came[32 * z : 32 * z + 32]
    keys = jnp.concatenate([came[64:128, 256 * i : 256 * i + 256] for i in range(4)], axis=0)
    keys = mm_tn(keys.astype(BF16), memory[...])
    for i in range(8):
        theirs = (t0, t1)[i // 4]
        at, to = 64 * (i % 4), 96 * i
        total[to : to + 64] = ours[64 * i : 64 * i + 64] + theirs[at : at + 64].astype(F32)
        total[to + 64 : to + 96] = keys[32 * i : 32 * i + 32]
    cut_chunks(place, total, (c0, c1, c2, c3))


def split_kernel(grads, ffn, cross):
    ffn[...] = grads[0:128]
    cross[...] = grads[128:384]


def chunk_shapes(rows):
    return [Cold(struct((2, rows, 1024), F32))] + [struct((2, rows, 1024), BF16)] * 3


def sum_y_kernel(place, c0, r1, r2, r3, mid, first, ffn, cross, keep, over_z, over_s):
    z = place[3]

    def half(n):
        rest = c0[n] + sum(r[n].astype(F32) for r in (r1, r2, r3))
        return jnp.concatenate([rest[0:64], mid[n], rest[64:96]], axis=0)

    over_z[...] = half(1 - z).astype(BF16)
    rest = half(z)

    def write_first():
        keep[0:128] = rest
        keep[128:256] = first[0:128].astype(F32)
        over_s[0:64] = first[128:192]
        over_s[64:128] = cross[...]
        over_s[128:256] = ffn[...]

    def write_second():
        keep[0:64] = first[128:192].astype(F32)
        keep[64:128] = cross[...].astype(F32)
        keep[128:256] = ffn[...].astype(F32)
        over_s[0:128] = rest.astype(BF16)
        over_s[128:256] = first[0:128]

    pl.when(place[4] == 0)(write_first)
    pl.when(place[4] == 1)(write_second)


def sum_rest_kernel(place, keep, from_z, from_s, from_both, norms, came, out):
    rest = keep[0:128] + from_s[0:128].astype(F32)
    other = from_z[...].astype(F32) + from_both[...].astype(F32)
    out[0:128] = jnp.where(place[4] == 0, rest + other, rest).astype(BF16)
    out[128:144] = (norms[...] + came[...]).astype(BF16)
    out[144:272] = (keep[128:256] + from_s[128:256].astype(F32)).astype(BF16)


def exchange(over_z, over_s):
    from_both = lax.ppermute(over_z, ("section", "dz"), [(2, 1), (3, 0)])
    return swap(over_z, "dz"), swap(over_s, "section"), from_both


def norms_kernel(place, all_ref, keep, over_s):
    total = sum(all_ref[272 * i + 128 : 272 * i + 144].astype(F32) for i in range(8))
    first, second = total[0:6], total[6:12]
    keep[0:6] = jnp.where(place[4] == 0, first, second)
    over_s[0:6] = jnp.where(place[4] == 0, second, first)
    keep[6:8] = jnp.zeros((2, 1024), F32)
    over_s[6:8] = jnp.zeros((2, 1024), F32)


def last_norms_kernel(mine, came, gains, biases, ffn):
    norms = mine[...] + came[...]
    for j in range(2):
        gains[j : j + 1] = norms[2 * j : 2 * j + 1]
        biases[j : j + 1] = norms[2 * j + 1 : 2 * j + 2]
    ffn[...] = norms[4:6]


def last_kernel(
    all_ref, out_ref, self_ref, q_ref, cross_ref, kv_ref, up_ref, down_ref
):
    def rows(at, count, span):
        return jnp.concatenate(
            [all_ref[272 * i + at : 272 * i + at + span] for i in range(count, count + 128 // span)],
            axis=0,
        ).astype(F32)

    out_ref[...] = rows(0, 0, 64)
    for i in range(3):
        self_ref[i] = rows(0, 2 + 2 * i, 64).T
    q_ref[...] = rows(64, 0, 32).T
    cross_ref[...] = rows(64, 4, 32)
    kv_ref[pl.ds(0, 1024, stride=2)] = rows(96, 0, 32).T
    kv_ref[pl.ds(1, 1024, stride=2)] = rows(96, 4, 32).T
    for i in range(4):
        here = slice(128 * i, 128 * i + 128)
        down_ref[here] = rows(144, i, 128)
        up = rows(144, 4 + i, 128)
        up_ref[here] = up[:, 0:512]
        up_ref[512 + 128 * i : 640 + 128 * i] = up[:, 512:1024]


def other_layer_kernel(place, text, unit, input_grad, text_grad, out):
    def write(rows, grads):
        out[0:BLOCK] = rows[...]
        out[BLOCK : 2 * BLOCK] = grads[...]

    pl.when(place[4] == 0)(lambda: write(unit, text_grad))
    pl.when(place[4] == 1)(lambda: write(text, input_grad))


def both_batches_kernel(place, text, unit, input_grad, text_grad, came, states, grads):
    mine = place[4]

    def write(rows, own):
        states[mine] = rows[...]
        grads[mine] = own[...]

    pl.when(mine == 0)(lambda: write(text, input_grad))
    pl.when(mine == 1)(lambda: write(unit, text_grad))
    states[1 - mine] = came[0:BLOCK]
    grads[1 - mine] = came[BLOCK : 2 * BLOCK]


def layer_forward(layer, v, first, weights, ffns, place, lengths, rows, after):
    own, far, cross, kv = weights
    heads = [struct((RING, BLOCK, 256), BF16), struct((RING, BLOCK, 512), BF16)]
    if layer == 0:
        q, kv_self, *rest = call(
            first_qkv_kernel,
            heads + cold(*[ROW16] * RING, ROW, COLUMN, struct((RING * BLOCK, 1024), BF16)),
            [*cold(*first, *own, *far), rows],
            after=after.get("qkv", ()),
        )
        full1, (s1, r1, all1) = rest[0:4], rest[4:7]
    else:
        a1, s1, r1, all1 = *first, None
        full1 = gather_x(a1)
        q, kv_self = call(qkv_kernel, heads, [*full1, *cold(*own, *far)], after=after.get("qkv", ()))
    kv_other = swap(kv_self, "core")
    if "keys" in after:
        after["keys"](q)
    mixed1, lse1, *sent = call(
        self_forward_kernel,
        cold_if(not layer, struct((RING, BLOCK, 256), BF16), struct((4, RING, 1, BLOCK), F32)) + SENT,
        [q, kv_self, kv_other, *cold(*own, *far)],
        scalars=[place],
        scratch=[pltpu.VMEM((KEYS, 256), BF16), pltpu.VMEM((KEYS, 256), BF16)],
        after=after.get("self", ()),
    )
    waits = after["sum1"](mixed1) if "sum1" in after else ()
    v1, a2, s2, r2 = sum_norm(1, v, sent[0], send_x(sent[1:]), rows, ROW, after=waits, new=not layer)
    a2_theirs = swap(a2, "core")
    cq, mixed2, lse2, near, far2 = call(
        functools.partial(cross_forward_kernel, layer),
        [
            struct((2 * BLOCK, 512), BF16),
            struct((2 * BLOCK, 512), BF16),
            struct((2 * RING, 1, 2 * BLOCK), F32),
            ROW,
            ROW16,
        ],
        [a2, a2_theirs, *cold(cross, *kv[0:4])],
        scalars=[place, lengths],
        after=after.get("cross", ()),
    )
    v2, a3, s3, r3 = sum_norm(
        2, v1, near, [swap(far2, "core")], rows, ROW, after=after.get("sum2", ()), old=not layer
    )
    full3 = gather_x(a3)
    hidden, slope, *sent = call(
        ffn_forward_kernel,
        [struct((RING * BLOCK, 1024), BF16), struct((RING * BLOCK, 1024), F32)] + SENT,
        [*full3, *cold(*ffns[layer])],
        after=after.get("ffn", ()),
    )
    stored = (
        (s1, r1, full1, q, kv_self, kv_other, mixed1, lse1, all1),
        (s2, r2, a2, a2_theirs, cq, mixed2, lse2),
        (s3, r3, full3, hidden, slope),
    )
    return v2, sent[0], send_x(sent[1:]), stored


def layer_back(layer, dv, full_g3, stored, weights, ffns, place, lengths, rows, steps):
    own, far, cross, kv = weights
    (s1, r1, full1, q, kv_self, kv_other, mixed1, lse1, all1), second, third = stored
    s2, r2, a2, a2_theirs, cq, mixed2, lse2 = second
    s3, r3, full3, hidden, slope = third
    old = layer == 0
    dpre, *sent = call(
        ffn_back_kernel,
        [struct((RING * BLOCK, 1024), BF16)] + SENT,
        [*full_g3, *cold(*ffns[layer]), *cold_if(old, slope)],
        after=steps.get("ffn", ()),
    )
    ffn_ours, *ffn_theirs = call(
        ffn_grads_kernel,
        [struct((1024, 1024), F32)] + [struct((CHUNK, 1024), BF16)] * 4,
        [*cold_if(old, hidden), *full_g3, dpre, *cold_if(old, *full3)],
    )
    ffn_parts = [ffn_ours, *(swap(part, "core") for part in ffn_theirs)]
    dv2, g2, norms3 = sum_back(
        2, dv, sent[0], send_x(sent[1:]), s3, r3, rows,
        after=[ffn_theirs[0], *steps.get("sum3", ())], old=old, new=old,
    )
    g2_theirs = swap(g2, "core")
    pair_keys = struct((2 * BLOCK, 256), BF16)
    dcq, *rest = call(
        functools.partial(cross_back_kernel, layer),
        [struct((2 * BLOCK, 512), BF16)] + [pair_keys] * RING + [ROW, ROW16],
        [g2, g2_theirs, *cold(cross, *kv[0:4]), *cold_if(old, cq, lse2)],
        scalars=[place, lengths],
        after=steps.get("cross", lambda parts, g2: ())(ffn_parts, g2),
    )
    dkv_cross, (near, far2) = rest[:RING], rest[RING:]
    dv1, g1, norms2 = sum_back(1, dv2, near, [swap(far2, "core")], s2, r2, rows, old=old, new=True)
    full_g1 = gather_x(g1)
    cross_grads = [*cold_if(old, mixed2), g2, g2_theirs, dcq, *cold_if(old, a2, a2_theirs)]
    middle, waits = steps["middle"](ffn_parts, cross_grads, dkv_cross, g1)
    dq, dkv_own, dkv_theirs = call(
        self_back_kernel,
        [
            struct((RING, BLOCK, 256), BF16),
            struct((RING, BLOCK, 512), F32),
            struct((RING, BLOCK, 512), BF16),
        ],
        [*full_g1, *cold(*own, *far, q, kv_self, kv_other, lse1)],
        scalars=[place],
        scratch=[
            pltpu.VMEM((KEYS, 256), BF16),
            pltpu.VMEM((KEYS, 256), BF16),
            pltpu.VMEM((RING, BLOCK, 256), BF16),
            pltpu.VMEM((KEYS, 256), F32),
            pltpu.VMEM((KEYS, 256), F32),
        ],
        after=waits,
    )
    back = [dq, dkv_own, swap(dkv_theirs, "core")]

    def self_grads(waits=()):
        ours, *theirs = call(
            self_grads_kernel,
            [struct((512, 1024), F32)] + [struct((2 * BLOCK, 1024), BF16)] * 2,
            [*cold(mixed1), *full_g1, *back, *cold(*full1)],
            after=waits,
        )
        return [ours, *(swap(part, "core") for part in theirs)], theirs

    if layer == 0:
        share, *others = call(cross_sum_kernel, [ROW, ROW16, ROW16, ROW16], middle)
        self_parts, theirs = self_grads([share])
        waits = steps["late"]([share, *send_x(others)], self_parts, theirs)
        tall = struct((BLOCK + 16, 1024), BF16)
        near, *others, sums = call(
            last_rows_back_kernel,
            [ROW, tall, tall, tall, struct((16, 1024), F32)],
            [*back, *cold(*own, *far, all1, norms2, norms3, *steps["norms"])],
            after=waits,
        )
        steps["tail"]["near"] = near
        g0, sums = call(
            last_sum_back_kernel,
            [ROW16, struct((16, 1024), F32)],
            [*cold(dv1), near, *send_x(others), *cold(s1, r1, rows, sums)],
        )
        return g0, middle, self_parts, sums
    else:
        sent = call(self_rows_back_kernel, SENT, [*back, *cold(*own, *far)])
        self_parts, theirs = self_grads()
        waits = [theirs[0], *steps["late"]()]
    dv0, g0, norms1 = sum_back(
        0, dv1, sent[0], send_x(sent[1:]), s1, r1, rows, after=waits, old=True
    )
    return g0, middle, self_parts, (norms1, norms2, norms3)


def reduce_dp(grads):
    total = lax.psum_scatter(grads, ("dz", "dy"), scatter_dimension=0, tiled=True)
    return total.reshape(grads.shape[1:])


def shards(
    inputs,
    memory_states,
    source_lengths,
    cotangent,
    norm_gain,
    norm_bias,
    w_self,
    w_self_out,
    w_cross_q,
    w_cross_kv,
    w_cross_out,
    up_weight,
    down_weight,
):
    place = PLACE

    def along_y(part):
        return [part] + [shift(part, "dy", k) for k in range(1, RING)]

    row16 = struct((BLOCK, 1024), BF16)
    kv_mine = w_cross_kv[0].reshape(w_cross_kv.shape[1], -1)
    half = struct((512, 512), BF16)
    *self_mine, mine = call(
        pack_kernel,
        [*cold(half, half), struct((256, 1024), BF16)],
        cold(w_self[0].transpose(1, 0, 2), w_self_out[0], w_cross_q[0], w_cross_out[0], kv_mine),
        scalars=[place],
        scratch=[pltpu.VMEM((1024, 1024), BF16)],
    )
    other = swap(mine, "section")
    x, rows_first, g_top = call(
        rows_kernel,
        cold(row16, struct((BLOCK + 32, 1024), BF16), row16),
        cold(inputs[:, :, 0], memory_states[:, :, 0], cotangent[:, :, 0]),
        scalars=[place],
        after=[mine],
    )
    norms = call(
        norm_rows_kernel, [struct((6, 1024), F32)], [norm_gain, norm_bias], after=[mine]
    )[0]
    norms_other = swap(norms, "section")
    rows_first = gather_x(rows_first)
    ffn_half = struct((512, 1024), BF16)
    ffn_mine, ffn_done = call(
        pack_ffn_kernel,
        cold(struct((1024, 1024), BF16)),
        cold(up_weight[0], down_weight[0]),
        after=[other, *rows_first[1:]],
        token=True,
    )
    ffn_other = swap(ffn_mine, "section")
    norms = call(
        both_norms_kernel, [struct((6, 1024), F32)] * 2, [norms, norms_other], scalars=[place]
    )

    rest, parts = call(
        rest_kernel,
        [struct((256, 768), BF16), Cold(struct((2, 256, 256), BF16))],
        [mine, other],
        scalars=[place],
        after=[norms_other, *rows_first[1:]], lazy=False)
    rests = along_y(rest)
    e_far = swap(call(memory_blocks_kernel, [row16], rows_first)[0], "core")
    a0, a1, b0, b1 = call(
        both_selfs_kernel,
        [half, half, *cold(half, half)],
        [*cold(*self_mine), *rests],
        scalars=[place],
        after=[e_far, norms[0], ffn_done], lazy=False)
    selfs = [(a0, a1), (b0, b1)]
    selfs_far = [tuple(swap(w, "core") for w in pair) for pair in selfs]
    crosses = lax.all_gather(parts, ("tx", "dy"), axis=0, tiled=True)
    ffns, kvs = [], []

    def make_keys(q):
        keyed, memory = call(
            keys_kernel,
            cold(struct((2, 256, 256), BF16), struct((256, 1024), BF16)),
            cold(kv_mine, *rests, *rows_first, e_far),
            scalars=[place],
            scratch=[pltpu.VMEM((1024, 256), BF16)],
            after=[q],
        )
        kvs.extend(gather_x(keyed))
        kvs.append(memory)


    def made(mixed):
        a0, a1, b0, b1, done = call(
            both_ffns_kernel,
            cold(*[ffn_half] * 4),
            cold(ffn_mine, ffn_other),
            scalars=[place],
            after=[mixed],
            token=True, lazy=False)
        for first, second in ((a0, a1), (b0, b1)):
            ffns.append((first, second, swap(first, "core"), swap(second, "core")))
        return [done]

    weights = [(selfs[i], selfs_far[i], crosses, kvs) for i in range(2)]

    v, near, far, stored0 = layer_forward(
        0, x, rows_first, weights[0], ffns, place, source_lengths, norms[0], {"keys": make_keys, "sum1": lambda mixed: [*kvs[1:4], *made(mixed)]}
    )
    text, *normed = sum_norm(0, v, near, far, norms[1], ROW16)
    v, near, far, stored1 = layer_forward(
        1, text, normed, weights[1], ffns, place, source_lengths, norms[1], {}
    )
    memory = kvs[4]
    full_top = gather_x(g_top)
    unit = call(sum_last_kernel, cold(ROW16), [*cold(v), near, *far])[0]

    def middle_second(ffn_parts, cross_grads, keys, after):
        out, done = call(
            cross_first_kernel,
            cold(struct((8, 384, 1024), BF16)),
            [*ffn_parts, *cross_grads, *keys, *cold(memory)],
            scalars=[place],
            after=[after],
            token=True,
        )
        return out, [done]

    text_grad, grads_a, self1, norms1 = layer_back(
        1, g_top, full_top, stored1, weights[1], ffns, place, source_lengths, norms[1],
        {
            "ffn": full_top[1:],
            "sum3": [unit],
            "middle": middle_second,
            "late": lambda: (),
        },
    )
    grads_a = reduce_dp(grads_a)

    tail = {}

    def join(ffn_parts, g2):
        tail["joined"], done = call(
            join_kernel,
            cold(struct((8, 192, 1024), BF16)),
            [*ffn_parts, *self1],
            after=[g2],
            token=True,
        )
        return [done]

    def middle_first(ffn_parts, cross_grads, keys, after):
        chunks_of = call(
            cross_chunk_kernel,
            chunk_shapes(128),
            cross_grads,
            scalars=[place],
            scratch=[pltpu.VMEM((1024, 1024), F32)],
            after=[after],
        )
        arrived = [shift(c, "dy", -k) for k, c in enumerate(chunks_of[1:], 1)]
        return [*cold(chunks_of[0]), *arrived, *keys], [chunks_of[1]]

    def late_first(cross_parts, self_parts, theirs):
        *tail["chunks"], tail["cross"] = call(
            rest_chunk_kernel,
            chunk_shapes(96) + cold(struct((2, 32, 1024), F32)),
            [*self_parts, *cross_parts, *cold(memory)],
            scalars=[place],
            scratch=[pltpu.VMEM((768, 1024), F32)],
        )
        return [tail["chunks"][1]]

    input_grad, _, _, norms = layer_back(
        0, text_grad, gather_x(text_grad), stored0, weights[0], ffns, place, source_lengths, norms[0],
        {
            "cross": join,
            "middle": middle_first,
            "late": late_first,
            "norms": norms1,
            "tail": tail,
        },
    )
    grads_b = reduce_dp(tail["joined"])
    ffn1, cross1 = call(
        split_kernel,
        cold(row16, struct((256, 1024), BF16)),
        cold(grads_a),
        after=[tail["near"]],
    )
    cross1 = lax.psum_scatter(cross1, "tx", scatter_dimension=0, tiled=True)
    chunks_of = tail["chunks"]
    arrived = [shift(c, "dy", -k) for k, c in enumerate(chunks_of[1:], 1)]
    two = struct((256, 1024), F32)
    keep, over_z, over_s = call(
        sum_y_kernel,
        [Cold(two), row16, struct((256, 1024), BF16)],
        [*cold(chunks_of[0]), *arrived, *cold(tail["cross"], grads_b, ffn1, cross1)],
        scalars=[place],
        after=[tail["near"]], lazy=False)
    last = call(
        sum_rest_kernel,
        cold(struct((272, 1024), BF16)),
        [*cold(keep), *exchange(over_z, over_s), norms, swap(norms, "core")],
        scalars=[place],
    )[0]
    whole = lax.all_gather(last, ("dz", "dy"), axis=0, tiled=True)
    rows = cold(text, unit, input_grad, text_grad)
    lacks = call(
        other_layer_kernel, [struct((256, 1024), BF16)], rows, scalars=[place], after=[last], lazy=False)[0]
    lacks = swap(lacks, "section")
    eight, pair32 = struct((8, 1024), F32), struct((2, 1024), F32)
    own, over_s = call(
        norms_kernel, [eight] * 2, cold(whole), scalars=[place]
    )
    grad_out, grad_self, grad_cq, grad_co, grad_ckv, grad_up, grad_down, done = call(
        last_kernel,
        cold(
            struct((128, 1024), F32),
            struct((3, 1024, 128), F32),
            struct((1024, 128), F32),
            struct((128, 1024), F32),
            struct((2048, 128), F32),
            struct((1024, 512), F32),
            struct((512, 1024), F32),
        ),
        cold(whole),
        after=[own],
        token=True,
    )
    both = struct((2, BLOCK, 1024), BF16)
    states, input_grads = call(
        both_batches_kernel, cold(both, both), [*rows, lacks], scalars=[place], after=[done], lazy=False)
    grad_gain, grad_bias, grad_ffn = call(
        last_norms_kernel, [pair32] * 3, [own, swap(over_s, "section")], after=[done]
    )
    return (
        states[None, :, :, None],
        input_grads[None, :, :, None],
        grad_gain[None],
        grad_bias[None],
        grad_ffn[None],
        grad_self.transpose(1, 0, 2)[None],
        grad_out[None],
        grad_cq[None],
        grad_ckv.reshape(1, 1024, 2, 128),
        grad_co[None],
        grad_up[None],
        grad_down[None],
    )


def solution(mesh):
    sections = mesh.devices.shape[0]
    fine = Mesh(
        mesh.devices.reshape(sections, 2, RING, RING, 2), ("section", "dz", "dy", "tx", "core")
    )
    dp, tensor = ("dz", "dy"), ("tx", "core")
    rows = P(None, tensor, dp, None)
    return jax.shard_map(
        shards,
        mesh=fine,
        in_specs=(
            rows,
            rows,
            P(None, dp),
            rows,
            P("section", None, None),
            P("section", None, None),
            P("section", None, None, tensor),
            P("section", tensor, None),
            P("section", None, tensor),
            P("section", None, None, tensor),
            P("section", tensor, None),
            P("section", None, tensor),
            P("section", tensor, None),
        ),
        out_specs=(
            P("section", None, tensor, dp, None),
            P("section", None, tensor, dp, None),
            P("section", None, None),
            P("section", None, None),
            P("section", None, None),
            P("section", None, None, tensor),
            P("section", tensor, None),
            P("section", None, tensor),
            P("section", None, None, tensor),
            P("section", tensor, None),
            P("section", None, tensor),
            P("section", tensor, None),
        ),
        check_vma=False,
    )
```

```python
import functools
import math

import jax
import jax.numpy as jnp
from jax import lax
from jax.experimental import pallas as pl
from jax.experimental.pallas import tpu as pltpu
from jax.sharding import Mesh, PartitionSpec as P

HD = 64
EPSILON = 1e-05
NEG_FILL = -1000000000.0
BLOCK = 128
RING = 4
BF16 = jnp.bfloat16
F32 = jnp.float32


def shift(value, axis, steps):
    count = lax.axis_size(axis)
    return lax.ppermute(value, axis, [(i, (i + steps) % count) for i in range(count)])


def swap(value, axis):
    return shift(value, axis, 1)


def dot(a, b, dims):
    return lax.dot_general(a, b, ((dims[0], dims[1]), ((), ())), preferred_element_type=F32)


def mm(a, b):
    return dot(a, b, ((1,), (0,)))


def mm_nt(a, b):
    return dot(a, b, ((1,), (1,)))


def mm_tn(a, b):
    return dot(a, b, ((0,), (0,)))


def gather_x(value):
    return [value] + [shift(value, "tx", k) for k in range(1, RING)]


def send_x(others):
    return [shift(block, "tx", -k) for k, block in enumerate(others, 1)]


SMEM = pl.BlockSpec(memory_space=pltpu.SMEM)
VMEM = pl.BlockSpec(memory_space=pltpu.VMEM)
ANY = pl.BlockSpec(memory_space=pl.ANY)
HBM = pl.BlockSpec(memory_space=pltpu.HBM)
CHUNK = 256


def struct(shape, dtype):
    return jax.ShapeDtypeStruct(shape, dtype)


class Cold:
    def __init__(self, array):
        self.array = array


class Awaited:
    def __init__(self, buffer, move):
        self.buffer, self.move = buffer, move
        self.shape, self.dtype = buffer.shape, buffer.dtype

    def arrived(self):
        if self.move is not None:
            self.move.wait()
            self.move = None
        return self.buffer

    def __getitem__(self, key):
        return self.arrived()[key]


def cold(*arrays):
    return [Cold(array) for array in arrays]


def cold_if(flag, *arrays):
    return cold(*arrays) if flag else list(arrays)


def vmem(o):
    return pltpu.VMEM(o.shape, o.dtype)


class Place:
    axes = ("tx", "core", "dy", "dz", "section")

    def __getitem__(self, at):
        return lax.axis_index(self.axes[at])


PLACE = Place()


def settled(array):
    return pltpu.with_memory_space_constraint(array, pltpu.HBM)


def call(kernel, outs, operands, scalars=(), scratch=(), after=(), room=8, token=False, lazy=True):
    ins = [o if isinstance(o, Cold) else None for o in operands]
    arrays = [o.array if isinstance(o, Cold) else o for o in operands]
    puts = [o if isinstance(o, Cold) else None for o in outs]
    shapes = [o.array if isinstance(o, Cold) else o for o in outs]
    if token:
        puts.append(None)
        shapes.append(struct((8, 128), F32))
    placed = any(o is PLACE for o in scalars)
    scalars = [o for o in scalars if o is not PLACE]
    first, waits = len(scalars), len(after)
    last = first + len(arrays)
    brought = [vmem(o.array) for o in ins if o]
    taken = [vmem(o.array) for o in puts if o]
    held = sum(math.prod(o.shape) * o.dtype.itemsize for o in (*scratch, *brought, *taken))
    name = kernel.func.__name__ if isinstance(kernel, functools.partial) else kernel.__name__

    def body(*refs):
        given = list(refs[first:last])
        results = list(refs[last + waits : last + waits + len(shapes)])
        rest = list(refs[last + waits + len(shapes) :])
        semaphores = rest.pop() if brought or taken else None
        buffers = rest[len(scratch) :]
        moves, stores = [], []
        for at, o in enumerate(ins):
            if o:
                buffer = buffers[len(moves)]
                moves.append(
                    pltpu.make_async_copy(given[at], buffer, semaphores.at[len(moves)])
                )
                moves[-1].start()
                given[at] = buffer
        for at, o in enumerate(puts):
            if o:
                n = len(moves) + len(stores)
                stores.append(pltpu.make_async_copy(buffers[n], results[at], semaphores.at[n]))
                results[at] = buffers[n]
        for at, o in enumerate(ins):
            if o and lazy:
                given[at] = Awaited(given[at], moves[sum(1 for p in ins[:at] if p)])
        for move in () if lazy else moves:
            move.wait()
        if token:
            results.pop()[...] = jnp.zeros((8, 128), F32)
        lead = [PLACE] if placed else []
        kernel(*lead, *refs[:first], *given, *results, *rest[: len(scratch)])
        for ref in given:
            if isinstance(ref, Awaited):
                ref.arrived()
        for store in stores:
            store.start()
        for store in stores:
            store.wait()

    kept = [*scratch, *brought, *taken]
    if brought or taken:
        kept.append(pltpu.SemaphoreType.DMA((len(brought) + len(taken),)))
    return pl.pallas_call(
        body,
        name=name,
        out_shape=[pltpu.HBM(o.shape, o.dtype) if c else o for o, c in zip(shapes, puts)],
        in_specs=[SMEM] * first + [HBM if o else VMEM for o in ins] + [ANY] * waits,
        out_specs=[HBM if o else VMEM for o in puts],
        scratch_shapes=kept,
        compiler_params=pltpu.CompilerParams(vmem_limit_bytes=held + room * 1024 * 1024),
    )(*scalars, *(settled(a) if c else a for a, c in zip(arrays, ins)), *after)


ROW = struct((BLOCK, 1024), F32)
ROW16 = struct((BLOCK, 1024), BF16)
COLUMN = struct((BLOCK, 1), F32)
SENT = [ROW] + [ROW16] * (RING - 1)


def stack_rows(refs, cols=slice(None)):
    return jnp.concatenate([ref[:, cols] for ref in refs], axis=0)


def split_rows(total, outs, cols):
    outs[0][:, cols] = total[0:BLOCK]
    for k in range(1, len(outs)):
        outs[k][:, cols] = total[BLOCK * k : BLOCK * (k + 1)].astype(BF16)


def chunks(width=1024):
    return [slice(at, at + CHUNK) for at in range(0, width, CHUNK)]


def norm(v, gain, bias, a_ref, s_ref, r_ref):
    average = jnp.mean(v, axis=-1, keepdims=True)
    centred = v - average
    inv = lax.rsqrt(jnp.mean(centred * centred, axis=-1, keepdims=True) + EPSILON)
    standard = centred * inv
    s_ref[...] = standard
    r_ref[...] = inv
    a_ref[...] = (standard * gain + bias).astype(BF16)


def total_of(v_ref, near, far):
    total = v_ref[...].astype(F32) + near[...]
    for ref in far:
        total = total + ref[...].astype(F32)
    return total


def sum_norm_kernel(j, count, v_ref, near, *refs):
    far, (rows, v_out, a_ref, s_ref, r_ref) = refs[:count], refs[count:]
    v = total_of(v_ref, near, far)
    v_out[...] = v.astype(v_out.dtype)
    v = v_out[...].astype(F32)
    norm(v, rows[j : j + 1], rows[3 + j : 4 + j], a_ref, s_ref, r_ref)


def sum_norm(j, v, near, far, rows, kept, after=(), old=False, new=False):
    outs = [*cold_if(new, kept), ROW16, *cold_if(new, ROW, COLUMN)]
    return call(
        functools.partial(sum_norm_kernel, j, len(far)),
        outs,
        [*cold_if(old, v), near, *far, rows],
        after=after,
    )


def sum_last_kernel(v_ref, near, r1, r2, r3, v_out):
    v_out[...] = total_of(v_ref, near, (r1, r2, r3)).astype(BF16)


def sum_back_kernel(j, count, dv_ref, near, *refs):
    far, (s_ref, r_ref, rows, dv_out, g_out, norms) = refs[:count], refs[count:]
    da = near[...]
    for ref in far:
        da = da + ref[...].astype(F32)
    standard = s_ref[...]
    scaled = da * rows[j : j + 1]
    inner = (
        scaled
        - jnp.mean(scaled, axis=-1, keepdims=True)
        - standard * jnp.mean(scaled * standard, axis=-1, keepdims=True)
    )
    dv = dv_ref[...].astype(F32) + inner * r_ref[...]
    dv_out[...] = dv
    g_out[...] = dv.astype(BF16)
    norms[0:1] = jnp.sum(da * standard, axis=0, keepdims=True)
    norms[1:2] = jnp.sum(da, axis=0, keepdims=True)


def sum_back(j, dv, near, far, s, r, rows, after=(), old=False, new=False):
    return call(
        functools.partial(sum_back_kernel, j, len(far)),
        [*cold_if(new, ROW), ROW16, *cold_if(new, struct((2, 1024), F32))],
        [*cold_if(old, dv), near, *far, *cold_if(old, s, r, rows)],
        after=after,
    )


KEYS = 2 * RING * BLOCK


def block_of(place, b):
    return lax.rem(place[0] - b + RING, RING)


def lay_out_keys(place, own_ref, other_ref, kbuf, vbuf):
    core = place[1]
    for b in range(RING):
        j = block_of(place, b)
        own_at = pl.ds(pl.multiple_of((2 * b + core) * BLOCK, BLOCK), BLOCK)
        other_at = pl.ds(pl.multiple_of((2 * b + 1 - core) * BLOCK, BLOCK), BLOCK)
        for pair in range(2):
            here = slice(pair * 128, pair * 128 + 128)
            kbuf[own_at, here] = own_ref[j, :, 256 * pair : 256 * pair + 128]
            vbuf[own_at, here] = own_ref[j, :, 256 * pair + 128 : 256 * pair + 256]
            theirs = 1 - pair
            kbuf[other_at, here] = other_ref[j, :, 256 * theirs : 256 * theirs + 128]
            vbuf[other_at, here] = other_ref[j, :, 256 * theirs + 128 : 256 * theirs + 256]


def causal_tail(scores, core):
    key_at = lax.broadcasted_iota(jnp.int32, scores.shape, 0)
    query_at = lax.broadcasted_iota(jnp.int32, scores.shape, 1) + core * BLOCK
    return jnp.where(key_at <= query_at, scores, NEG_FILL)


class Tall:
    def __init__(self, *halves):
        self.halves = halves

    def __getitem__(self, key):
        rows, cols = key
        if rows.start is None:
            return jnp.concatenate([half[:, cols] for half in self.halves], axis=0)
        return self.halves[rows.start // 512][rows.start % 512 : rows.stop - 512 * (rows.start // 512), cols]


def qkv_rows(rows, own, far, q_ref, kv_ref):
    weights = (
        jnp.concatenate([own[:, 0:128], far[:, 0:128]], axis=1),
        own[:, 128:384],
        far[:, 128:384],
    )
    for n, weight in enumerate(weights):
        out = mm(rows, weight).astype(BF16)
        for k in range(RING):
            block = out[BLOCK * k : BLOCK * (k + 1)]
            if n == 0:
                q_ref[k] = block
            else:
                kv_ref[k, :, 256 * n - 256 : 256 * n] = block


def qkv_kernel(a0, a1, a2, a3, own0, own1, far0, far1, q_ref, kv_ref):
    own, far = Tall(own0, own1), Tall(far0, far1)
    qkv_rows(stack_rows((a0, a1, a2, a3)), own, far, q_ref, kv_ref)


def first_qkv_kernel(
    x0, x1, x2, x3, own0, own1, far0, far1, norms, q_ref, kv_ref, *refs
):
    outs, (s_ref, r_ref, all_ref) = refs[0:4], refs[4:7]
    own, far = Tall(own0, own1), Tall(far0, far1)
    for k, x_ref in enumerate((x0, x1, x2, x3)):
        x = x_ref[0:BLOCK].astype(F32)
        centred = x - jnp.mean(x, axis=-1, keepdims=True)
        inv = lax.rsqrt(jnp.mean(centred * centred, axis=-1, keepdims=True) + EPSILON)
        standard = centred * inv
        if k == 0:
            s_ref[...] = standard
            r_ref[...] = inv
        all_ref[BLOCK * k : BLOCK * (k + 1)] = standard.astype(BF16)
        outs[k][...] = (standard * norms[0:1] + norms[3:4]).astype(BF16)
    qkv_rows(stack_rows(outs), own, far, q_ref, kv_ref)


def lane_blocks(ref, at, cols):
    return jnp.concatenate(
        [ref[c : c + 128, at : at + 128] for c in range(cols.start, cols.stop, 128)], axis=1
    )


ALL_COLS = slice(0, 1024)


def self_forward_kernel(
    place, q_ref, own_ref, other_ref, w0, w1, w2, w3, o_ref, lse_ref, near, f1, f2, f3, kbuf, vbuf
):
    lay_out_keys(place, own_ref, other_ref, kbuf, vbuf)
    core = place[1]
    for b in range(RING):
        j = block_of(place, b)
        span = 2 * BLOCK * (b + 1)
        head = span - 2 * BLOCK
        for pair in range(2):
            outs = []
            for h in (2 * pair, 2 * pair + 1):
                cols = slice(HD * h, HD * h + HD)
                q = q_ref[j, :, cols] * 0.125
                last = causal_tail(mm_nt(kbuf[head:span, cols], q), core)
                top = jnp.max(last, axis=0, keepdims=True)
                if head:
                    early = mm_nt(kbuf[0:head, cols], q)
                    top = jnp.maximum(top, jnp.max(early, axis=0, keepdims=True))
                    early = jnp.exp(early - top)
                last = jnp.exp(last - top)
                total = jnp.sum(last, axis=0, keepdims=True)
                mixed = mm_tn(vbuf[head:span, cols], last.astype(BF16))
                if head:
                    total = total + jnp.sum(early, axis=0, keepdims=True)
                    mixed = mixed + mm_tn(vbuf[0:head, cols], early.astype(BF16))
                outs.append(mixed / total)
                lse_ref[h, j] = top + jnp.log(total)
            both = jnp.concatenate(outs, axis=0)
            o_ref[j, :, 128 * pair : 128 * pair + 128] = both.T.astype(BF16)
    rows = jnp.concatenate([o_ref[k] for k in range(RING)], axis=0)
    for cols in chunks():
        weight = jnp.concatenate([lane_blocks(w, 384, cols) for w in (Tall(w0, w1), Tall(w2, w3))], axis=0)
        split_rows(mm(rows, weight), (near, f1, f2, f3), cols)


def self_back_kernel(
    place, g0, g1, g2, g3, w0, w1, w2, w3, q_ref, own_ref, other_ref, lse_ref,
    dq_ref, down_ref, dother_ref, kbuf, vbuf, dobuf, dk, dv,
):
    rows = stack_rows((g0, g1, g2, g3))
    weight = jnp.concatenate([lane_blocks(w, 384, ALL_COLS) for w in (Tall(w0, w1), Tall(w2, w3))], axis=0)
    dobuf[...] = mm_nt(rows, weight).astype(BF16).reshape(dobuf.shape)
    lay_out_keys(place, own_ref, other_ref, kbuf, vbuf)
    core = place[1]
    for b in reversed(range(RING)):
        j = block_of(place, b)
        span = 2 * BLOCK * (b + 1)
        head = span - 2 * BLOCK
        for pair in range(2):
            lanes = slice(128 * pair, 128 * pair + 128)
            dqs, dks, dvs = [], [], []
            for h in (2 * pair, 2 * pair + 1):
                cols = slice(HD * h, HD * h + HD)
                q = q_ref[j, :, cols] * 0.125
                do = dobuf[j, :, cols]
                k = kbuf[0:span, cols]
                scores = mm_nt(k, q)
                last = causal_tail(scores[head:span], core)
                scores = jnp.concatenate([scores[0:head], last], axis=0) if head else last
                probs = jnp.exp(scores - lse_ref[h, j])
                dprobs = mm_nt(vbuf[0:span, cols], do)
                delta = jnp.sum(probs * dprobs, axis=0, keepdims=True)
                dscores = (probs * (dprobs - delta)).astype(BF16)
                dqs.append(mm_tn(k, dscores) * 0.125)
                dks.append(mm(dscores, q))
                dvs.append(mm(probs.astype(BF16), do))
            dq_ref[j, :, lanes] = jnp.concatenate(dqs, axis=0).T.astype(BF16)
            dk_new = jnp.concatenate(dks, axis=1)
            dv_new = jnp.concatenate(dvs, axis=1)
            if b == RING - 1:
                dk[0:span, lanes] = dk_new
                dv[0:span, lanes] = dv_new
            else:
                dk[0:span, lanes] += dk_new
                dv[0:span, lanes] += dv_new
    for b in range(RING):
        j = block_of(place, b)
        own_at = pl.ds(pl.multiple_of((2 * b + core) * BLOCK, BLOCK), BLOCK)
        other_at = pl.ds(pl.multiple_of((2 * b + 1 - core) * BLOCK, BLOCK), BLOCK)
        for pair in range(2):
            here = slice(pair * 128, pair * 128 + 128)
            theirs = 1 - pair
            down_ref[j, :, 256 * pair : 256 * pair + 128] = dk[own_at, here]
            down_ref[j, :, 256 * pair + 128 : 256 * pair + 256] = dv[own_at, here]
            dother_ref[j, :, 256 * theirs : 256 * theirs + 128] = dk[other_at, here].astype(BF16)
            dother_ref[j, :, 256 * theirs + 128 : 256 * theirs + 256] = dv[other_at, here].astype(BF16)


def keys_total(down_ref, dother_ref):
    total = [down_ref[k] + dother_ref[k].astype(F32) for k in range(RING)]
    return jnp.concatenate(total, axis=0).astype(BF16)


def self_rows_back_kernel(
    dq_ref, down_ref, dother_ref, own0, own1, far0, far1, near, f1, f2, f3
):
    own, far = Tall(own0, own1), Tall(far0, far1)
    dq = jnp.concatenate([dq_ref[k] for k in range(RING)], axis=0)
    rows = jnp.concatenate([dq, keys_total(down_ref, dother_ref)], axis=1)
    for cols in chunks():
        weight = jnp.concatenate(
            [own[cols, 0:128], far[cols, 0:128], own[cols, 128:384], far[cols, 128:384]], axis=1
        )
        split_rows(mm_nt(rows, weight), (near, f1, f2, f3), cols)


def last_rows_back_kernel(
    dq_ref, down_ref, dother_ref, own0, own1, far0, far1, all_ref, n0, n1, n2, n3, n4,
    near, f1, f2, f3, norms,
):
    own, far = Tall(own0, own1), Tall(far0, far1)
    dq = jnp.concatenate([dq_ref[k] for k in range(RING)], axis=0)
    rows = jnp.concatenate([dq, keys_total(down_ref, dother_ref)], axis=1)
    for n, ref in enumerate((n0, n1, n2, n3, n4), 1):
        norms[2 * n : 2 * n + 2] = ref[...]
    norms[12:16] = jnp.zeros((4, 1024), F32)
    for cols in chunks():
        weight = jnp.concatenate(
            [own[cols, 0:128], far[cols, 0:128], own[cols, 128:384], far[cols, 128:384]], axis=1
        )
        total = mm_nt(rows, weight)
        near[:, cols] = total[0:BLOCK]
        for k, out in enumerate((f1, f2, f3), 1):
            out[0:BLOCK, cols] = total[BLOCK * k : BLOCK * (k + 1)].astype(BF16)
        norms[0:1, cols] = jnp.sum(total * all_ref[:, cols].astype(F32), axis=0, keepdims=True)
        norms[1:2, cols] = jnp.sum(total, axis=0, keepdims=True)
    for out in (f1, f2, f3):
        out[BLOCK : BLOCK + 16] = norms[...].astype(BF16)


def last_sum_back_kernel(dv_ref, near, r1, r2, r3, s_ref, r_ref, rows, norms, g_out, total):
    da = near[...]
    for ref in (r1, r2, r3):
        da = da + ref[0:BLOCK].astype(F32)
    standard = s_ref[...]
    scaled = da * rows[0:1]
    inner = (
        scaled
        - jnp.mean(scaled, axis=-1, keepdims=True)
        - standard * jnp.mean(scaled * standard, axis=-1, keepdims=True)
    )
    g_out[...] = (dv_ref[...].astype(F32) + inner * r_ref[...]).astype(BF16)
    total[...] = norms[...] + sum(ref[BLOCK : BLOCK + 16].astype(F32) for ref in (r1, r2, r3))


def cross_cols(w, layer, place, g, at, rows):
    first = RING * block_of(place, g)
    parts = [
        w[2 * (first + y) + layer, :, at : at + 128]
        for y in range(rows.start // 256, rows.stop // 256)
    ]
    return parts[0] if len(parts) == 1 else jnp.concatenate(parts, axis=0)


def cross_blocks(w, layer, place, g, cols):
    first = RING * block_of(place, g)
    parts = []
    for c in range(cols.start, cols.stop, 128):
        at = c % 256
        parts.append(w[2 * (first + c // 256) + layer, at : at + 128, 128:256])
    return jnp.concatenate(parts, axis=1)


def cross_mask(scores, length):
    slots = lax.broadcasted_iota(jnp.int32, scores.shape, 0)
    return jnp.where(slots < length, scores, NEG_FILL)


def cross_forward_kernel(layer, place, lengths, mine, theirs, *refs):
    w, kv, (q_ref, o_ref, lse_ref, near, far) = refs[0], refs[1:5], refs[5:]
    rows = stack_rows((mine, theirs))
    for g in range(RING):
        lanes = slice(128 * g, 128 * g + 128)
        q_ref[:, lanes] = mm(rows, cross_cols(w, layer, place, g, 0, slice(0, 1024))).astype(BF16)
        outs = []
        for p in range(2):
            h = 2 * g + p
            q = q_ref[:, HD * h : HD * h + HD] * 0.125
            k = kv[g][layer, :, HD * p : HD * p + HD]
            v = kv[g][layer, :, 128 + HD * p : 128 + HD * p + HD]
            scores = cross_mask(mm_nt(k, q), lengths[place[4], 0])
            top = jnp.max(scores, axis=0, keepdims=True)
            raised = jnp.exp(scores - top)
            total = jnp.sum(raised, axis=0, keepdims=True)
            outs.append(mm_tn(v, raised.astype(BF16)) / total)
            lse_ref[h] = top + jnp.log(total)
        o_ref[:, lanes] = jnp.concatenate(outs, axis=0).T.astype(BF16)
    for cols in chunks():
        weight = jnp.concatenate([cross_blocks(w, layer, place, g, cols) for g in range(RING)], axis=0)
        split_rows(mm(o_ref[...], weight), (near, far), cols)


def cross_back_kernel(layer, place, lengths, mine, theirs, *refs):
    w, kv, (q_ref, lse_ref) = refs[0], refs[1:5], refs[5:7]
    dq_ref, dkv, (near, far) = refs[7], refs[8:12], refs[12:14]
    rows = stack_rows((mine, theirs))
    for g in range(RING):
        lanes = slice(128 * g, 128 * g + 128)
        dmixed = mm_nt(rows, cross_blocks(w, layer, place, g, ALL_COLS)).astype(BF16)
        dqs, dks, dvs = [], [], []
        for p in range(2):
            h = 2 * g + p
            q = q_ref[:, HD * h : HD * h + HD] * 0.125
            do = dmixed[:, HD * p : HD * p + HD]
            k = kv[g][layer, :, HD * p : HD * p + HD]
            v = kv[g][layer, :, 128 + HD * p : 128 + HD * p + HD]
            probs = jnp.exp(cross_mask(mm_nt(k, q), lengths[place[4], 0]) - lse_ref[h])
            dprobs = mm_nt(v, do)
            delta = jnp.sum(probs * dprobs, axis=0, keepdims=True)
            dscores = (probs * (dprobs - delta)).astype(BF16)
            dqs.append(mm_tn(k, dscores) * 0.125)
            dks.append(mm(dscores, q))
            dvs.append(mm(probs.astype(BF16), do))
        dq_ref[:, lanes] = jnp.concatenate(dqs, axis=0).T.astype(BF16)
        dkv[g][...] = jnp.concatenate(dks + dvs, axis=1).astype(BF16)
    for cols in chunks():
        weight = jnp.concatenate([cross_cols(w, layer, place, g, 0, cols) for g in range(RING)], axis=1)
        split_rows(mm_nt(dq_ref[...], weight), (near, far), cols)


def up_cols(own, far, at):
    refs, at = (own, at) if at < 512 else (far, at - 512)
    return jnp.concatenate([ref[:, at : at + CHUNK] for ref in refs], axis=0)


def up_rows(own, far, cols):
    half, rows = cols.start // 512, slice(cols.start % 512, cols.start % 512 + CHUNK)
    return jnp.concatenate([own[half][rows, 0:512], far[half][rows, 0:512]], axis=1)


def down_rows(own, far, at):
    refs, at = (own, at) if at < 512 else (far, at - 512)
    return jnp.concatenate([ref[at : at + CHUNK, 512:1024] for ref in refs], axis=1)


def down_cols(own, far, at):
    half, lanes = at // 512, slice(512 + at % 512, 512 + at % 512 + CHUNK)
    return jnp.concatenate([own[half][:, lanes], far[half][:, lanes]], axis=0)


def ffn_forward_kernel(
    a0, a1, a2, a3, own0, own1, far0, far1, hidden_ref, slope_ref, near, f1, f2, f3
):
    own, far = (own0, own1), (far0, far1)
    root = 0.7978845608028654
    rows = stack_rows((a0, a1, a2, a3))
    for cols in chunks():
        pre = mm(rows, up_cols(own, far, cols.start))
        square = pre * pre
        t = jnp.tanh(root * (pre + 0.044715 * pre * square))
        half = 0.5 * (1.0 + t)
        hidden_ref[:, cols] = (pre * half).astype(BF16)
        slope_ref[:, cols] = half + 0.5 * pre * (1.0 - t * t) * (root * (1.0 + 3 * 0.044715 * square))
    for cols in chunks():
        split_rows(mm(hidden_ref[...], down_cols(own, far, cols.start)), (near, f1, f2, f3), cols)


def ffn_back_kernel(
    g0, g1, g2, g3, own0, own1, far0, far1, slope_ref, dpre_ref, near, f1, f2, f3
):
    own, far = (own0, own1), (far0, far1)
    rows = stack_rows((g0, g1, g2, g3))
    for cols in chunks():
        dhidden = mm_nt(rows, down_rows(own, far, cols.start))
        dpre_ref[:, cols] = (dhidden * slope_ref[:, cols]).astype(BF16)
    for cols in chunks():
        split_rows(mm_nt(dpre_ref[...], up_rows(own, far, cols)), (near, f1, f2, f3), cols)


def ffn_grads_kernel(hidden, g0, g1, g2, g3, dpre, a0, a1, a2, a3, ours, t0, t1, t2, t3):
    theirs = (t0, t1, t2, t3)
    g = stack_rows((g0, g1, g2, g3))
    a = stack_rows((a0, a1, a2, a3))
    for n in (2, 3, 0, 1):
        down = mm_tn(hidden[:, CHUNK * n : CHUNK * n + CHUNK], g)
        if n >= 2:
            theirs[n - 2][...] = down.astype(BF16)
        else:
            ours[CHUNK * n : CHUNK * n + CHUNK] = down
    for half in (1, 0):
        for n in range(4):
            up = mm_tn(a[:, CHUNK * n : CHUNK * n + CHUNK], dpre[:, 512 * half : 512 * half + 512])
            lanes = slice(512 * (n // 2), 512 * (n // 2) + 512)
            if half:
                theirs[2 + n % 2][:, lanes] = up.astype(BF16)
            else:
                ours[512 + CHUNK * (n % 2) : 512 + CHUNK * (n % 2) + CHUNK, lanes] = up


def ffn_total(ours, came, rows):
    n, at = rows.start // CHUNK, rows.start % CHUNK
    return ours[rows] + came[n][at : at + rows.stop - rows.start].astype(F32)


def cross_shares(k, g, a, mixed, dq, keys, memory):
    lanes = slice(128 * k, 128 * k + 128)
    return mm_tn(dq[:, lanes], a), mm_tn(mixed[:, lanes], g), mm_tn(keys[...], memory)


def cross_chunk_kernel(place, mixed, g_mine, g_theirs, dq, a_mine, a_theirs, c0, c1, c2, c3, total):
    g = stack_rows((g_mine, g_theirs))
    a = stack_rows((a_mine, a_theirs))
    for k in range(RING):
        lanes = slice(128 * k, 128 * k + 128)
        parts = (mm_tn(dq[:, lanes], a), mm_tn(mixed[:, lanes], g))
        for i in range(8):
            at = 32 * (i % 4)
            total[128 * i + 32 * k : 128 * i + 32 * k + 32] = parts[i // 4][at : at + 32]
    cut_chunks(place, total, (c0, c1, c2, c3))


def cross_sum_kernel(c0, r1, r2, r3, k0, k1, k2, k3, *outs):
    sums = [c0[z] + sum(r[z].astype(F32) for r in (r1, r2, r3)) for z in range(2)]
    for k, (key, out) in enumerate(zip((k0, k1, k2, k3), outs)):
        for z in range(2):
            out[32 * z : 32 * z + 32] = sums[z][32 * k : 32 * k + 32].astype(out.dtype)
        for i in range(4):
            out[64:128, 256 * i : 256 * i + 256] = key[64 * i : 64 * i + 64].astype(out.dtype)


def cross_first_kernel(
    place, ours, q0, q1, q2, q3, mixed, g_mine, g_theirs, dq, a_mine, a_theirs, k0, k1, k2, k3,
    memory, out,
):
    g = stack_rows((g_mine, g_theirs))
    a = stack_rows((a_mine, a_theirs))
    for i in range(8):
        rows = slice(128 * i, 128 * i + 128)
        out[i, 0:128] = ffn_total(ours, (q0, q1, q2, q3), rows).astype(BF16)
    for k, key in enumerate((k0, k1, k2, k3)):
        queries, outs, keys = cross_shares(k, g, a, mixed, dq, key, memory[...])
        for i in range(8):
            part, at = (queries, outs)[i // 4], 32 * (i % 4)
            to = pl.multiple_of(128 + 64 * block_of(place, k), 64)
            out[i, pl.ds(to, 32)] = part[at : at + 32].astype(BF16)
            out[i, pl.ds(pl.multiple_of(to + 32, 32), 32)] = keys[32 * i : 32 * i + 32].astype(BF16)


def self_grads_kernel(
    mixed, g0, g1, g2, g3, dq, down_ref, dother_ref, a0, a1, a2, a3, ours, t0, t1
):
    g = stack_rows((g0, g1, g2, g3))
    a = stack_rows((a0, a1, a2, a3))
    keys = keys_total(down_ref, dother_ref)
    outs, queries = [jnp.concatenate([r[k] for k in range(RING)], axis=0) for r in (mixed, dq)]
    t0[0:128] = mm_tn(outs[:, 128:256], g).astype(BF16)
    t0[128:256] = mm_tn(queries[:, 128:256], a).astype(BF16)
    t1[...] = mm_tn(keys[:, 256:512], a).astype(BF16)
    ours[0:128] = mm_tn(outs[:, 0:128], g)
    ours[128:256] = mm_tn(queries[:, 0:128], a)
    ours[256:512] = mm_tn(keys[:, 0:256], a)


def rows_kernel(place, x_ref, memory_ref, g_ref, x, both, g):
    mine = place[4]
    x[...] = x_ref[mine]
    both[0:BLOCK] = x_ref[mine]
    both[BLOCK : BLOCK + 32] = memory_ref[mine]
    g[...] = g_ref[mine]


def norm_rows_kernel(gain, bias, out):
    out[0:3] = gain[0]
    out[3:6] = bias[0]


def both_norms_kernel(place, mine, other, first, second):
    first[...] = jnp.where(place[4] == 0, mine[...], other[...])
    second[...] = jnp.where(place[4] == 0, other[...], mine[...])


def memory_blocks_kernel(x0, x1, x2, x3, out):
    for k, ref in enumerate((x0, x1, x2, x3)):
        out[32 * k : 32 * k + 32] = ref[BLOCK : BLOCK + 32]


def pack_kernel(place, w_ref, out_ref, q_ref, cross_ref, kv_ref, first, second, part, whole):
    for i in range(3):
        whole[:, 128 * i : 128 * i + 128] = w_ref[i]
    for i in range(8):
        rows = slice(128 * i, 128 * i + 128)
        whole[rows, 384:512] = out_ref[:, rows]
        whole[rows, 640:768] = cross_ref[:, rows]
    whole[:, 512:640] = q_ref[...]
    whole[:, 768:1024] = kv_ref[...]
    first[...] = whole[0:512, 0:512]
    second[...] = whole[512:1024, 0:512]
    part[...] = whole[pl.ds(pl.multiple_of(place[2] * 256, 256), 256)]


def pack_ffn_kernel(up_ref, down_ref, out):
    out[:, 0:512] = up_ref[...]
    out[0:512, 512:1024] = down_ref[:, 0:512]
    out[512:1024, 512:1024] = down_ref[:, 512:1024]


def quarter(place, k):
    return pl.ds(pl.multiple_of(lax.rem(place[2] - k + RING, RING) * 256, 256), 256)


def by_section(place, write):
    pl.when(place[4] == 0)(lambda: write(0, 1))
    pl.when(place[4] == 1)(lambda: write(1, 0))


def fill_halves(place, parts, halves, cols):
    for k, ref in enumerate(parts):
        y = lax.rem(place[2] - k + RING, RING)
        rows = pl.ds(pl.multiple_of(lax.rem(y, 2) * 256, 256), 256)

        def put(half, ref=ref, rows=rows):
            halves[half][rows] = ref[:, cols]

        pl.when(y < 2)(functools.partial(put, 0))
        pl.when(y >= 2)(functools.partial(put, 1))


def both_selfs_kernel(
    place, mine0, mine1, r0, r1, r2, r3, a0, a1, b0, b1
):
    def write(own, far):
        halves = ((a0, a1), (b0, b1))
        halves[own][0][...] = mine0[...]
        halves[own][1][...] = mine1[...]
        fill_halves(place, (r0, r1, r2, r3), halves[far], slice(0, 512))

    by_section(place, write)


def rest_kernel(place, mine, other, out, parts):
    def write(own, far):
        parts[own] = mine[:, 512:768]
        parts[far] = other[:, 512:768]

    by_section(place, write)
    out[:, 0:512] = other[:, 0:512]
    out[:, 512:768] = other[:, 768:1024]


def keys_kernel(place, kv_ref, k0, k1, k2, k3, x0, x1, x2, x3, e_far, out, memory, pair):
    for k, ref in enumerate((x0, x1, x2, x3)):
        at = 64 * block_of(place, k)
        memory[pl.ds(pl.multiple_of(at + 32 * place[1], 32), 32)] = ref[BLOCK : BLOCK + 32]
        memory[pl.ds(pl.multiple_of(at + 32 - 32 * place[1], 32), 32)] = e_far[32 * k : 32 * k + 32]
    for k, ref in enumerate((k0, k1, k2, k3)):
        pair[quarter(place, k)] = ref[:, 512:768]
    mine = mm(memory[...], kv_ref[...]).astype(BF16)
    other = mm(memory[...], pair[...]).astype(BF16)

    def write(own, far):
        out[own] = mine
        out[far] = other

    by_section(place, write)


def both_ffns_kernel(place, mine, other, a0, a1, b0, b1):
    def write(own, far):
        halves = ((a0, a1), (b0, b1))
        for half in range(2):
            rows = slice(512 * half, 512 * half + 512)
            halves[own][half][...] = mine[rows]
            halves[far][half][...] = other[rows]

    by_section(place, write)


def cut_chunks(place, total, outs):
    rows = total.shape[0] // 8
    for k, out in enumerate(outs):
        y = lax.rem(place[2] - k + RING, RING)
        for z in range(2):
            at = pl.ds(pl.multiple_of((RING * z + y) * rows, rows), rows)
            out[z] = total[at].astype(out.dtype)


def join_kernel(f, q0, q1, q2, q3, ours, t0, t1, out):
    for i in range(8):
        out[i, 0:128] = ffn_total(f, (q0, q1, q2, q3), slice(128 * i, 128 * i + 128)).astype(BF16)
        theirs = (t0, t1)[i // 4]
        at = 64 * (i % 4)
        out[i, 128:192] = (ours[64 * i : 64 * i + 64] + theirs[at : at + 64].astype(F32)).astype(BF16)


def rest_chunk_kernel(
    place, ours, t0, t1, w0, w1, w2, w3, memory, c0, c1, c2, c3, cross, total
):
    came = w0[...] + sum(w[...].astype(F32) for w in (w1, w2, w3))
    for z in range(2):
        cross[z] = came[32 * z : 32 * z + 32]
    keys = jnp.concatenate([came[64:128, 256 * i : 256 * i + 256] for i in range(4)], axis=0)
    keys = mm_tn(keys.astype(BF16), memory[...])
    for i in range(8):
        theirs = (t0, t1)[i // 4]
        at, to = 64 * (i % 4), 96 * i
        total[to : to + 64] = ours[64 * i : 64 * i + 64] + theirs[at : at + 64].astype(F32)
        total[to + 64 : to + 96] = keys[32 * i : 32 * i + 32]
    cut_chunks(place, total, (c0, c1, c2, c3))


def split_kernel(grads, ffn, cross):
    ffn[...] = grads[0:128]
    cross[...] = grads[128:384]


def chunk_shapes(rows):
    return [Cold(struct((2, rows, 1024), F32))] + [struct((2, rows, 1024), BF16)] * 3


def sum_y_kernel(place, c0, r1, r2, r3, mid, first, ffn, cross, keep, over_z, over_s):
    z = place[3]

    def half(n):
        rest = c0[n] + sum(r[n].astype(F32) for r in (r1, r2, r3))
        return jnp.concatenate([rest[0:64], mid[n], rest[64:96]], axis=0)

    over_z[...] = half(1 - z).astype(BF16)
    rest = half(z)

    def write_first():
        keep[0:128] = rest
        keep[128:256] = first[0:128].astype(F32)
        over_s[0:64] = first[128:192]
        over_s[64:128] = cross[...]
        over_s[128:256] = ffn[...]

    def write_second():
        keep[0:64] = first[128:192].astype(F32)
        keep[64:128] = cross[...].astype(F32)
        keep[128:256] = ffn[...].astype(F32)
        over_s[0:128] = rest.astype(BF16)
        over_s[128:256] = first[0:128]

    pl.when(place[4] == 0)(write_first)
    pl.when(place[4] == 1)(write_second)


def sum_rest_kernel(place, keep, from_z, from_s, from_both, norms, came, out):
    rest = keep[0:128] + from_s[0:128].astype(F32)
    other = from_z[...].astype(F32) + from_both[...].astype(F32)
    out[0:128] = jnp.where(place[4] == 0, rest + other, rest).astype(BF16)
    out[128:144] = (norms[...] + came[...]).astype(BF16)
    out[144:272] = (keep[128:256] + from_s[128:256].astype(F32)).astype(BF16)


def exchange(over_z, over_s):
    from_both = lax.ppermute(over_z, ("section", "dz"), [(2, 1), (3, 0)])
    return swap(over_z, "dz"), swap(over_s, "section"), from_both


def norms_kernel(place, all_ref, keep, over_s):
    total = sum(all_ref[272 * i + 128 : 272 * i + 144].astype(F32) for i in range(8))
    first, second = total[0:6], total[6:12]
    keep[0:6] = jnp.where(place[4] == 0, first, second)
    over_s[0:6] = jnp.where(place[4] == 0, second, first)
    keep[6:8] = jnp.zeros((2, 1024), F32)
    over_s[6:8] = jnp.zeros((2, 1024), F32)


def last_norms_kernel(mine, came, gains, biases, ffn):
    norms = mine[...] + came[...]
    for j in range(2):
        gains[j : j + 1] = norms[2 * j : 2 * j + 1]
        biases[j : j + 1] = norms[2 * j + 1 : 2 * j + 2]
    ffn[...] = norms[4:6]


def last_kernel(
    all_ref, out_ref, self_ref, q_ref, cross_ref, kv_ref, up_ref, down_ref
):
    def rows(at, count, span):
        return jnp.concatenate(
            [all_ref[272 * i + at : 272 * i + at + span] for i in range(count, count + 128 // span)],
            axis=0,
        ).astype(F32)

    out_ref[...] = rows(0, 0, 64)
    for i in range(3):
        self_ref[i] = rows(0, 2 + 2 * i, 64).T
    q_ref[...] = rows(64, 0, 32).T
    cross_ref[...] = rows(64, 4, 32)
    kv_ref[pl.ds(0, 1024, stride=2)] = rows(96, 0, 32).T
    kv_ref[pl.ds(1, 1024, stride=2)] = rows(96, 4, 32).T
    for i in range(4):
        here = slice(128 * i, 128 * i + 128)
        down_ref[here] = rows(144, i, 128)
        up = rows(144, 4 + i, 128)
        up_ref[here] = up[:, 0:512]
        up_ref[512 + 128 * i : 640 + 128 * i] = up[:, 512:1024]


def other_layer_kernel(place, text, unit, input_grad, text_grad, out):
    def write(rows, grads):
        out[0:BLOCK] = rows[...]
        out[BLOCK : 2 * BLOCK] = grads[...]

    pl.when(place[4] == 0)(lambda: write(unit, text_grad))
    pl.when(place[4] == 1)(lambda: write(text, input_grad))


def both_batches_kernel(place, text, unit, input_grad, text_grad, came, states, grads):
    mine = place[4]

    def write(rows, own):
        states[mine] = rows[...]
        grads[mine] = own[...]

    pl.when(mine == 0)(lambda: write(text, input_grad))
    pl.when(mine == 1)(lambda: write(unit, text_grad))
    states[1 - mine] = came[0:BLOCK]
    grads[1 - mine] = came[BLOCK : 2 * BLOCK]


def layer_forward(layer, v, first, weights, ffns, place, lengths, rows, after):
    own, far, cross, kv = weights
    heads = [struct((RING, BLOCK, 256), BF16), struct((RING, BLOCK, 512), BF16)]
    if layer == 0:
        q, kv_self, *rest = call(
            first_qkv_kernel,
            heads + cold(*[ROW16] * RING, ROW, COLUMN, struct((RING * BLOCK, 1024), BF16)),
            [*cold(*first, *own, *far), rows],
            after=after.get("qkv", ()),
        )
        full1, (s1, r1, all1) = rest[0:4], rest[4:7]
    else:
        a1, s1, r1, all1 = *first, None
        full1 = gather_x(a1)
        q, kv_self = call(qkv_kernel, heads, [*full1, *cold(*own, *far)], after=after.get("qkv", ()))
    kv_other = swap(kv_self, "core")
    if "keys" in after:
        after["keys"](q)
    mixed1, lse1, *sent = call(
        self_forward_kernel,
        cold_if(not layer, struct((RING, BLOCK, 256), BF16), struct((4, RING, 1, BLOCK), F32)) + SENT,
        [q, kv_self, kv_other, *cold(*own, *far)],
        scalars=[place],
        scratch=[pltpu.VMEM((KEYS, 256), BF16), pltpu.VMEM((KEYS, 256), BF16)],
        after=after.get("self", ()),
    )
    waits = after["sum1"](mixed1) if "sum1" in after else ()
    v1, a2, s2, r2 = sum_norm(1, v, sent[0], send_x(sent[1:]), rows, ROW, after=waits, new=not layer)
    a2_theirs = swap(a2, "core")
    cq, mixed2, lse2, near, far2 = call(
        functools.partial(cross_forward_kernel, layer),
        [
            struct((2 * BLOCK, 512), BF16),
            struct((2 * BLOCK, 512), BF16),
            struct((2 * RING, 1, 2 * BLOCK), F32),
            ROW,
            ROW16,
        ],
        [a2, a2_theirs, *cold(cross, *kv[0:4])],
        scalars=[place, lengths],
        after=after.get("cross", ()),
    )
    v2, a3, s3, r3 = sum_norm(
        2, v1, near, [swap(far2, "core")], rows, ROW, after=after.get("sum2", ()), old=not layer
    )
    full3 = gather_x(a3)
    hidden, slope, *sent = call(
        ffn_forward_kernel,
        [struct((RING * BLOCK, 1024), BF16), struct((RING * BLOCK, 1024), F32)] + SENT,
        [*full3, *cold(*ffns[layer])],
        after=after.get("ffn", ()),
    )
    stored = (
        (s1, r1, full1, q, kv_self, kv_other, mixed1, lse1, all1),
        (s2, r2, a2, a2_theirs, cq, mixed2, lse2),
        (s3, r3, full3, hidden, slope),
    )
    return v2, sent[0], send_x(sent[1:]), stored


def layer_back(layer, dv, full_g3, stored, weights, ffns, place, lengths, rows, steps):
    own, far, cross, kv = weights
    (s1, r1, full1, q, kv_self, kv_other, mixed1, lse1, all1), second, third = stored
    s2, r2, a2, a2_theirs, cq, mixed2, lse2 = second
    s3, r3, full3, hidden, slope = third
    old = layer == 0
    dpre, *sent = call(
        ffn_back_kernel,
        [struct((RING * BLOCK, 1024), BF16)] + SENT,
        [*full_g3, *cold(*ffns[layer]), *cold_if(old, slope)],
        after=steps.get("ffn", ()),
    )
    ffn_ours, *ffn_theirs = call(
        ffn_grads_kernel,
        [struct((1024, 1024), F32)] + [struct((CHUNK, 1024), BF16)] * 4,
        [*cold_if(old, hidden), *full_g3, dpre, *cold_if(old, *full3)],
    )
    ffn_parts = [ffn_ours, *(swap(part, "core") for part in ffn_theirs)]
    dv2, g2, norms3 = sum_back(
        2, dv, sent[0], send_x(sent[1:]), s3, r3, rows,
        after=[ffn_theirs[0], *steps.get("sum3", ())], old=old, new=old,
    )
    g2_theirs = swap(g2, "core")
    pair_keys = struct((2 * BLOCK, 256), BF16)
    dcq, *rest = call(
        functools.partial(cross_back_kernel, layer),
        [struct((2 * BLOCK, 512), BF16)] + [pair_keys] * RING + [ROW, ROW16],
        [g2, g2_theirs, *cold(cross, *kv[0:4]), *cold_if(old, cq, lse2)],
        scalars=[place, lengths],
        after=steps.get("cross", lambda parts, g2: ())(ffn_parts, g2),
    )
    dkv_cross, (near, far2) = rest[:RING], rest[RING:]
    dv1, g1, norms2 = sum_back(1, dv2, near, [swap(far2, "core")], s2, r2, rows, old=old, new=True)
    full_g1 = gather_x(g1)
    cross_grads = [*cold_if(old, mixed2), g2, g2_theirs, dcq, *cold_if(old, a2, a2_theirs)]
    middle, waits = steps["middle"](ffn_parts, cross_grads, dkv_cross, g1)
    dq, dkv_own, dkv_theirs = call(
        self_back_kernel,
        [
            struct((RING, BLOCK, 256), BF16),
            struct((RING, BLOCK, 512), F32),
            struct((RING, BLOCK, 512), BF16),
        ],
        [*full_g1, *cold(*own, *far, q, kv_self, kv_other, lse1)],
        scalars=[place],
        scratch=[
            pltpu.VMEM((KEYS, 256), BF16),
            pltpu.VMEM((KEYS, 256), BF16),
            pltpu.VMEM((RING, BLOCK, 256), BF16),
            pltpu.VMEM((KEYS, 256), F32),
            pltpu.VMEM((KEYS, 256), F32),
        ],
        after=waits,
    )
    back = [dq, dkv_own, swap(dkv_theirs, "core")]

    def self_grads(waits=()):
        ours, *theirs = call(
            self_grads_kernel,
            [struct((512, 1024), F32)] + [struct((2 * BLOCK, 1024), BF16)] * 2,
            [*cold(mixed1), *full_g1, *back, *cold(*full1)],
            after=waits,
        )
        return [ours, *(swap(part, "core") for part in theirs)], theirs

    if layer == 0:
        share, *others = call(cross_sum_kernel, [ROW, ROW16, ROW16, ROW16], middle)
        self_parts, theirs = self_grads([share])
        shares = [share, *send_x(others)]
        tall = struct((BLOCK + 16, 1024), BF16)
        near, *others, sums = call(
            last_rows_back_kernel,
            [ROW, tall, tall, tall, struct((16, 1024), F32)],
            [*back, *cold(*own, *far, all1, norms2, norms3, *steps["norms"])],
            after=[theirs[0]],
        )
        steps["late"](shares, self_parts, near)
        steps["tail"]["near"] = near
        g0, sums = call(
            last_sum_back_kernel,
            [ROW16, struct((16, 1024), F32)],
            [*cold(dv1), near, *send_x(others), *cold(s1, r1, rows, sums)],
        )
        return g0, middle, self_parts, sums
    else:
        sent = call(self_rows_back_kernel, SENT, [*back, *cold(*own, *far)])
        self_parts, theirs = self_grads()
        waits = [theirs[0], *steps["late"]()]
    dv0, g0, norms1 = sum_back(
        0, dv1, sent[0], send_x(sent[1:]), s1, r1, rows, after=waits, old=True
    )
    return g0, middle, self_parts, (norms1, norms2, norms3)


def reduce_dp(grads):
    total = lax.psum_scatter(grads, ("dz", "dy"), scatter_dimension=0, tiled=True)
    return total.reshape(grads.shape[1:])


def shards(
    inputs,
    memory_states,
    source_lengths,
    cotangent,
    norm_gain,
    norm_bias,
    w_self,
    w_self_out,
    w_cross_q,
    w_cross_kv,
    w_cross_out,
    up_weight,
    down_weight,
):
    place = PLACE

    def along_y(part):
        return [part] + [shift(part, "dy", k) for k in range(1, RING)]

    row16 = struct((BLOCK, 1024), BF16)
    kv_mine = w_cross_kv[0].reshape(w_cross_kv.shape[1], -1)
    half = struct((512, 512), BF16)
    *self_mine, mine = call(
        pack_kernel,
        [*cold(half, half), struct((256, 1024), BF16)],
        cold(w_self[0].transpose(1, 0, 2), w_self_out[0], w_cross_q[0], w_cross_out[0], kv_mine),
        scalars=[place],
        scratch=[pltpu.VMEM((1024, 1024), BF16)],
    )
    other = swap(mine, "section")
    x, rows_first, g_top = call(
        rows_kernel,
        cold(row16, struct((BLOCK + 32, 1024), BF16), row16),
        cold(inputs[:, :, 0], memory_states[:, :, 0], cotangent[:, :, 0]),
        scalars=[place],
        after=[mine],
    )
    norms = call(
        norm_rows_kernel, [struct((6, 1024), F32)], [norm_gain, norm_bias], after=[mine]
    )[0]
    norms_other = swap(norms, "section")
    rows_first = gather_x(rows_first)
    ffn_half = struct((512, 1024), BF16)
    ffn_mine, ffn_done = call(
        pack_ffn_kernel,
        cold(struct((1024, 1024), BF16)),
        cold(up_weight[0], down_weight[0]),
        after=[other, *rows_first[1:]],
        token=True,
    )
    ffn_other = swap(ffn_mine, "section")
    norms = call(
        both_norms_kernel, [struct((6, 1024), F32)] * 2, [norms, norms_other], scalars=[place]
    )

    rest, parts = call(
        rest_kernel,
        [struct((256, 768), BF16), Cold(struct((2, 256, 256), BF16))],
        [mine, other],
        scalars=[place],
        after=[norms_other, *rows_first[1:]], lazy=False)
    rests = along_y(rest)
    e_far = swap(call(memory_blocks_kernel, [row16], rows_first)[0], "core")
    a0, a1, b0, b1 = call(
        both_selfs_kernel,
        [half, half, *cold(half, half)],
        [*cold(*self_mine), *rests],
        scalars=[place],
        after=[e_far, norms[0], ffn_done], lazy=False)
    selfs = [(a0, a1), (b0, b1)]
    selfs_far = [tuple(swap(w, "core") for w in pair) for pair in selfs]
    crosses = lax.all_gather(parts, ("tx", "dy"), axis=0, tiled=True)
    ffns, kvs = [], []

    def make_keys(q):
        keyed, memory = call(
            keys_kernel,
            cold(struct((2, 256, 256), BF16), struct((256, 1024), BF16)),
            cold(kv_mine, *rests, *rows_first, e_far),
            scalars=[place],
            scratch=[pltpu.VMEM((1024, 256), BF16)],
            after=[q],
        )
        kvs.extend(gather_x(keyed))
        kvs.append(memory)


    def made(mixed):
        a0, a1, b0, b1, done = call(
            both_ffns_kernel,
            cold(*[ffn_half] * 4),
            cold(ffn_mine, ffn_other),
            scalars=[place],
            after=[mixed],
            token=True, lazy=False)
        for first, second in ((a0, a1), (b0, b1)):
            ffns.append((first, second, swap(first, "core"), swap(second, "core")))
        return [done]

    weights = [(selfs[i], selfs_far[i], crosses, kvs) for i in range(2)]

    v, near, far, stored0 = layer_forward(
        0, x, rows_first, weights[0], ffns, place, source_lengths, norms[0], {"keys": make_keys, "sum1": lambda mixed: [*kvs[1:4], *made(mixed)]}
    )
    text, *normed = sum_norm(0, v, near, far, norms[1], ROW16)
    v, near, far, stored1 = layer_forward(
        1, text, normed, weights[1], ffns, place, source_lengths, norms[1], {}
    )
    memory = kvs[4]
    full_top = gather_x(g_top)
    unit = call(sum_last_kernel, cold(ROW16), [*cold(v), near, *far])[0]

    def middle_second(ffn_parts, cross_grads, keys, after):
        out, done = call(
            cross_first_kernel,
            cold(struct((8, 384, 1024), BF16)),
            [*ffn_parts, *cross_grads, *keys, *cold(memory)],
            scalars=[place],
            after=[after],
            token=True,
        )
        return out, [done]

    text_grad, grads_a, self1, norms1 = layer_back(
        1, g_top, full_top, stored1, weights[1], ffns, place, source_lengths, norms[1],
        {
            "ffn": full_top[1:],
            "sum3": [unit],
            "middle": middle_second,
            "late": lambda: (),
        },
    )
    grads_a = reduce_dp(grads_a)

    tail = {}

    def join(ffn_parts, g2):
        tail["joined"], done = call(
            join_kernel,
            cold(struct((8, 192, 1024), BF16)),
            [*ffn_parts, *self1],
            after=[g2],
            token=True,
        )
        return [done]

    def middle_first(ffn_parts, cross_grads, keys, after):
        chunks_of = call(
            cross_chunk_kernel,
            chunk_shapes(128),
            cross_grads,
            scalars=[place],
            scratch=[pltpu.VMEM((1024, 1024), F32)],
            after=[after],
        )
        arrived = [shift(c, "dy", -k) for k, c in enumerate(chunks_of[1:], 1)]
        return [*cold(chunks_of[0]), *arrived, *keys], [chunks_of[1]]

    def late_first(cross_parts, self_parts, near):
        *tail["chunks"], tail["cross"] = call(
            rest_chunk_kernel,
            chunk_shapes(96) + cold(struct((2, 32, 1024), F32)),
            [*self_parts, *cross_parts, *cold(memory)],
            scalars=[place],
            scratch=[pltpu.VMEM((768, 1024), F32)],
            after=[near],
        )

    input_grad, _, _, norms = layer_back(
        0, text_grad, gather_x(text_grad), stored0, weights[0], ffns, place, source_lengths, norms[0],
        {
            "cross": join,
            "middle": middle_first,
            "late": late_first,
            "norms": norms1,
            "tail": tail,
        },
    )
    grads_b = reduce_dp(tail["joined"])
    ffn1, cross1 = call(
        split_kernel,
        cold(row16, struct((256, 1024), BF16)),
        cold(grads_a),
        after=[tail["chunks"][1]],
    )
    cross1 = lax.psum_scatter(cross1, "tx", scatter_dimension=0, tiled=True)
    chunks_of = tail["chunks"]
    arrived = [shift(c, "dy", -k) for k, c in enumerate(chunks_of[1:], 1)]
    two = struct((256, 1024), F32)
    keep, over_z, over_s = call(
        sum_y_kernel,
        [Cold(two), row16, struct((256, 1024), BF16)],
        [*cold(chunks_of[0]), *arrived, *cold(tail["cross"], grads_b, ffn1, cross1)],
        scalars=[place],
        after=[tail["near"]], lazy=False)
    last = call(
        sum_rest_kernel,
        cold(struct((272, 1024), BF16)),
        [*cold(keep), *exchange(over_z, over_s), norms, swap(norms, "core")],
        scalars=[place],
    )[0]
    whole = lax.all_gather(last, ("dz", "dy"), axis=0, tiled=True)
    rows = cold(text, unit, input_grad, text_grad)
    lacks = call(
        other_layer_kernel, [struct((256, 1024), BF16)], rows, scalars=[place], after=[last], lazy=False)[0]
    lacks = swap(lacks, "section")
    eight, pair32 = struct((8, 1024), F32), struct((2, 1024), F32)
    own, over_s = call(
        norms_kernel, [eight] * 2, cold(whole), scalars=[place]
    )
    grad_out, grad_self, grad_cq, grad_co, grad_ckv, grad_up, grad_down, done = call(
        last_kernel,
        cold(
            struct((128, 1024), F32),
            struct((3, 1024, 128), F32),
            struct((1024, 128), F32),
            struct((128, 1024), F32),
            struct((2048, 128), F32),
            struct((1024, 512), F32),
            struct((512, 1024), F32),
        ),
        cold(whole),
        after=[own],
        token=True,
    )
    both = struct((2, BLOCK, 1024), BF16)
    states, input_grads = call(
        both_batches_kernel, cold(both, both), [*rows, lacks], scalars=[place], after=[done], lazy=False)
    grad_gain, grad_bias, grad_ffn = call(
        last_norms_kernel, [pair32] * 3, [own, swap(over_s, "section")], after=[done]
    )
    return (
        states[None, :, :, None],
        input_grads[None, :, :, None],
        grad_gain[None],
        grad_bias[None],
        grad_ffn[None],
        grad_self.transpose(1, 0, 2)[None],
        grad_out[None],
        grad_cq[None],
        grad_ckv.reshape(1, 1024, 2, 128),
        grad_co[None],
        grad_up[None],
        grad_down[None],
    )


def solution(mesh):
    sections = mesh.devices.shape[0]
    fine = Mesh(
        mesh.devices.reshape(sections, 2, RING, RING, 2), ("section", "dz", "dy", "tx", "core")
    )
    dp, tensor = ("dz", "dy"), ("tx", "core")
    rows = P(None, tensor, dp, None)
    return jax.shard_map(
        shards,
        mesh=fine,
        in_specs=(
            rows,
            rows,
            P(None, dp),
            rows,
            P("section", None, None),
            P("section", None, None),
            P("section", None, None, tensor),
            P("section", tensor, None),
            P("section", None, tensor),
            P("section", None, None, tensor),
            P("section", tensor, None),
            P("section", None, tensor),
            P("section", tensor, None),
        ),
        out_specs=(
            P("section", None, tensor, dp, None),
            P("section", None, tensor, dp, None),
            P("section", None, None),
            P("section", None, None),
            P("section", None, None),
            P("section", None, None, tensor),
            P("section", tensor, None),
            P("section", None, tensor),
            P("section", None, None, tensor),
            P("section", tensor, None),
            P("section", None, tensor),
            P("section", tensor, None),
        ),
        check_vma=False,
    )
```
